32 devices in a mesh: gx: 8 (over y, x, core), gy: 4 (over z).
Axes of the slice: x: 2, y: 2, z: 4, core: 2. Of those that a mesh axis runs over, the one named last changes fastest.
Arguments:
- windows: bfloat16 [96, 196, 1280], P(('gx', 'gy')), may hold values from -6 to 6
- cotangent: bfloat16 [96, 196, 1280], P(('gx', 'gy')), may hold values from -6 to 6
- placement: int32 [96, 2], P(('gx', 'gy')), may hold values from 0 to 4
- counts: int32 [32], P(('gx', 'gy')), may hold values from 1 to 3, as said below
- qkv_weight: float32 [1280, 3840], P(None, ('gx', 'gy')), may hold values from -0.15625 to 0.15625
- proj_weight: float32 [1280, 1280], P(('gx', 'gy')), may hold values from -0.625 to 0.625
- up_weight: float32 [1280, 5120], P(None, ('gx', 'gy')), may hold values from -0.15625 to 0.15625
- down_weight: float32 [5120, 1280], P(('gx', 'gy')), may hold values from -0.078125 to 0.078125
- qkv_moment: float32 [1280, 3840], P(None, ('gx', 'gy')), may hold values from -128 to 128
- proj_moment: float32 [1280, 1280], P(('gx', 'gy')), may hold values from -80 to 80
- up_moment: float32 [1280, 5120], P(None, ('gx', 'gy')), may hold values from -256 to 256
- down_moment: float32 [5120, 1280], P(('gx', 'gy')), may hold values from -256 to 256
- vectors: float32 [15360], P(('gx', 'gy')), may hold values from -1.8 to 1.8, as said below
- vector_moment: float32 [15360], P(('gx', 'gy')), may hold values from -256 to 256
- rel_pos: float32 [2, 27, 80], replicated, may hold values from -1.5 to 1.5
- rel_moment: float32 [2, 27, 80], replicated, may hold values from -320 to 320
Outputs:
- block_out: bfloat16 [96, 196, 1280], P(('gx', 'gy'))
- input_grad: float32 [96, 196, 1280], P(('gx', 'gy'))
- qkv_moment_new: float32 [1280, 3840], P(None, ('gx', 'gy'))
- proj_moment_new: float32 [1280, 1280], P(('gx', 'gy'))
- up_moment_new: float32 [1280, 5120], P(None, ('gx', 'gy'))
- down_moment_new: float32 [5120, 1280], P(('gx', 'gy'))
- qkv_weight_new: float32 [1280, 3840], P(None, ('gx', 'gy'))
- proj_weight_new: float32 [1280, 1280], P(('gx', 'gy'))
- up_weight_new: float32 [1280, 5120], P(None, ('gx', 'gy'))
- down_weight_new: float32 [5120, 1280], P(('gx', 'gy'))
- vector_moment_new: float32 [15360], P(('gx', 'gy'))
- vectors_new: float32 [15360], P(('gx', 'gy'))
- rel_moment_new: float32 [2, 27, 80], replicated
- rel_pos_new: float32 [2, 27, 80], replicated
The draws below stay inside these ranges and needn't reach their ends.
Inputs may be any that keep to these rules, and one draw needn't show every extreme that they name: `counts`: the first, the middle and the last device have 3 live slots in every draw; the live slots of a device are its first ones. `vectors`: gains lie in 0.7 to 1.3, biases are of either sign.
All inputs are finite; a program needn't handle non-finite values.
Results may differ from the reference program's by a relative error of at most 0.019.
Values may be sent and summed in bfloat16 or wider, within the bound.
No kernel may reach another device: no remote copies, remote signals or barrier semaphores. Data moves between devices by JAX's collectives and lax.ppermute only.
A program may use at most 640 MiB of HBM per device.

```python
import jax
import jax.numpy as jnp
from jax import lax

D = 1280
FF = 5120
HEADS = 16
WIN = 14
GRID = 64
SLOTS = 3
ITERS = 5
HD = 80
WT = 196
NWIN = 5
RELS = 27
NVEC = 15360
TOTAL_SLOTS = 96


def draw_counts(key, part):
    key = jax.random.fold_in(key, 11)
    first_key, second_key = jax.random.split(key)
    device_count = TOTAL_SLOTS // SLOTS
    values_drawn = jax.random.randint(first_key, (device_count,), 1, SLOTS + 1)
    chosen = jax.random.randint(second_key, (), 0, device_count)
    places = jnp.arange(device_count)
    full = (places == chosen) | (places == 0) | (places == device_count // 2) | (places == device_count - 1)
    return jnp.where(full, SLOTS, values_drawn).astype(jnp.int32)


def draw_vectors(key, part):
    key = jax.random.fold_in(key, 5)
    first_key, second_key = jax.random.split(key)
    positions = jnp.arange(8 * D + FF)
    segment_id = positions // D
    gains = (segment_id == 0) | (segment_id == 5)
    noise = jnp.clip(jax.random.normal(first_key, (8 * D + FF,), jnp.float32), -6.0, 6.0)
    spread = jax.random.uniform(second_key, (8 * D + FF,), jnp.float32, -1.0, 1.0)
    return jnp.where(gains, 1.0 + 0.3 * spread, 0.3 * noise).astype(jnp.float32)


def set_ends(values, rng, low, high):
    spot = [jax.random.randint(jax.random.fold_in(rng, axis), (), 0, length) for axis, length in enumerate(values.shape)]
    longest = values.shape.index(max(values.shape))
    beside = spot[:longest] + [(spot[longest] + 1) % values.shape[longest]] + spot[longest + 1:]
    return values.at[tuple(spot)].set(low).at[tuple(beside)].set(high)


def levels(own_key, shape, cuts, smallest, largest):
    gain = 1.0
    for position, shards_of in cuts:
        steps = jax.random.uniform(jax.random.fold_in(jax.random.fold_in(own_key, 6), position), (shards_of,), jnp.float32, smallest / len(cuts), largest / len(cuts))
        gain = gain * jnp.repeat(jnp.exp(steps), shape[position] // shards_of).reshape((-1,) + (1,) * (len(shape) - 1 - position))
    return gain


def scatter_about(own_key, extent, scale, reach, pieces=(), kind=jnp.bfloat16):
    array = jax.random.normal(own_key, extent, jnp.float32) * scale
    if len(pieces) > 0:
        array = levels(own_key, extent, pieces, -0.22, 0.18) * array
    return jnp.clip(array, min=-reach, max=reach).astype(kind)


def setup_inputs(seed: int = 0) -> dict:
    keys = jax.random.split(jax.random.key(seed), 17)
    windows = scatter_about(keys[0], (TOTAL_SLOTS, WT, D), 1.0, 6.0, ((0, 32),))
    cotangent = scatter_about(keys[1], (TOTAL_SLOTS, WT, D), 1.0, 6.0, ((0, 32),))
    placement = set_ends(jax.random.randint(keys[2], (TOTAL_SLOTS, 2), 0, NWIN), jax.random.fold_in(keys[2], 1), 0, NWIN - 1).astype(jnp.int32)
    counts = draw_counts(jax.random.fold_in(keys[16], 71), 0)
    qkv_weight = scatter_about(keys[4], (D, 3 * D), D ** -0.5, 0.15625, ((1, 32),), jnp.float32)
    proj_weight = scatter_about(keys[5], (D, D), (D // WIN) ** -0.5, 0.625, ((0, 32),), jnp.float32)
    up_weight = scatter_about(keys[6], (D, FF), D ** -0.5, 0.15625, ((1, 32),), jnp.float32)
    down_weight = scatter_about(keys[7], (FF, D), FF ** -0.5, 0.078125, ((0, 32),), jnp.float32)
    qkv_moment = scatter_about(keys[8], (D, 3 * D), (0.15 * (TOTAL_SLOTS * WT) ** 0.5), 128.0, ((1, 32),), jnp.float32)
    proj_moment = scatter_about(keys[9], (D, D), (0.1 * (TOTAL_SLOTS * WT) ** 0.5), 80.0, ((0, 32),), jnp.float32)
    up_moment = scatter_about(keys[10], (D, FF), (0.3 * (TOTAL_SLOTS * WT) ** 0.5), 256.0, ((1, 32),), jnp.float32)
    down_moment = scatter_about(keys[11], (FF, D), (0.3 * (TOTAL_SLOTS * WT) ** 0.5), 256.0, ((0, 32),), jnp.float32)
    vectors = draw_vectors(jax.random.fold_in(keys[16], 71), 0)
    vector_moment = scatter_about(keys[13], (NVEC,), (0.3 * (TOTAL_SLOTS * WT) ** 0.5), 256.0, ((0, 32),), jnp.float32)
    rel_pos = scatter_about(keys[14], (2, RELS, HD), 0.1, 1.5, (), jnp.float32)
    rel_moment = scatter_about(keys[15], (2, RELS, HD), (0.4 * (TOTAL_SLOTS * WT) ** 0.5), 320.0, (), jnp.float32)
    return dict(windows=windows, cotangent=cotangent, placement=placement, counts=counts, qkv_weight=qkv_weight, proj_weight=proj_weight, up_weight=up_weight, down_weight=down_weight, qkv_moment=qkv_moment, proj_moment=proj_moment, up_moment=up_moment, down_moment=down_moment, vectors=vectors, vector_moment=vector_moment, rel_pos=rel_pos, rel_moment=rel_moment)


@jax.custom_vjp
def low(v):
    return lax.optimization_barrier(v.astype(jnp.bfloat16)).astype(jnp.float32)

@jax.custom_vjp
def low_back(v):
    return v

def low_keep(v):
    return (low(v), None)

def low_pass(kept, grad):
    return (grad,)

def back_keep(v):
    return (v, None)

def back_low(kept, grad):
    return (low(grad),)
low.defvjp(low_keep, low_pass)
low_back.defvjp(back_keep, back_low)
NORM_EPSILON = 1e-06
ORTHO_EPSILON = 1e-07
COEFF_LINEAR = 3.4445
COEFF_CUBIC = -4.775
COEFF_QUINTIC = 2.0315
MOMENT_MATRIX = 0.95
MOMENT_VECTOR = 0.9
RATE_MATRIX = 0.5

def norm_affine(values_in, gain_vec, shift_vec, masked):
    centre = lax.optimization_barrier(jnp.mean(values_in, axis=-1, keepdims=True))
    centred = values_in - centre
    inverse = lax.rsqrt(lax.optimization_barrier(jnp.mean(centred * centred, axis=-1, keepdims=True)) + NORM_EPSILON)
    return (centred * inverse * gain_vec + shift_vec) * masked

def segment(vec_full, index, model_width):
    return vec_full[index * model_width:(index + 1) * model_width]

def block_forward(windows, mask, qkv_w, proj_w, up_w, down_w, vec_w, rel_w):
    highest = lax.Precision.HIGHEST
    slot_count, tokens, model_width = windows.shape
    row_count = slot_count * tokens
    head_dim = model_width // HEADS
    masked = mask[:, :, None]
    vec_low = low(vec_w)
    rel_low = low(rel_w)
    offsets = (jnp.arange(WIN)[:, None] - jnp.arange(WIN)[None, :] + WIN - 1).astype(jnp.int32)
    rel_rows = rel_low[0][offsets]
    rel_cols = rel_low[1][offsets]
    shortcut = windows * masked
    normed_one = low(norm_affine(shortcut, segment(vec_low, 0, model_width), segment(vec_low, 1, model_width), masked))
    qkv_bias = jnp.concatenate([segment(vec_low, 2, model_width), jnp.zeros((model_width,), jnp.float32), segment(vec_low, 3, model_width)])
    qkv_rows = jnp.dot(normed_one.reshape(row_count, model_width), low(qkv_w), precision=highest) + qkv_bias
    qkv_rows = low(low_back(qkv_rows)).reshape(slot_count, WIN, WIN, 3, HEADS, head_dim)
    queries = qkv_rows[:, :, :, 0]
    key_vecs = qkv_rows[:, :, :, 1]
    val_vecs = qkv_rows[:, :, :, 2].reshape(slot_count, tokens, HEADS, head_dim)
    base_scores = jnp.einsum('sabhc,sdehc->shabde', queries, key_vecs, precision=highest) * head_dim ** (-0.5)
    along_h = jnp.einsum('sabhc,adc->shabd', queries, rel_rows, precision=highest)
    along_w = jnp.einsum('sabhc,bec->shabe', queries, rel_cols, precision=highest)
    scores = base_scores + along_h[:, :, :, :, :, None] + along_w[:, :, :, :, None, :]
    scores = low_back(scores.reshape(slot_count, HEADS, tokens, tokens))
    row_peak = lax.optimization_barrier(jnp.max(scores, axis=-1, keepdims=True))
    exponent = jnp.exp(scores - row_peak)
    attn_probs = low(exponent / lax.optimization_barrier(jnp.sum(exponent, axis=-1, keepdims=True)))
    attended = jnp.einsum('shij,sjhc->sihc', attn_probs, val_vecs, precision=highest)
    attended = low(low_back(attended)).reshape(row_count, model_width)
    branch = low_back(jnp.dot(attended, low(proj_w), precision=highest) + segment(vec_low, 4, model_width))
    middle = (shortcut + branch.reshape(slot_count, tokens, model_width)) * masked
    normed_two = low(norm_affine(middle, segment(vec_low, 5, model_width), segment(vec_low, 6, model_width), 1.0))
    pre_act = low_back(jnp.dot(normed_two.reshape(row_count, model_width), low(up_w), precision=highest) + vec_low[8 * model_width:])
    gelu_out = low(jax.nn.gelu(pre_act, approximate=False))
    mlp_out = low_back(jnp.dot(gelu_out, low(down_w), precision=highest) + segment(vec_low, 7, model_width))
    return (middle + mlp_out.reshape(slot_count, tokens, model_width)) * masked

def token_mask(placement, counts):
    total = placement.shape[0]
    slot_ids = jnp.arange(total, dtype=jnp.int32)
    device_of = (slot_ids // SLOTS).astype(jnp.int32)
    live = (slot_ids % SLOTS < counts[device_of]).astype(jnp.float32)
    inner = jnp.arange(WIN * WIN, dtype=jnp.int32)
    row_pos = placement[:, 0:1] * WIN + inner[None, :] // WIN
    col_pos = placement[:, 1:2] * WIN + inner[None, :] % WIN
    inside = ((row_pos < GRID) & (col_pos < GRID)).astype(jnp.float32)
    return inside * live[:, None]

def orthogonal(moment, flipped):
    iterate = moment.T if flipped else moment
    iterate = iterate / (jnp.sqrt(jnp.sum(iterate * iterate)) + ORTHO_EPSILON)
    for iteration in range(ITERS):
        iter_low = iterate.astype(jnp.bfloat16)
        gram = jnp.dot(iter_low, iter_low.T, preferred_element_type=jnp.float32).astype(jnp.bfloat16)
        first_p = jnp.dot(gram, iter_low, preferred_element_type=jnp.float32)
        second_p = jnp.dot(gram, first_p.astype(jnp.bfloat16), preferred_element_type=jnp.float32)
        iterate = COEFF_LINEAR * iterate + COEFF_CUBIC * first_p + COEFF_QUINTIC * second_p
    return iterate.T if flipped else iterate

def reference(windows, cotangent, placement, counts, qkv_weight, proj_weight, up_weight, down_weight, qkv_moment, proj_moment, up_moment, down_moment, vectors, vector_moment, rel_pos, rel_moment):
    device_count = counts.shape[0]
    mask = token_mask(placement, counts)
    grouped_in = windows.reshape((device_count, SLOTS) + windows.shape[1:])
    grouped_cot = cotangent.reshape((device_count, SLOTS) + cotangent.shape[1:])
    grouped_mask = mask.reshape(device_count, SLOTS, mask.shape[1])
    params = (qkv_weight, proj_weight, up_weight, down_weight, vectors, rel_pos)
    zeros = tuple((jnp.zeros_like(item) for item in params))

    def group_step(totals, inputs):
        win_group, cot_group, mask_group = inputs

        def local_block(x_in, qkv_w, proj_w, up_w, down_w, vec_w, rel_w):
            return block_forward(x_in, mask_group, qkv_w, proj_w, up_w, down_w, vec_w, rel_w)
        result, back_fn = jax.vjp(local_block, win_group.astype(jnp.float32), qkv_weight, proj_weight, up_weight, down_weight, vectors, rel_pos)
        grads = back_fn(cot_group.astype(jnp.float32))
        totals = tuple((acc + grad for acc, grad in zip(totals, grads[1:])))
        return (totals, (result.astype(jnp.bfloat16), grads[0]))
    totals, (outputs, in_grads) = lax.scan(group_step, zeros, (grouped_in, grouped_cot, grouped_mask))
    block_out = outputs.reshape(windows.shape)
    input_grad = in_grads.reshape(windows.shape)
    g_qkv, g_proj, g_up, g_down, g_vec, g_rel = totals
    model_width = qkv_weight.shape[0]
    hidden = up_weight.shape[1]
    m_qkv = MOMENT_MATRIX * qkv_moment + g_qkv
    m_proj = MOMENT_MATRIX * proj_moment + g_proj
    m_up = MOMENT_MATRIX * up_moment + g_up
    m_down = MOMENT_MATRIX * down_moment + g_down
    w_qkv = qkv_weight - RATE_MATRIX * jnp.sqrt(3.0) * orthogonal(m_qkv, False)
    w_proj = proj_weight - RATE_MATRIX * orthogonal(m_proj, True)
    w_up = up_weight - RATE_MATRIX * jnp.sqrt(max(1.0, hidden / model_width)) * orthogonal(m_up, False)
    w_down = down_weight - RATE_MATRIX * jnp.sqrt(max(1.0, model_width / hidden)) * orthogonal(m_down, True)
    rate_vec = 0.5 / jnp.sqrt(float(windows.shape[0] * windows.shape[1]))
    m_vec = MOMENT_VECTOR * vector_moment + g_vec
    m_rel = MOMENT_VECTOR * rel_moment + g_rel
    return (block_out, input_grad, m_qkv, m_proj, m_up, m_down, w_qkv, w_proj, w_up, w_down, m_vec, vectors - rate_vec * m_vec, m_rel, rel_pos - 0.2 * rate_vec * m_rel)
```

```python
from functools import partial
import math

import jax
import jax.numpy as jnp
from jax import lax
from jax.experimental import pallas as pl
from jax.experimental.pallas import tpu as pltpu
from jax.sharding import Mesh, PartitionSpec as P

D = 1280
FF = 5120
HEADS = 16
HD = 80
WIN = 14
GRID = 64
ITERS = 5
LANES = 256
ROWS = 208

NORM_EPSILON = 1e-06
ORTHO_EPSILON = 1e-07
COEFF_LINEAR = 3.4445
COEFF_CUBIC = -4.775
COEFF_QUINTIC = 2.0315
MOMENT_MATRIX = 0.95
MOMENT_VECTOR = 0.9
RATE_MATRIX = 0.5

BF = jnp.bfloat16
F32 = jnp.float32


def dot_nn(left, right):
    return jnp.dot(left, right, preferred_element_type=F32)


def dot_tn(left, right):
    return lax.dot_general(left, right, (((0,), (0,)), ((), ())), preferred_element_type=F32)


def dot_nt(left, right):
    return lax.dot_general(left, right, (((1,), (1,)), ((), ())), preferred_element_type=F32)


def split_low(value):
    high = value.astype(BF)
    return high, (value - high.astype(F32)).astype(BF)


GROUP = 8


def spots():
    row = lax.broadcasted_iota(jnp.int32, (32, LANES), 0)
    lane = lax.broadcasted_iota(jnp.int32, (32, LANES), 1)
    along = jnp.where(row < 16, lane // WIN, lane % WIN + 16)
    return jnp.where((along == row) & (lane < WIN * WIN), 1.0, 0.0).astype(BF)


def shifts():
    lane = lax.broadcasted_iota(jnp.int32, (32, LANES), 1)
    down_h = jnp.maximum(WIN - 1 - lane // WIN, 0)
    return down_h, WIN - 1 - lane % WIN


def barrel(value, amount, up):
    for bit in (1, 2, 4, 8):
        moved = pltpu.roll(value, 32 - bit if up else bit, 0)
        value = jnp.where((amount & bit) != 0, moved, value)
    return value


def attend_kernel(q_ref, k_ref, v_ref, rel_ref, out_ref, probs_ref):
    marks = spots()
    marks2 = jnp.concatenate([marks, marks], axis=0)
    shift_h, shift_w = shifts()
    tail_row = lax.broadcasted_iota(jnp.int32, (16, LANES), 0) + (ROWS - 16)
    pad = jnp.zeros((LANES - ROWS, LANES), BF)
    scale = HD ** (-0.5) / math.log(2.0)
    for head in range(GROUP):
        query = q_ref[0, head]
        rel_q = dot_nn(rel_ref[...], query) * (HD**0.5)
        along_h = barrel(rel_q[:32], shift_h, True)[:16]
        along_w = barrel(rel_q[32:], shift_w, True)[:16]
        high, rest = split_low(jnp.concatenate([along_h, along_w], axis=0))
        query_all = jnp.concatenate([query, high, rest], axis=0)
        key_all = jnp.concatenate([k_ref[0, head], marks2], axis=0)
        scores = dot_tn(key_all, query_all)[:ROWS]
        tail = jnp.where(tail_row < WIN * WIN, scores[ROWS - 16 :], -1e30)
        scores = jnp.concatenate([scores[: ROWS - 16], tail], axis=0)
        peak = jnp.max(scores, axis=0, keepdims=True)
        exponent = jnp.exp2((scores - peak) * scale)
        probs = (exponent * (1.0 / jnp.sum(exponent, axis=0, keepdims=True))).astype(BF)
        probs_ref[0, head] = probs
        out_ref[head] = dot_nn(v_ref[0, head], jnp.concatenate([probs, pad], axis=0)).astype(BF)


def attend(qkv, rel_rows):
    slots = qkv.shape[-1] // LANES
    cut = lambda part: pl.BlockSpec((1, GROUP, HD, LANES), lambda s, g, part=part: (part, g, 0, s))
    return pl.pallas_call(
        attend_kernel,
        grid=(slots, HEADS // GROUP),
        in_specs=[cut(0), cut(1), cut(2), pl.BlockSpec((64, HD), lambda s, g: (0, 0))],
        out_specs=[
            pl.BlockSpec((GROUP, HD, LANES), lambda s, g: (g, 0, s)),
            pl.BlockSpec((1, GROUP, ROWS, LANES), lambda s, g: (s, g, 0, 0)),
        ],
        out_shape=[
            jax.ShapeDtypeStruct((HEADS, HD, slots * LANES), BF),
            jax.ShapeDtypeStruct((slots, HEADS, ROWS, LANES), BF),
        ],
        compiler_params=pltpu.CompilerParams(vmem_limit_bytes=16 * 2**20),
        cost_estimate=cheap(slots * HEADS * 2 * LANES * LANES * 256),
        name="attend",
    )(qkv, qkv, qkv, rel_rows)


def attend_back_kernel(q_ref, k_ref, v_ref, g_ref, probs_ref, rel_ref, out_ref, drel_ref):
    marks = spots()
    shift_h, shift_w = shifts()
    pad = jnp.zeros((LANES - ROWS, LANES), BF)
    none = jnp.zeros((16, LANES), F32)
    scale = HD ** (-0.5)
    total = jnp.zeros((64, HD), F32)
    for head in range(GROUP):
        query = q_ref[0, head]
        grad = g_ref[head]
        probs_low = probs_ref[0, head]
        probs = probs_low.astype(F32)
        weighted = dot_tn(v_ref[0, head], grad)[:ROWS] * probs
        flow = jnp.sum(weighted, axis=0, keepdims=True)
        score_low = jnp.concatenate([(weighted - probs * flow).astype(BF), pad], axis=0)
        out_ref[2, head] = dot_nt(grad, jnp.concatenate([probs_low, pad], axis=0)).astype(BF)
        out_ref[1, head] = (dot_nt(query, score_low) * scale).astype(BF)
        mixed = dot_nn(jnp.concatenate([k_ref[0, head], marks], axis=0), score_low)
        rows_h = barrel(jnp.concatenate([mixed[HD : HD + 16], none], axis=0), shift_h, False)
        rows_w = barrel(jnp.concatenate([mixed[HD + 16 :], none], axis=0), shift_w, False)
        both = jnp.concatenate(split_low(jnp.concatenate([rows_h, rows_w], axis=0)), axis=0)
        out_ref[0, head] = (mixed[:HD] * scale + dot_nn(rel_ref[...], both)).astype(BF)
        parts = dot_nt(both, query)
        total = total + parts[:64] + parts[64:]

    @pl.when((pl.program_id(0) == 0) & (pl.program_id(1) == 0))
    def _():
        drel_ref[...] = jnp.zeros_like(drel_ref)

    drel_ref[...] += total


def attend_back(qkv, grad, probs, rel_cols):
    slots = qkv.shape[-1] // LANES
    cut = lambda part: pl.BlockSpec((1, GROUP, HD, LANES), lambda s, g, part=part: (part, g, 0, s))
    return pl.pallas_call(
        attend_back_kernel,
        grid=(slots, HEADS // GROUP),
        in_specs=[
            cut(0),
            cut(1),
            cut(2),
            pl.BlockSpec((GROUP, HD, LANES), lambda s, g: (g, 0, s)),
            pl.BlockSpec((1, GROUP, ROWS, LANES), lambda s, g: (s, g, 0, 0)),
            pl.BlockSpec((HD, 128), lambda s, g: (0, 0)),
        ],
        out_specs=[
            pl.BlockSpec((3, GROUP, HD, LANES), lambda s, g: (0, g, 0, s)),
            pl.BlockSpec((64, HD), lambda s, g: (0, 0)),
        ],
        out_shape=[
            jax.ShapeDtypeStruct((3, HEADS, HD, slots * LANES), BF),
            jax.ShapeDtypeStruct((64, HD), F32),
        ],
        compiler_params=pltpu.CompilerParams(vmem_limit_bytes=20 * 2**20),
        cost_estimate=cheap(slots * HEADS * 5 * LANES * LANES * 256),
        name="attend_back",
    )(qkv, qkv, qkv, grad, probs, rel_cols)


def resident(shape):
    return pl.BlockSpec(shape, lambda *_: (0,) * len(shape))


def cheap(flops):
    return pl.CostEstimate(flops=flops // 8, bytes_accessed=1_000_000, transcendentals=0)


def settings(mebibytes):
    return pltpu.CompilerParams(vmem_limit_bytes=mebibytes * 2**20)


def middle_kernel(att_ref, proj_ref, short_ref, mask_ref, rows_ref, middle_ref, normed_ref):
    branch = dot_tn(att_ref[...], proj_ref[...])[:ROWS] + rows_ref[0:1]
    middle = (short_ref[...].astype(F32) + branch) * mask_ref[...]
    middle_ref[...] = middle
    centred = middle - jnp.mean(middle, axis=1, keepdims=True)
    inverse = lax.rsqrt(jnp.mean(centred * centred, axis=1, keepdims=True) + NORM_EPSILON)
    normed_ref[...] = (centred * inverse * rows_ref[1:2] + rows_ref[2:3]).astype(BF)


def to_middle(attended, proj_full, short, mask, rows):
    slots = attended.shape[1] // LANES
    by_slot = lambda width: pl.BlockSpec((ROWS, width), lambda s: (s, 0))
    return pl.pallas_call(
        middle_kernel,
        grid=(slots,),
        in_specs=[
            pl.BlockSpec((D, LANES), lambda s: (0, s)),
            resident((D, D)),
            by_slot(D),
            by_slot(1),
            resident((8, D)),
        ],
        out_specs=[by_slot(D), by_slot(D)],
        out_shape=[
            jax.ShapeDtypeStruct((slots * ROWS, D), F32),
            jax.ShapeDtypeStruct((slots * ROWS, D), BF),
        ],
        compiler_params=settings(24),
        cost_estimate=cheap(2 * slots * LANES * D * D),
        name="middle",
    )(attended, proj_full, short, mask, rows)


def norm_parts(grad, value, gain):
    centred = value - jnp.mean(value, axis=1, keepdims=True)
    inverse = lax.rsqrt(jnp.mean(centred * centred, axis=1, keepdims=True) + NORM_EPSILON)
    hat = centred * inverse
    scaled = grad * gain
    mean_one = jnp.mean(scaled, axis=1, keepdims=True)
    mean_two = jnp.mean(scaled * hat, axis=1, keepdims=True)
    sums = [jnp.sum(grad * hat, axis=0, keepdims=True), jnp.sum(grad, axis=0, keepdims=True)]
    sums = jnp.concatenate(sums + [jnp.zeros((6, D), F32)], axis=0)
    return inverse * (scaled - mean_one - hat * mean_two), sums


def add_sums(sums_ref, sums):
    @pl.when(pl.program_id(0) == 0)
    def _():
        sums_ref[...] = jnp.zeros_like(sums_ref)

    sums_ref[...] += sums


def second_norm_kernel(grad_ref, came_ref, middle_ref, out_ref, mask_ref, rows_ref, total_ref, pad_ref, sums_ref):
    grad = grad_ref[...] + came_ref[...].astype(F32)
    back, sums = norm_parts(grad, middle_ref[...], rows_ref[1:2])
    total = (out_ref[...].astype(F32) + back) * mask_ref[...]
    total_ref[...] = total
    low = total.astype(BF)
    pad_ref[...] = jnp.concatenate([low, jnp.zeros((LANES - ROWS, D), BF)], axis=0)
    add_sums(sums_ref, sums)


def first_norm_kernel(grad_ref, came_ref, short_ref, total_ref, mask_ref, rows_ref, out_ref, sums_ref):
    mask = mask_ref[...]
    grad = (grad_ref[:ROWS] + came_ref[...].astype(F32)) * mask
    back, sums = norm_parts(grad, short_ref[...].astype(F32), rows_ref[3:4])
    out_ref[0] = ((total_ref[...] + back) * mask)[: WIN * WIN]
    add_sums(sums_ref, sums)


def by_slots(kernel, name, given, outs):
    slots = given[1].shape[0] // ROWS

    def spec(shape):
        if len(shape) == 3:
            return pl.BlockSpec((1,) + shape[1:], lambda s: (s, 0, 0))
        if shape[0] == 8:
            return resident(shape)
        return pl.BlockSpec((shape[0] // slots, shape[1]), lambda s: (s, 0))

    return pl.pallas_call(
        kernel,
        grid=(slots,),
        in_specs=[spec(item.shape) for item in given],
        out_specs=[spec(item.shape) for item in outs],
        out_shape=list(outs),
        compiler_params=settings(32),
        cost_estimate=cheap(1_000_000),
        name=name,
    )(*given)


SIDE = 256
SPOTS = [(row, column) for row in range(D // SIDE) for column in range(row, D // SIDE)]


def upper_blocks(gram):
    parts = [
        gram[row * SIDE : (row + 1) * SIDE, column * SIDE : (column + 1) * SIDE] for row, column in SPOTS
    ]
    return jnp.concatenate(parts, axis=0)


def chain_kernel(gram_ref, y_ref, out_ref, high_ref, rest_ref, b_ref, t_high, t_rest, z_high, z_rest):
    columns = [slice(start, start + SIDE) for start in range(0, D, SIDE)]
    row = lax.broadcasted_iota(jnp.int32, (SIDE, SIDE), 0)
    spot = row == lax.broadcasted_iota(jnp.int32, (SIDE, SIDE), 1)
    trace = jnp.zeros((), F32)
    for place, (row, column) in enumerate(SPOTS):
        if row == column:
            trace = trace + jnp.sum(jnp.where(spot, gram_ref[place * SIDE : (place + 1) * SIDE, :], 0.0))
    inverse = 1.0 / (jnp.sqrt(trace) + ORTHO_EPSILON)
    for place, (row, column) in enumerate(SPOTS):
        block = gram_ref[place * SIDE : (place + 1) * SIDE, :] * inverse * inverse
        for part, over, down in ((block, row, column), (block.T, column, row)):
            high, rest = split_low(part)
            high_ref[columns[over], columns[down]] = high
            rest_ref[columns[over], columns[down]] = rest
    z_high[0] = y_ref[...]
    z_rest[0] = jnp.zeros_like(y_ref)

    def polynomial():
        for place, cut in enumerate(columns):
            square = dot_nn(high_ref[...], high_ref[:, cut])
            value = high_ref[:, cut].astype(F32) + rest_ref[:, cut].astype(F32)
            poly = COEFF_CUBIC * value + COEFF_QUINTIC * square
            line = lax.broadcasted_iota(jnp.int32, (D, SIDE), 0) - place * SIDE
            eye = line == lax.broadcasted_iota(jnp.int32, (D, SIDE), 1)
            b_ref[:, cut] = (poly + jnp.where(eye, COEFF_LINEAR, 0.0)).astype(BF)

    def follow(now, cut):
        return dot_nn(z_high[now], b_ref[:, cut]) + dot_nn(z_rest[now], b_ref[:, cut])

    def advance(now, fine):
        later = 1 - now
        polynomial()
        for cut in columns:
            value = dot_nn(b_ref[...], high_ref[:, cut])
            if fine:
                value = value + dot_nn(b_ref[...], rest_ref[:, cut])
            t_high[:, cut], rest = split_low(value)
            if fine:
                t_rest[:, cut] = rest
            z_high[later, :, cut], z_rest[later, :, cut] = split_low(follow(now, cut))
        for cut in columns:
            value = dot_nn(t_high[...], b_ref[:, cut])
            if fine:
                value = value + dot_nn(t_rest[...], b_ref[:, cut])
            high_ref[:, cut], rest_ref[:, cut] = split_low(value)

    @pl.loop(0, ITERS - 2)
    def _(step):
        advance(step % 2, True)

    advance((ITERS - 2) % 2, False)
    polynomial()
    for cut in columns:
        out_ref[:, cut] = (follow((ITERS - 1) % 2, cut) * inverse).astype(BF)


def chain(gram, rows):
    half = pltpu.VMEM((D, D), BF)
    flow = pltpu.VMEM((2,) + rows.shape, BF)
    whole = pl.BlockSpec(memory_space=pltpu.VMEM)
    return pl.pallas_call(
        chain_kernel,
        in_specs=[whole, whole],
        out_specs=whole,
        out_shape=jax.ShapeDtypeStruct(rows.shape, BF),
        scratch_shapes=[half] * 5 + [flow] * 2,
        compiler_params=settings(56),
        cost_estimate=pl.CostEstimate(flops=23 * 2 * D**3, bytes_accessed=6 * D * D, transcendentals=0),
        name="chain",
    )(gram, rows)


EVERY = ("ga", "gb", "gc", "gy")


def peer(value):
    return lax.ppermute(value, "gc", [(0, 1), (1, 0)])


def steps_of(axis):
    return lax.axis_size(axis).bit_length() - 1


def first_stages():
    return [("f", step) for step in reversed(range(steps_of("ga")))]


def second_stages():
    return [("s", step) for step in reversed(range(steps_of("gb")))]


def plane_stages():
    return [("z", step) for step in range(steps_of("gy"))]


def gather_groups():
    deep = plane_stages()
    return [deep[1:][::-1], deep[:1]], [second_stages()[::-1]], [first_stages()[::-1]]


def reduce_groups():
    deep = plane_stages()
    return [first_stages()], [second_stages()], [deep[:1], deep[1:]]


def half_stages():
    return first_stages() + second_stages() + plane_stages()


def bit_of(stage, core):
    kind, step = stage
    if kind == "z":
        return "gy", steps_of("gy") - 1 - step if core == 0 else step
    return ("ga" if (kind == "f") == (core == 0) else "gb"), step


def my_bit(stage):
    values = []
    for core in range(2):
        axis, step = bit_of(stage, core)
        values.append((lax.axis_index(axis) >> step) & 1)
    return jnp.where(lax.axis_index("gc") == 0, values[0], values[1])


def swap(value, stage):
    if stage == "c":
        return peer(value)
    sizes = [lax.axis_size(axis) for axis in EVERY]
    pairs = []
    for place in range(math.prod(sizes)):
        spot, rest = [], place
        for size in reversed(sizes):
            spot.insert(0, rest % size)
            rest //= size
        axis, step = bit_of(stage, spot[2])
        spot[EVERY.index(axis)] ^= 1 << step
        other = 0
        for size, at in zip(sizes, spot):
            other = other * size + at
        pairs.append((place, other))
    return lax.ppermute(value, EVERY, pairs)


class Rounds:
    def __init__(self):
        self.last = None

    def go(self, chains, work=None, *values):
        chains = [chain for chain in chains if not chain.done]
        while long := [chain for chain in chains if chain.left > 1]:
            self.once(long)
        out = self.once(chains, work, *values)
        for chain in chains:
            chain.left = chain.counts.pop(0) if chain.counts else 0
        return out

    def once(self, chains, work=None, *values):
        [chain.look() for chain in chains]
        marks = [] if self.last is None else [self.last]
        held = [lax.optimization_barrier((chain.value, *marks))[0] for chain in chains]
        came = [swap(value, chain.stage) for value, chain in zip(held, chains)]
        ready = lax.optimization_barrier((*values, *held, *marks))
        out = () if work is None else work(*ready[: len(values)])
        leaves, tree = jax.tree.flatten(out)
        ended = lax.optimization_barrier(tuple(came) + tuple(leaves))
        self.last = ended[0]
        for chain, value in zip(chains, ended):
            chain.take(value)
            chain.left -= 1
        return jax.tree.unflatten(tree, ended[len(chains) :])


class Chain:
    def __init__(self, work, groups):
        self.work, self.ended, self.result = work, False, None
        self.pending = [None]
        self.counts = [len(group) for group in groups if group]
        self.left = self.counts.pop(0)

    def take(self, came):
        self.pending = [came]

    def look(self):
        if self.pending:
            try:
                self.value, self.stage = self.work.send(self.pending.pop())
            except StopIteration as stop:
                self.ended, self.result = True, stop.value

    @property
    def done(self):
        self.look()
        return self.ended

    @property
    def out(self):
        self.look()
        return self.result


def gather_half(shard):
    groups = sum(gather_groups(), [])

    def work():
        held = shard[None]
        for stage in sum(groups, []):
            came = yield held, stage
            first = my_bit(stage) == 0
            held = jnp.concatenate([jnp.where(first, held, came), jnp.where(first, came, held)], axis=0)
        return held.reshape(-1, shard.shape[-1])

    return Chain(work(), groups)


def gather_relative(shard, groups):
    def work():
        order, canon = sum(groups, []), half_stages()
        held = shard
        for stage in order[:-1]:
            came = yield held, stage
            held = jnp.stack([held, came])
        came = yield held, order[-1]
        there = order[-2::-1]
        turn = [there.index(stage) for stage in canon[1:]] + [len(there), len(there) + 1]
        return tuple(half.transpose(turn).reshape(-1, shard.shape[-1]) for half in (held, came))

    return Chain(work(), groups)


def relative(value):
    stages = half_stages()
    shape = value.shape
    value = value.reshape((2,) * len(stages) + shape[1:])
    for place, stage in enumerate(stages):
        value = jnp.where(my_bit(stage) == 1, jnp.flip(value, place), value)
    return value.reshape(shape)


def reduce_half(grad, groups, kind=BF):
    def work():
        live = half_stages()
        parts = [grad.reshape((2,) * len(live) + (-1, grad.shape[-1]))]
        for stage in sum(groups, []):
            place, mine = live.index(stage), my_bit(stage)
            live.remove(stage)

            def pick(which):
                cuts = [lax.dynamic_index_in_dim(part, which, place, False) for part in parts]
                return cuts[0] if len(cuts) == 1 else (cuts[0].astype(F32) + cuts[1].astype(F32)).astype(kind)

            keep = pick(mine)
            came = yield pick(1 - mine), stage
            parts = [keep, came]
        return parts[0].astype(F32) + parts[1].astype(F32)

    return Chain(work(), groups)


def reduce_relative(keep, send, groups):
    def work():
        live, order = half_stages(), sum(groups, [])
        came = yield send, order[0]
        assert order[0] == live[0]
        live.remove(order[0])
        shape = (2,) * len(live) + (-1, send.shape[-1])
        parts = [keep().reshape(shape), came.reshape(shape)]
        for stage in order[1:]:
            place = live.index(stage)
            live.remove(stage)

            def pick(which):
                cuts = [lax.index_in_dim(part, which, place, False).astype(F32) for part in parts]
                return (cuts[0] + cuts[1]).astype(BF)

            kept = pick(0)
            came = yield pick(1), stage
            parts = [kept, came]
        return parts[0].astype(F32) + parts[1].astype(F32)

    return Chain(work(), groups)


def turned(value):
    stages = half_stages()
    shape = value.shape
    value = value.reshape((2,) * len(stages) + shape[1:])
    side, deep = len(first_stages()), len(plane_stages())
    order = list(range(side, 2 * side)) + list(range(side)) + list(reversed(range(2 * side, 2 * side + deep)))
    order += list(range(2 * side + deep, value.ndim))
    return value.transpose(order).reshape(shape)


def join_halves(mine, theirs):
    chips = 1 << len(half_stages())
    planes = lax.axis_size("gy")
    first = lax.axis_index("gc") == 0
    shape = (chips, -1) + mine.shape[1:]
    mine, theirs = mine.reshape(shape), theirs.reshape(shape)
    both = [jnp.where(first, mine, theirs), turned(jnp.where(first, theirs, mine))]
    both = [half.reshape((chips // planes, planes) + half.shape[1:]) for half in both]
    return jnp.stack(both, axis=1).reshape((-1,) + mine.shape[2:])


def cut_half(value, which):
    chips = 1 << len(half_stages())
    planes = lax.axis_size("gy")
    shape = value.shape
    value = value.reshape((chips // planes, 2, planes, -1) + shape[1:])
    halves = [value[:, core].reshape((chips, -1) + shape[1:]) for core in range(2)]
    return jnp.where(which == 0, halves[0], turned(halves[1])).reshape((-1,) + shape[1:])


def sum_rows(value, stages):
    def work():
        held = value
        for stage in stages:
            halves = held.reshape((2, held.shape[0] // 2) + held.shape[1:])
            mine = my_bit(stage)
            keep = lax.dynamic_index_in_dim(halves, mine, 0, False)
            came = yield lax.dynamic_index_in_dim(halves, 1 - mine, 0, False), stage
            held = keep + came
        return held

    return Chain(work(), [[stage] for stage in stages])


def spread_rows(value, stages):
    def work():
        held = value
        for stage in stages:
            came = yield held, stage
            first = my_bit(stage) == 0
            held = jnp.concatenate([jnp.where(first, held, came), jnp.where(first, came, held)], axis=0)
        return held

    return Chain(work(), [[stage] for stage in stages])


def plane_sum(rounds, value, others):
    core = lax.axis_index("gc")
    halves = value.reshape((2, value.shape[0] // 2) + value.shape[1:])

    def over_cores(mine, theirs):
        return mine + peer(theirs)

    held = rounds.go(
        others(),
        over_cores,
        lax.dynamic_index_in_dim(halves, core, 0, False),
        lax.dynamic_index_in_dim(halves, 1 - core, 0, False),
    )
    stages = first_stages() + second_stages()
    for make, order in ((sum_rows, stages), (spread_rows, stages[::-1])):
        chain = make(held, order)
        while not chain.done:
            rounds.go([chain] + others())
        held = chain.out
    came = rounds.go(others(), peer, held)
    return jnp.concatenate([jnp.where(core == 0, held, came), jnp.where(core == 0, came, held)], axis=0)


def token_mask(placement, counts):
    slot_count = placement.shape[0]
    live = (jnp.arange(slot_count, dtype=jnp.int32) < counts[0]).astype(F32)
    inner = jnp.arange(WIN * WIN, dtype=jnp.int32)
    row_pos = placement[:, 0:1] * WIN + inner[None, :] // WIN
    col_pos = placement[:, 1:2] * WIN + inner[None, :] % WIN
    inside = ((row_pos < GRID) & (col_pos < GRID)).astype(F32)
    return inside * live[:, None]


def normalised(value):
    centred = value - jnp.mean(value, axis=-1, keepdims=True)
    inverse = lax.rsqrt(jnp.mean(centred * centred, axis=-1, keepdims=True) + NORM_EPSILON)
    return centred * inverse, inverse


def norm_back(grad, hat, inverse, gain):
    scaled = grad * gain
    mean_one = jnp.mean(scaled, axis=-1, keepdims=True)
    mean_two = jnp.mean(scaled * hat, axis=-1, keepdims=True)
    return inverse * (scaled - mean_one - hat * mean_two)


def pad_slots(value, rows):
    slots, given, width = value.shape
    return jnp.pad(value, ((0, 0), (0, rows - given), (0, 0))).reshape(slots * rows, width)


def widen_slots(value):
    return pad_slots(value.reshape(-1, ROWS, value.shape[1]), LANES)


def narrow_slots(value):
    return value.reshape(-1, LANES, value.shape[1])[:, :ROWS].reshape(-1, value.shape[1])


def body(
    windows,
    cotangent,
    placement,
    counts,
    qkv_weight,
    proj_weight,
    up_weight,
    down_weight,
    qkv_moment,
    proj_moment,
    up_moment,
    down_moment,
    vectors,
    vector_moment,
    rel_pos,
    rel_moment,
):
    core = lax.axis_index("gc")
    planes = lax.axis_size("gy")
    chips = 1 << len(half_stages())
    devices = 2 * chips
    slots, tokens, _ = windows.shape
    wide = slots * LANES
    first, second, deep = first_stages(), second_stages(), plane_stages()
    rounds = Rounds()

    def block(work, *values):
        shapes = jax.eval_shape(work, *values)

        def idle(*_):
            return jax.tree.map(lambda item: jnp.zeros(item.shape, item.dtype), shapes)

        return lax.cond(counts[0] > 0, work, idle, *values)

    mask = pad_slots(token_mask(placement, counts)[:, :, None], ROWS)
    short_low = pad_slots(windows, ROWS) * mask.astype(BF)
    out_low = pad_slots(cotangent, ROWS) * mask.astype(BF)
    count = short_low.shape[0]
    by_z, by_second, by_first = gather_groups()
    part, spare = qkv_weight.shape[1], vectors.shape[0]
    vec_rows = jnp.pad(vectors.astype(BF)[None], ((0, 7), (0, D - spare)))
    take_qkv = gather_half(jnp.concatenate([qkv_weight.astype(BF).T, vec_rows], axis=0))
    take_proj = gather_half(proj_weight.astype(BF))
    take_up = gather_relative(up_weight.astype(BF).T, by_z + by_second + by_first)
    take_down = gather_relative(down_weight.astype(BF), by_second + by_z + by_first)

    def spread_chain(value, stages):
        def work():
            held = value
            for stage in stages:
                came = yield held, stage
                side = core == 0 if stage == "c" else my_bit(stage) == 0
                held = jnp.stack([jnp.where(side, held, came), jnp.where(side, came, held)])
            return held

        return Chain(work(), [[stage] for stage in stages])

    def ordered_small(value, stages):
        value = value.reshape((2,) * len(stages) + value.shape[len(stages) :])
        order = list(reversed(stages))
        canon = first + second + deep + ["c"]
        value = value.transpose([order.index(stage) for stage in canon] + list(range(len(canon), value.ndim)))
        value = value.reshape((chips, 2) + value.shape[len(canon) :])
        both = jnp.stack([value[:, 0], turned(value[:, 1])], axis=1)
        both = both.reshape((chips // planes, planes, 2) + both.shape[2:])
        return jnp.swapaxes(both, 1, 2).reshape((devices,) + both.shape[3:])

    mask_row = jnp.pad(mask.astype(BF).T, ((0, 7), (0, D - count)))
    rounds.go([take_qkv, take_down])
    short_peer = rounds.go([take_qkv, take_proj], peer, jnp.concatenate([short_low, mask_row], axis=0))
    rounds.go([take_qkv, take_up, take_proj])

    def first_hats(mine, theirs):
        return normalised(mine.astype(F32))[0], normalised(theirs[:count].astype(F32))[0]

    (hat_mine, hat_peer), out_peer = rounds.go(
        [take_qkv, take_up, take_proj],
        lambda one, two, three: (block(first_hats, one, two), peer(three)),
        short_low,
        short_peer,
        out_low,
    )
    qkv_half = take_qkv.out
    wide_part = part + 8

    def slim(value):
        return value.reshape((chips, wide_part) + value.shape[1:])[:, :part].reshape((-1,) + value.shape[1:])

    def stout(value):
        value = value.reshape((chips, part) + value.shape[1:])
        return jnp.pad(value, ((0, 0), (0, 8)) + ((0, 0),) * (value.ndim - 2)).reshape((-1,) + value.shape[2:])

    def to_qkv(qkv_half, hat, vec, live, bias):
        rows = widen_slots(((hat * vec[:D] + vec[D : 2 * D]) * live).astype(BF))
        return (dot_nt(qkv_half, rows) + bias).astype(BF), rows

    def both_qkv(qkv_half, hat_mine, hat_peer, short_peer, mask):
        vec_half = qkv_half.reshape(chips, wide_part, D)[:, part, :spare]
        vec = join_halves(vec_half, peer(vec_half)).reshape(-1).astype(F32)
        bias_qkv = jnp.concatenate([vec[2 * D : 3 * D], jnp.zeros((D,), F32), vec[3 * D : 4 * D]])
        bias_qkv = stout(cut_half(bias_qkv, core))[:, None]
        live = short_peer[count, :count].astype(F32)[:, None]
        theirs, pad_peer = block(to_qkv, qkv_half, hat_peer, vec, live, bias_qkv)
        came = tuple(peer(piece) for piece in jnp.split(theirs, 4, axis=0))
        mine, pad_mine = block(to_qkv, qkv_half, hat_mine, vec, mask, bias_qkv)
        return mine, came, vec, pad_mine, pad_peer

    qkv_mine, qkv_came, vec, pad_mine, pad_peer = rounds.go(
        [take_up, take_proj, take_down], both_qkv, qkv_half, hat_mine, hat_peer, short_peer, mask
    )
    proj_half = take_proj.out
    gain_one, shift_one, _, _, bias_proj, gain_two, shift_two, bias_down = (
        vec[index * D : (index + 1) * D] for index in range(8)
    )
    bias_up = relative(cut_half(vec[8 * D :], core).reshape(chips, -1)).reshape(1, -1)
    middle_rows = jnp.pad(jnp.stack([bias_proj, gain_two, shift_two, gain_one]), ((0, 4), (0, 0)))
    rel_low = rel_pos.astype(BF)[:, ::-1]
    rel_rows = jnp.pad(rel_low, ((0, 0), (0, 5), (0, 0))).reshape(64, HD)
    rel_cols = jnp.concatenate([rel_rows, rel_rows], axis=0).T

    def to_attended(mine, came, proj_half, out_low, out_peer):
        proj_came = peer(proj_half)
        qkv = join_halves(slim(mine), slim(jnp.concatenate(came, axis=0))).reshape(3, HEADS, HD, wide)
        attended, probs = attend(qkv, rel_rows)
        out_both = jnp.concatenate([out_low, out_peer], axis=0)
        return join_halves(proj_half, proj_came), out_both, qkv, attended, probs

    proj_full, out_both, qkv, attended, probs = rounds.go(
        [take_up, take_down], to_attended, qkv_mine, qkv_came, proj_half, out_low, out_peer
    )
    attended = attended.reshape(D, wide)
    up_halves = take_up.out
    width = up_halves[0].shape[0]

    def to_gelu(mine, came, up_full, out_both):
        both = jnp.concatenate([mine, came], axis=0)
        pre = dot_nt(both, up_full) + bias_up
        bell = jnp.exp(-0.5 * pre * pre)
        below = 0.5 * (1.0 + lax.erf(pre * (0.5**0.5)))
        gelu = (pre * below).astype(BF)
        slope = (below + pre * bell * (2.0 * math.pi) ** -0.5).astype(BF)
        return both, gelu, slope, dot_tn(gelu, out_both).astype(BF)

    def to_hidden(attended, up_one, up_two):
        middle, normed = to_middle(attended, proj_full, short_low, mask, middle_rows)
        came = peer(normed)
        up_full = jnp.concatenate([up_one, up_two], axis=0)
        return middle, up_full, *to_gelu(normed, came, up_full, out_both)

    middle, up_full, normed_both, gelu_both, slope, grad_down = rounds.go(
        [take_down], to_hidden, attended, *up_halves
    )
    down_halves = take_down.out

    by_first, by_second, by_z = reduce_groups()
    mixed_order = by_first + by_z + by_second
    plane_last = by_first + by_second + by_z
    give_down = reduce_relative(lambda: grad_down[:width], grad_down[width:], mixed_order)

    def to_pre(down_one, down_two, out_both, slope, up_full):
        down_full = jnp.concatenate([down_one, down_two], axis=0)
        pre = (dot_nt(out_both, down_full) * slope.astype(F32)).astype(BF)
        return down_full, pre, dot_nn(pre[count:], up_full).astype(BF)

    def second_mine(pre, up_full):
        return dot_nn(pre[:count], up_full)

    def up_back(pre, normed_both):
        return dot_tn(pre, normed_both).astype(BF), jnp.sum(pre, axis=0, dtype=F32)

    def to_branch(down_one, down_two, out_both, slope, up_full, normed_both, middle):
        down_full, pre, theirs = to_pre(down_one, down_two, out_both, slope, up_full)
        came = peer(theirs)
        grad_up, up_bias = block(up_back, pre, normed_both)
        given = (block(second_mine, pre, up_full), came, middle, out_low, mask, middle_rows)
        shapes = (((count, D), F32), ((wide, D), BF), ((8, D), F32))
        outs = [jax.ShapeDtypeStruct(*shape) for shape in shapes]
        return down_full, grad_up, up_bias, *by_slots(second_norm_kernel, "second_norm", given, outs)

    down_full, grad_up, up_bias, grad_total, branch_pad, second_sums = rounds.go(
        [give_down], to_branch, *down_halves, out_both, slope, up_full, normed_both, middle
    )
    give_up = reduce_relative(lambda: grad_up[:width], grad_up[width:], plane_last)

    def attention_back(branch_pad, attended):
        grad_proj = dot_nn(attended, branch_pad).astype(BF)
        proj_came = peer(cut_half(grad_proj, 1 - core))
        grad_att = dot_nt(proj_full, branch_pad).astype(BF).reshape(HEADS, HD, wide)
        grad_qkv, grad_rel = attend_back(qkv, grad_att, probs, rel_cols)
        grad_qkv = grad_qkv.reshape(3 * D, wide)
        grad_proj = (cut_half(grad_proj, core).astype(F32) + proj_came.astype(F32)).astype(BF)
        halves = [stout(cut_half(grad_qkv, which)) for which in (core, 1 - core)]
        return grad_qkv, grad_rel, *halves, grad_proj

    grad_qkv, grad_rel, qkv_grad_mine, qkv_grad_theirs, grad_proj = rounds.go(
        [give_up, give_down], attention_back, branch_pad, attended
    )
    give_proj = reduce_half(grad_proj, plane_last)
    normed_pad = jnp.concatenate([pad_mine, pad_peer], axis=0)

    def qkv_back(mine, came, normed_pad):
        both = jnp.concatenate([mine, came], axis=1)
        return both, dot_nn(both, normed_pad).astype(BF)

    def to_qkv_grad(mine, theirs, normed_pad):
        return qkv_back(mine, peer(theirs), normed_pad)

    qkv_grad_both, grad_qkv_half = rounds.go(
        [give_up, give_down, give_proj], to_qkv_grad, qkv_grad_mine, qkv_grad_theirs, normed_pad
    )
    give_qkv = reduce_half(grad_qkv_half, plane_last)

    def first_theirs(both, weight):
        return narrow_slots(dot_tn(both[:, wide:], weight).astype(BF))

    def first_mine(both, weight):
        return dot_tn(both[:, :wide], weight)

    def mlp_theirs(gelu_both, down_full):
        return dot_nn(gelu_both[count:], down_full).astype(BF)

    def mlp_mine(gelu_both, down_full, came, middle):
        mlp_out = dot_nn(gelu_both[:count], down_full) + came.astype(F32) + bias_down
        return ((middle + mlp_out) * mask).astype(BF).reshape(slots, ROWS, D)[:, :tokens]

    def for_peer(both, weight, gelu_both, down_full):
        return block(first_theirs, both, weight), block(mlp_theirs, gelu_both, down_full)

    first_sent, mlp_sent = rounds.go(
        [give_qkv, give_up, give_down, give_proj], for_peer, qkv_grad_both, qkv_half, gelu_both, down_full
    )

    stride = max(planes // 4, 1)
    homes = {"down": 0, "qkv": stride, "up": 2 * stride, "proj": 3 * stride}
    me_z = lax.axis_index("gy")
    room = max(up_weight.shape[1], down_weight.shape[0], part, proj_weight.shape[0])
    pieces = [[] for _ in range(planes)]

    def home(**lows):
        parts = []
        for far in range(planes):
            value = sum(
                jnp.where((me_z ^ far) == homes[name], low, jnp.zeros_like(low)) for name, low in lows.items()
            )
            if far:
                value = lax.ppermute(value, "gy", [(homes[name] ^ far, homes[name]) for name in lows])
            parts.append(value)
        return parts

    def arrive(parts):
        for row, piece in zip(pieces, parts):
            row.append(jnp.pad(piece, ((0, room - piece.shape[0]), (0, 0))))

    def moment(old, grad, flip):
        new = MOMENT_MATRIX * old + (grad.T if flip else grad)
        return new, (new.T if flip else new).astype(BF)

    first_came, mlp_came = rounds.go(
        [give_qkv, give_up, give_proj], lambda one, two: (peer(one), peer(two)), first_sent, mlp_sent
    )
    new_down, low_down = moment(down_moment, give_down.out, False)
    new_up, low_up = moment(up_moment, give_up.out, True)

    def to_ends(low_down, low_up, both, weight, first_came, grad_total, short_low, gelu_both, down_full, mlp_came, middle):
        arrived = home(down=low_down, up=low_up)
        given = (block(first_mine, both, weight), first_came, short_low, grad_total, mask, middle_rows)
        outs = [jax.ShapeDtypeStruct((slots, tokens, D), F32), jax.ShapeDtypeStruct((8, D), F32)]
        grad_input, sums = by_slots(first_norm_kernel, "first_norm", given, outs)
        return arrived, grad_input, sums, block(mlp_mine, gelu_both, down_full, mlp_came, middle)

    arrived, grad_input, first_sums, block_out = rounds.go(
        [give_qkv, give_proj],
        to_ends,
        low_down,
        low_up,
        qkv_grad_both,
        qkv_half,
        first_came,
        grad_total,
        short_low,
        gelu_both,
        down_full,
        mlp_came,
        middle,
    )
    arrive(arrived)
    new_proj, low_proj = moment(proj_moment, give_proj.out, False)

    def to_small(low_proj, first_sums, grad_qkv, branch_pad, second_sums, out_low, up_bias, grad_rel):
        up_bias = relative(up_bias.reshape(chips, -1))
        up_bias = [jnp.where(core == 0, up_bias, 0.0), turned(jnp.where(core == 0, 0.0, up_bias))]
        up_bias = jnp.stack(up_bias, axis=1).reshape(chips // planes, planes, 2, -1)
        up_bias = jnp.swapaxes(up_bias, 1, 2).reshape(FF)
        qkv_bias_grad = jnp.sum(grad_qkv, axis=1, dtype=F32)
        vec_grad = [
            first_sums[0],
            first_sums[1],
            qkv_bias_grad[:D],
            qkv_bias_grad[2 * D :],
            jnp.sum(branch_pad, axis=0, dtype=F32),
            second_sums[0],
            second_sums[1],
            jnp.sum(out_low, axis=0, dtype=F32),
            up_bias,
        ]
        small = [jnp.concatenate(vec_grad).reshape(devices, -1), grad_rel.reshape(devices, -1)]
        small = jnp.concatenate(small, axis=1)
        return home(proj=low_proj), cut_half(small, core) + peer(cut_half(small, 1 - core))

    arrived, small = rounds.go(
        [give_qkv, give_proj],
        to_small,
        low_proj,
        first_sums,
        grad_qkv,
        branch_pad,
        second_sums,
        out_low,
        up_bias,
        grad_rel,
    )
    arrive(arrived)
    while not give_qkv.done:
        rounds.go([give_qkv])
    new_qkv, low_qkv = moment(qkv_moment, give_qkv.out[:part], True)
    give_small = reduce_half(small, plane_last, F32)
    arrive(rounds.go([give_small], lambda value: home(qkv=value), low_qkv))
    held = jnp.concatenate([sum(row[1:], row[0]) for row in pieces], axis=0)
    small_order = deep + second + first + ["c"]
    take_rel = []

    def small_chains():
        if not give_small.done:
            return [give_small]
        if not take_rel:
            take_rel.append(spread_chain(give_small.out.reshape(1, -1)[:, vectors.shape[0] :], small_order))
        return take_rel

    gram = plane_sum(rounds, upper_blocks(dot_tn(held, held)), small_chains)
    def send_back(ortho):
        back = [ortho[0]]
        for far in range(1, planes):
            back.append(lax.ppermute(ortho[far], "gy", [(place, place ^ far) for place in range(planes)]))
        return jnp.stack(back)

    (ortho,) = rounds.go(small_chains(), lambda *pair: (chain(*pair),), gram, held)
    back = rounds.go(small_chains(), send_back, ortho.reshape(planes, room, D))
    while not (give_small.done and small_chains()[0].done):
        rounds.go(small_chains())
    vec_total = give_small.out.reshape(-1)[: vectors.shape[0]]
    rel_total = ordered_small(take_rel[0].out, small_order).reshape(2, 32, HD)

    def part_of(name, rows):
        return lax.dynamic_index_in_dim(back, me_z ^ homes[name], 0, False)[:rows].astype(F32)

    parts = [
        part_of("qkv", qkv_weight.shape[1]),
        part_of("proj", proj_weight.shape[0]),
        part_of("up", up_weight.shape[1]),
        part_of("down", down_weight.shape[0]),
    ]

    scales = (math.sqrt(3.0), 1.0, math.sqrt(max(1.0, FF / D)), math.sqrt(max(1.0, D / FF)))
    masters = (qkv_weight, proj_weight, up_weight, down_weight)
    flipped = (True, False, True, False)
    new_weights = [
        master - RATE_MATRIX * factor * (part.T if turn else part)
        for master, factor, part, turn in zip(masters, scales, parts, flipped)
    ]

    rate_vec = 0.5 / math.sqrt(float(devices * slots * tokens))
    vec_moment_new = MOMENT_VECTOR * vector_moment + vec_total
    rel_grad = rel_total[:, : 2 * WIN - 1][:, ::-1]
    rel_moment_new = MOMENT_VECTOR * rel_moment + rel_grad
    return (
        block_out,
        grad_input,
        new_qkv,
        new_proj,
        new_up,
        new_down,
        new_weights[0],
        new_weights[1],
        new_weights[2],
        new_weights[3],
        vec_moment_new,
        vectors - rate_vec * vec_moment_new,
        rel_moment_new,
        rel_pos - 0.2 * rate_vec * rel_moment_new,
    )


def solution(mesh):
    size_x, size_y = mesh.shape["gx"], mesh.shape["gy"]
    side = math.isqrt(size_x // 2)
    assert side * side * 2 == size_x
    grid = (side, size_x // 2 // side, 2, size_y)
    split = Mesh(mesh.devices.reshape(grid), ("ga", "gb", "gc", "gy"))
    flat = ("ga", "gb", "gc", "gy")
    slab, cols, rows, line = P(flat, None, None), P(None, flat), P(flat, None), P(flat)
    return jax.shard_map(
        body,
        mesh=split,
        in_specs=(
            (slab, slab, rows, line) + (cols, rows, cols, rows) * 2 + (line, line, P(), P())
        ),
        out_specs=(
            (slab, slab) + (cols, rows, cols, rows) * 2 + (line, line, P(), P())
        ),
        check_vma=False,
    )
```

```python
from functools import partial
import math

import jax
import jax.numpy as jnp
from jax import lax
from jax.experimental import pallas as pl
from jax.experimental.pallas import tpu as pltpu
from jax.sharding import Mesh, PartitionSpec as P

D = 1280
FF = 5120
HEADS = 16
HD = 80
WIN = 14
GRID = 64
ITERS = 5
LANES = 256
ROWS = 208

NORM_EPSILON = 1e-06
ORTHO_EPSILON = 1e-07
COEFF_LINEAR = 3.4445
COEFF_CUBIC = -4.775
COEFF_QUINTIC = 2.0315
MOMENT_MATRIX = 0.95
MOMENT_VECTOR = 0.9
RATE_MATRIX = 0.5

BF = jnp.bfloat16
F32 = jnp.float32


def dot_nn(left, right):
    return jnp.dot(left, right, preferred_element_type=F32)


def dot_tn(left, right):
    return lax.dot_general(left, right, (((0,), (0,)), ((), ())), preferred_element_type=F32)


def dot_nt(left, right):
    return lax.dot_general(left, right, (((1,), (1,)), ((), ())), preferred_element_type=F32)


def split_low(value):
    high = value.astype(BF)
    return high, (value - high.astype(F32)).astype(BF)


GROUP = 8


def spots():
    row = lax.broadcasted_iota(jnp.int32, (32, LANES), 0)
    lane = lax.broadcasted_iota(jnp.int32, (32, LANES), 1)
    along = jnp.where(row < 16, lane // WIN, lane % WIN + 16)
    return jnp.where((along == row) & (lane < WIN * WIN), 1.0, 0.0).astype(BF)


def shifts():
    lane = lax.broadcasted_iota(jnp.int32, (32, LANES), 1)
    down_h = jnp.maximum(WIN - 1 - lane // WIN, 0)
    return down_h, WIN - 1 - lane % WIN


def barrel(value, amount, up):
    for bit in (1, 2, 4, 8):
        moved = pltpu.roll(value, 32 - bit if up else bit, 0)
        value = jnp.where((amount & bit) != 0, moved, value)
    return value


def attend_kernel(q_ref, k_ref, v_ref, rel_ref, out_ref, probs_ref):
    marks = spots()
    marks2 = jnp.concatenate([marks, marks], axis=0)
    shift_h, shift_w = shifts()
    tail_row = lax.broadcasted_iota(jnp.int32, (16, LANES), 0) + (ROWS - 16)
    pad = jnp.zeros((LANES - ROWS, LANES), BF)
    scale = HD ** (-0.5) / math.log(2.0)
    for head in range(GROUP):
        query = q_ref[0, head]
        rel_q = dot_nn(rel_ref[...], query) * (HD**0.5)
        along_h = barrel(rel_q[:32], shift_h, True)[:16]
        along_w = barrel(rel_q[32:], shift_w, True)[:16]
        high, rest = split_low(jnp.concatenate([along_h, along_w], axis=0))
        query_all = jnp.concatenate([query, high, rest], axis=0)
        key_all = jnp.concatenate([k_ref[0, head], marks2], axis=0)
        scores = dot_tn(key_all, query_all)[:ROWS]
        tail = jnp.where(tail_row < WIN * WIN, scores[ROWS - 16 :], -1e30)
        scores = jnp.concatenate([scores[: ROWS - 16], tail], axis=0)
        peak = jnp.max(scores, axis=0, keepdims=True)
        exponent = jnp.exp2((scores - peak) * scale)
        probs = (exponent * (1.0 / jnp.sum(exponent, axis=0, keepdims=True))).astype(BF)
        probs_ref[0, head] = probs
        out_ref[head] = dot_nn(v_ref[0, head], jnp.concatenate([probs, pad], axis=0)).astype(BF)


def attend(qkv, rel_rows):
    slots = qkv.shape[-1] // LANES
    cut = lambda part: pl.BlockSpec((1, GROUP, HD, LANES), lambda s, g, part=part: (part, g, 0, s))
    return pl.pallas_call(
        attend_kernel,
        grid=(slots, HEADS // GROUP),
        in_specs=[cut(0), cut(1), cut(2), pl.BlockSpec((64, HD), lambda s, g: (0, 0))],
        out_specs=[
            pl.BlockSpec((GROUP, HD, LANES), lambda s, g: (g, 0, s)),
            pl.BlockSpec((1, GROUP, ROWS, LANES), lambda s, g: (s, g, 0, 0)),
        ],
        out_shape=[
            jax.ShapeDtypeStruct((HEADS, HD, slots * LANES), BF),
            jax.ShapeDtypeStruct((slots, HEADS, ROWS, LANES), BF),
        ],
        compiler_params=pltpu.CompilerParams(vmem_limit_bytes=16 * 2**20),
        cost_estimate=cheap(slots * HEADS * 2 * LANES * LANES * 256),
        name="attend",
    )(qkv, qkv, qkv, rel_rows)


def attend_back_kernel(q_ref, k_ref, v_ref, g_ref, probs_ref, rel_ref, out_ref, drel_ref):
    marks = spots()
    shift_h, shift_w = shifts()
    pad = jnp.zeros((LANES - ROWS, LANES), BF)
    none = jnp.zeros((16, LANES), F32)
    scale = HD ** (-0.5)
    total = jnp.zeros((64, HD), F32)
    for head in range(GROUP):
        query = q_ref[0, head]
        grad = g_ref[head]
        probs_low = probs_ref[0, head]
        probs = probs_low.astype(F32)
        weighted = dot_tn(v_ref[0, head], grad)[:ROWS] * probs
        flow = jnp.sum(weighted, axis=0, keepdims=True)
        score_low = jnp.concatenate([(weighted - probs * flow).astype(BF), pad], axis=0)
        out_ref[2, head] = dot_nt(grad, jnp.concatenate([probs_low, pad], axis=0)).astype(BF)
        out_ref[1, head] = (dot_nt(query, score_low) * scale).astype(BF)
        mixed = dot_nn(jnp.concatenate([k_ref[0, head], marks], axis=0), score_low)
        rows_h = barrel(jnp.concatenate([mixed[HD : HD + 16], none], axis=0), shift_h, False)
        rows_w = barrel(jnp.concatenate([mixed[HD + 16 :], none], axis=0), shift_w, False)
        both = jnp.concatenate(split_low(jnp.concatenate([rows_h, rows_w], axis=0)), axis=0)
        out_ref[0, head] = (mixed[:HD] * scale + dot_nn(rel_ref[...], both)).astype(BF)
        parts = dot_nt(both, query)
        total = total + parts[:64] + parts[64:]

    @pl.when((pl.program_id(0) == 0) & (pl.program_id(1) == 0))
    def _():
        drel_ref[...] = jnp.zeros_like(drel_ref)

    drel_ref[...] += total


def attend_back(qkv, grad, probs, rel_cols):
    slots = qkv.shape[-1] // LANES
    cut = lambda part: pl.BlockSpec((1, GROUP, HD, LANES), lambda s, g, part=part: (part, g, 0, s))
    return pl.pallas_call(
        attend_back_kernel,
        grid=(slots, HEADS // GROUP),
        in_specs=[
            cut(0),
            cut(1),
            cut(2),
            pl.BlockSpec((GROUP, HD, LANES), lambda s, g: (g, 0, s)),
            pl.BlockSpec((1, GROUP, ROWS, LANES), lambda s, g: (s, g, 0, 0)),
            pl.BlockSpec((HD, 128), lambda s, g: (0, 0)),
        ],
        out_specs=[
            pl.BlockSpec((3, GROUP, HD, LANES), lambda s, g: (0, g, 0, s)),
            pl.BlockSpec((64, HD), lambda s, g: (0, 0)),
        ],
        out_shape=[
            jax.ShapeDtypeStruct((3, HEADS, HD, slots * LANES), BF),
            jax.ShapeDtypeStruct((64, HD), F32),
        ],
        compiler_params=pltpu.CompilerParams(vmem_limit_bytes=20 * 2**20),
        cost_estimate=cheap(slots * HEADS * 5 * LANES * LANES * 256),
        name="attend_back",
    )(qkv, qkv, qkv, grad, probs, rel_cols)


def resident(shape):
    return pl.BlockSpec(shape, lambda *_: (0,) * len(shape))


def cheap(flops):
    return pl.CostEstimate(flops=flops // 8, bytes_accessed=1_000_000, transcendentals=0)


def settings(mebibytes):
    return pltpu.CompilerParams(vmem_limit_bytes=mebibytes * 2**20)


def middle_kernel(att_ref, proj_ref, short_ref, mask_ref, rows_ref, middle_ref, normed_ref):
    branch = dot_tn(att_ref[...], proj_ref[...])[:ROWS] + rows_ref[0:1]
    middle = (short_ref[...].astype(F32) + branch) * mask_ref[...]
    middle_ref[...] = middle
    centred = middle - jnp.mean(middle, axis=1, keepdims=True)
    inverse = lax.rsqrt(jnp.mean(centred * centred, axis=1, keepdims=True) + NORM_EPSILON)
    normed_ref[...] = (centred * inverse * rows_ref[1:2] + rows_ref[2:3]).astype(BF)


def to_middle(attended, proj_full, short, mask, rows):
    slots = attended.shape[1] // LANES
    by_slot = lambda width: pl.BlockSpec((ROWS, width), lambda s: (s, 0))
    return pl.pallas_call(
        middle_kernel,
        grid=(slots,),
        in_specs=[
            pl.BlockSpec((D, LANES), lambda s: (0, s)),
            resident((D, D)),
            by_slot(D),
            by_slot(1),
            resident((8, D)),
        ],
        out_specs=[by_slot(D), by_slot(D)],
        out_shape=[
            jax.ShapeDtypeStruct((slots * ROWS, D), F32),
            jax.ShapeDtypeStruct((slots * ROWS, D), BF),
        ],
        compiler_params=settings(24),
        cost_estimate=cheap(2 * slots * LANES * D * D),
        name="middle",
    )(attended, proj_full, short, mask, rows)


def norm_parts(grad, value, gain):
    centred = value - jnp.mean(value, axis=1, keepdims=True)
    inverse = lax.rsqrt(jnp.mean(centred * centred, axis=1, keepdims=True) + NORM_EPSILON)
    hat = centred * inverse
    scaled = grad * gain
    mean_one = jnp.mean(scaled, axis=1, keepdims=True)
    mean_two = jnp.mean(scaled * hat, axis=1, keepdims=True)
    sums = [jnp.sum(grad * hat, axis=0, keepdims=True), jnp.sum(grad, axis=0, keepdims=True)]
    sums = jnp.concatenate(sums + [jnp.zeros((6, D), F32)], axis=0)
    return inverse * (scaled - mean_one - hat * mean_two), sums


def add_sums(sums_ref, sums):
    @pl.when(pl.program_id(0) == 0)
    def _():
        sums_ref[...] = jnp.zeros_like(sums_ref)

    sums_ref[...] += sums


def second_norm_kernel(grad_ref, came_ref, middle_ref, out_ref, mask_ref, rows_ref, total_ref, pad_ref, sums_ref):
    grad = grad_ref[...] + came_ref[...].astype(F32)
    back, sums = norm_parts(grad, middle_ref[...], rows_ref[1:2])
    total = (out_ref[...].astype(F32) + back) * mask_ref[...]
    total_ref[...] = total
    low = total.astype(BF)
    pad_ref[...] = jnp.concatenate([low, jnp.zeros((LANES - ROWS, D), BF)], axis=0)
    add_sums(sums_ref, sums)


def first_norm_kernel(grad_ref, came_ref, short_ref, total_ref, mask_ref, rows_ref, out_ref, sums_ref):
    mask = mask_ref[...]
    grad = (grad_ref[:ROWS] + came_ref[...].astype(F32)) * mask
    back, sums = norm_parts(grad, short_ref[...].astype(F32), rows_ref[3:4])
    out_ref[0] = ((total_ref[...] + back) * mask)[: WIN * WIN]
    add_sums(sums_ref, sums)


def by_slots(kernel, name, given, outs):
    slots = given[1].shape[0] // ROWS

    def spec(shape):
        if len(shape) == 3:
            return pl.BlockSpec((1,) + shape[1:], lambda s: (s, 0, 0))
        if shape[0] == 8:
            return resident(shape)
        return pl.BlockSpec((shape[0] // slots, shape[1]), lambda s: (s, 0))

    return pl.pallas_call(
        kernel,
        grid=(slots,),
        in_specs=[spec(item.shape) for item in given],
        out_specs=[spec(item.shape) for item in outs],
        out_shape=list(outs),
        compiler_params=settings(32),
        cost_estimate=cheap(1_000_000),
        name=name,
    )(*given)


SIDE = 256
SPOTS = [(row, column) for row in range(D // SIDE) for column in range(row, D // SIDE)]


def upper_blocks(gram):
    parts = [
        gram[row * SIDE : (row + 1) * SIDE, column * SIDE : (column + 1) * SIDE] for row, column in SPOTS
    ]
    return jnp.concatenate(parts, axis=0)


def chain_kernel(gram_ref, y_ref, out_ref, high_ref, rest_ref, b_ref, t_high, t_rest, z_high, z_rest):
    columns = [slice(start, start + SIDE) for start in range(0, D, SIDE)]
    row = lax.broadcasted_iota(jnp.int32, (SIDE, SIDE), 0)
    spot = row == lax.broadcasted_iota(jnp.int32, (SIDE, SIDE), 1)
    trace = jnp.zeros((), F32)
    for place, (row, column) in enumerate(SPOTS):
        if row == column:
            trace = trace + jnp.sum(jnp.where(spot, gram_ref[place * SIDE : (place + 1) * SIDE, :], 0.0))
    inverse = 1.0 / (jnp.sqrt(trace) + ORTHO_EPSILON)
    for place, (row, column) in enumerate(SPOTS):
        block = gram_ref[place * SIDE : (place + 1) * SIDE, :] * inverse * inverse
        for part, over, down in ((block, row, column), (block.T, column, row)):
            high, rest = split_low(part)
            high_ref[columns[over], columns[down]] = high
            rest_ref[columns[over], columns[down]] = rest
    z_high[0] = y_ref[...]
    z_rest[0] = jnp.zeros_like(y_ref)

    def polynomial():
        for place, cut in enumerate(columns):
            square = dot_nn(high_ref[...], high_ref[:, cut])
            value = high_ref[:, cut].astype(F32) + rest_ref[:, cut].astype(F32)
            poly = COEFF_CUBIC * value + COEFF_QUINTIC * square
            line = lax.broadcasted_iota(jnp.int32, (D, SIDE), 0) - place * SIDE
            eye = line == lax.broadcasted_iota(jnp.int32, (D, SIDE), 1)
            b_ref[:, cut] = (poly + jnp.where(eye, COEFF_LINEAR, 0.0)).astype(BF)

    def follow(now, cut):
        return dot_nn(z_high[now], b_ref[:, cut]) + dot_nn(z_rest[now], b_ref[:, cut])

    def advance(now, fine):
        later = 1 - now
        polynomial()
        for cut in columns:
            value = dot_nn(b_ref[...], high_ref[:, cut])
            if fine:
                value = value + dot_nn(b_ref[...], rest_ref[:, cut])
            t_high[:, cut], rest = split_low(value)
            if fine:
                t_rest[:, cut] = rest
            z_high[later, :, cut], z_rest[later, :, cut] = split_low(follow(now, cut))
        for cut in columns:
            value = dot_nn(t_high[...], b_ref[:, cut])
            if fine:
                value = value + dot_nn(t_rest[...], b_ref[:, cut])
            high_ref[:, cut], rest_ref[:, cut] = split_low(value)

    @pl.loop(0, ITERS - 2)
    def _(step):
        advance(step % 2, True)

    advance((ITERS - 2) % 2, False)
    polynomial()
    for cut in columns:
        out_ref[:, cut] = (follow((ITERS - 1) % 2, cut) * inverse).astype(BF)


def chain(gram, rows):
    half = pltpu.VMEM((D, D), BF)
    flow = pltpu.VMEM((2,) + rows.shape, BF)
    whole = pl.BlockSpec(memory_space=pltpu.VMEM)
    return pl.pallas_call(
        chain_kernel,
        in_specs=[whole, whole],
        out_specs=whole,
        out_shape=jax.ShapeDtypeStruct(rows.shape, BF),
        scratch_shapes=[half] * 5 + [flow] * 2,
        compiler_params=settings(56),
        cost_estimate=pl.CostEstimate(flops=23 * 2 * D**3, bytes_accessed=6 * D * D, transcendentals=0),
        name="chain",
    )(gram, rows)


EVERY = ("ga", "gb", "gc", "gy")


def peer(value):
    return lax.ppermute(value, "gc", [(0, 1), (1, 0)])


def steps_of(axis):
    return lax.axis_size(axis).bit_length() - 1


def first_stages():
    return [("f", step) for step in reversed(range(steps_of("ga")))]


def second_stages():
    return [("s", step) for step in reversed(range(steps_of("gb")))]


def plane_stages():
    return [("z", step) for step in range(steps_of("gy"))]


def gather_groups():
    deep = plane_stages()
    return [deep[1:][::-1], deep[:1]], [second_stages()[::-1]], [first_stages()[::-1]]


def reduce_groups():
    deep = plane_stages()
    return [first_stages()], [second_stages()], [deep[:1], deep[1:]]


def half_stages():
    return first_stages() + second_stages() + plane_stages()


def bit_of(stage, core):
    kind, step = stage
    if kind == "z":
        return "gy", steps_of("gy") - 1 - step if core == 0 else step
    return ("ga" if (kind == "f") == (core == 0) else "gb"), step


def my_bit(stage):
    values = []
    for core in range(2):
        axis, step = bit_of(stage, core)
        values.append((lax.axis_index(axis) >> step) & 1)
    return jnp.where(lax.axis_index("gc") == 0, values[0], values[1])


def swap(value, stage):
    if stage == "c":
        return peer(value)
    sizes = [lax.axis_size(axis) for axis in EVERY]
    pairs = []
    for place in range(math.prod(sizes)):
        spot, rest = [], place
        for size in reversed(sizes):
            spot.insert(0, rest % size)
            rest //= size
        axis, step = bit_of(stage, spot[2])
        spot[EVERY.index(axis)] ^= 1 << step
        other = 0
        for size, at in zip(sizes, spot):
            other = other * size + at
        pairs.append((place, other))
    return lax.ppermute(value, EVERY, pairs)


class Rounds:
    def __init__(self):
        self.last = None

    def go(self, chains, work=None, *values):
        chains = [chain for chain in chains if not chain.done]
        while long := [chain for chain in chains if chain.left > 1]:
            self.once(long)
        out = self.once(chains, work, *values)
        for chain in chains:
            chain.left = chain.counts.pop(0) if chain.counts else 0
        return out

    def once(self, chains, work=None, *values):
        [chain.look() for chain in chains]
        marks = [] if self.last is None else [self.last]
        held = [lax.optimization_barrier((chain.value, *marks))[0] for chain in chains]
        came = [swap(value, chain.stage) for value, chain in zip(held, chains)]
        ready = lax.optimization_barrier((*values, *held, *marks))
        out = () if work is None else work(*ready[: len(values)])
        leaves, tree = jax.tree.flatten(out)
        ended = lax.optimization_barrier(tuple(came) + tuple(leaves))
        self.last = ended[0]
        for chain, value in zip(chains, ended):
            chain.take(value)
            chain.left -= 1
        return jax.tree.unflatten(tree, ended[len(chains) :])


class Chain:
    def __init__(self, work, groups):
        self.work, self.ended, self.result = work, False, None
        self.pending = [None]
        self.counts = [len(group) for group in groups if group]
        self.left = self.counts.pop(0)

    def take(self, came):
        self.pending = [came]

    def look(self):
        if self.pending:
            try:
                self.value, self.stage = self.work.send(self.pending.pop())
            except StopIteration as stop:
                self.ended, self.result = True, stop.value

    @property
    def done(self):
        self.look()
        return self.ended

    @property
    def out(self):
        self.look()
        return self.result


def gather_half(shard):
    groups = sum(gather_groups(), [])

    def work():
        held = shard[None]
        for stage in sum(groups, []):
            came = yield held, stage
            first = my_bit(stage) == 0
            held = jnp.concatenate([jnp.where(first, held, came), jnp.where(first, came, held)], axis=0)
        return held.reshape(-1, shard.shape[-1])

    return Chain(work(), groups)


def gather_relative(shard, groups):
    def work():
        order, canon = sum(groups, []), half_stages()
        held = shard
        for stage in order[:-1]:
            came = yield held, stage
            held = jnp.stack([held, came])
        came = yield held, order[-1]
        there = order[-2::-1]
        turn = [there.index(stage) for stage in canon[1:]] + [len(there), len(there) + 1]
        return tuple(half.transpose(turn).reshape(-1, shard.shape[-1]) for half in (held, came))

    return Chain(work(), groups)


def relative(value):
    stages = half_stages()
    place = sum(my_bit(stage) << (len(stages) - 1 - at) for at, stage in enumerate(stages))
    spots = jnp.arange(value.shape[0])
    picker = ((spots[:, None] ^ place) == spots[None, :]).astype(F32)
    return jnp.dot(picker, value, precision=lax.Precision.HIGHEST, preferred_element_type=F32)


def reduce_half(grad, groups, kind=BF):
    def work():
        live = half_stages()
        parts = [grad.reshape((2,) * len(live) + (-1, grad.shape[-1]))]
        for stage in sum(groups, []):
            place, mine = live.index(stage), my_bit(stage)
            live.remove(stage)

            def pick(which):
                cuts = [lax.dynamic_index_in_dim(part, which, place, False) for part in parts]
                return cuts[0] if len(cuts) == 1 else (cuts[0].astype(F32) + cuts[1].astype(F32)).astype(kind)

            send = pick(1 - mine)
            parts = list(lax.optimization_barrier((*parts, send))[:-1])
            keep = pick(mine)
            came = yield send, stage
            parts = [keep, came]
        return parts[0].astype(F32) + parts[1].astype(F32)

    return Chain(work(), groups)


def reduce_relative(keep, send, groups):
    def work():
        live, order = half_stages(), sum(groups, [])
        came = yield send, order[0]
        assert order[0] == live[0]
        live.remove(order[0])
        shape = (2,) * len(live) + (-1, send.shape[-1])
        parts = [keep().reshape(shape), came.reshape(shape)]
        for stage in order[1:]:
            place = live.index(stage)
            live.remove(stage)

            def pick(which):
                cuts = [lax.index_in_dim(part, which, place, False).astype(F32) for part in parts]
                return (cuts[0] + cuts[1]).astype(BF)

            away = pick(1)
            parts = list(lax.optimization_barrier((*parts, away))[:-1])
            kept = pick(0)
            came = yield away, stage
            parts = [kept, came]
        return parts[0].astype(F32) + parts[1].astype(F32)

    return Chain(work(), groups)


def turned(value):
    stages = half_stages()
    shape = value.shape
    value = value.reshape((2,) * len(stages) + shape[1:])
    side, deep = len(first_stages()), len(plane_stages())
    order = list(range(side, 2 * side)) + list(range(side)) + list(reversed(range(2 * side, 2 * side + deep)))
    order += list(range(2 * side + deep, value.ndim))
    return value.transpose(order).reshape(shape)


def join_halves(mine, theirs):
    chips = 1 << len(half_stages())
    planes = lax.axis_size("gy")
    first = lax.axis_index("gc") == 0
    shape = (chips, -1) + mine.shape[1:]
    mine, theirs = mine.reshape(shape), theirs.reshape(shape)
    both = [jnp.where(first, mine, theirs), turned(jnp.where(first, theirs, mine))]
    both = [half.reshape((chips // planes, planes) + half.shape[1:]) for half in both]
    return jnp.stack(both, axis=1).reshape((-1,) + mine.shape[2:])


def cut_half(value, which):
    chips = 1 << len(half_stages())
    planes = lax.axis_size("gy")
    shape = value.shape
    value = value.reshape((chips // planes, 2, planes, -1) + shape[1:])
    halves = [value[:, core].reshape((chips, -1) + shape[1:]) for core in range(2)]
    return jnp.where(which == 0, halves[0], turned(halves[1])).reshape((-1,) + shape[1:])


def sum_rows(value, stages):
    def work():
        held = value
        for stage in stages:
            halves = held.reshape((2, held.shape[0] // 2) + held.shape[1:])
            mine = my_bit(stage)
            keep = lax.dynamic_index_in_dim(halves, mine, 0, False)
            came = yield lax.dynamic_index_in_dim(halves, 1 - mine, 0, False), stage
            held = keep + came
        return held

    return Chain(work(), [[stage] for stage in stages])


def spread_rows(value, stages):
    def work():
        held = value
        for stage in stages:
            came = yield held, stage
            first = my_bit(stage) == 0
            held = jnp.concatenate([jnp.where(first, held, came), jnp.where(first, came, held)], axis=0)
        return held

    return Chain(work(), [[stage] for stage in stages])


def plane_sum(rounds, value, work, *values):
    core = lax.axis_index("gc")
    halves = value.reshape((2, value.shape[0] // 2) + value.shape[1:])

    def over_cores(mine, theirs):
        return mine + peer(theirs)

    held = rounds.go(
        [],
        over_cores,
        lax.dynamic_index_in_dim(halves, core, 0, False),
        lax.dynamic_index_in_dim(halves, 1 - core, 0, False),
    )
    stages = first_stages() + second_stages()
    chain = sum_rows(held, stages)
    out = rounds.go([chain], work, *values)
    while not chain.done:
        rounds.go([chain])
    chain = spread_rows(chain.out, stages[::-1])
    while not chain.done:
        rounds.go([chain])
    held = chain.out
    came = rounds.go([], peer, held)
    held = [jnp.where(core == 0, held, came), jnp.where(core == 0, came, held)]
    return jnp.concatenate(held, axis=0), out


def sum_whole(value, stages):
    def work():
        held = value
        for stage in stages:
            came = yield held, stage
            held = held + came
        return held

    return Chain(work(), [[stage] for stage in stages])


def token_mask(placement, counts):
    slot_count = placement.shape[0]
    live = (jnp.arange(slot_count, dtype=jnp.int32) < counts[0]).astype(F32)
    inner = jnp.arange(WIN * WIN, dtype=jnp.int32)
    row_pos = placement[:, 0:1] * WIN + inner[None, :] // WIN
    col_pos = placement[:, 1:2] * WIN + inner[None, :] % WIN
    inside = ((row_pos < GRID) & (col_pos < GRID)).astype(F32)
    return inside * live[:, None]


def normalised(value):
    centred = value - jnp.mean(value, axis=-1, keepdims=True)
    inverse = lax.rsqrt(jnp.mean(centred * centred, axis=-1, keepdims=True) + NORM_EPSILON)
    return centred * inverse, inverse


def norm_back(grad, hat, inverse, gain):
    scaled = grad * gain
    mean_one = jnp.mean(scaled, axis=-1, keepdims=True)
    mean_two = jnp.mean(scaled * hat, axis=-1, keepdims=True)
    return inverse * (scaled - mean_one - hat * mean_two)


def pad_slots(value, rows):
    slots, given, width = value.shape
    return jnp.pad(value, ((0, 0), (0, rows - given), (0, 0))).reshape(slots * rows, width)


def widen_slots(value):
    return pad_slots(value.reshape(-1, ROWS, value.shape[1]), LANES)


def narrow_slots(value):
    return value.reshape(-1, LANES, value.shape[1])[:, :ROWS].reshape(-1, value.shape[1])


def body(
    windows,
    cotangent,
    placement,
    counts,
    qkv_weight,
    proj_weight,
    up_weight,
    down_weight,
    qkv_moment,
    proj_moment,
    up_moment,
    down_moment,
    vectors,
    vector_moment,
    rel_pos,
    rel_moment,
):
    core = lax.axis_index("gc")
    planes = lax.axis_size("gy")
    chips = 1 << len(half_stages())
    devices = 2 * chips
    slots, tokens, _ = windows.shape
    wide = slots * LANES
    first, second, deep = first_stages(), second_stages(), plane_stages()
    rounds = Rounds()

    def block(work, *values):
        shapes = jax.eval_shape(work, *values)

        def idle(*_):
            return jax.tree.map(lambda item: jnp.zeros(item.shape, item.dtype), shapes)

        return lax.cond(counts[0] > 0, work, idle, *values)

    mask = pad_slots(token_mask(placement, counts)[:, :, None], ROWS)
    short_low = pad_slots(windows, ROWS) * mask.astype(BF)
    out_low = pad_slots(cotangent, ROWS) * mask.astype(BF)
    count = short_low.shape[0]
    by_z, by_second, by_first = gather_groups()
    part, spare = qkv_weight.shape[1], vectors.shape[0]
    vec_rows = jnp.pad(vectors.astype(BF)[None], ((0, 7), (0, D - spare)))
    take_qkv = gather_half(jnp.concatenate([qkv_weight.astype(BF).T, vec_rows], axis=0))
    take_proj = gather_half(proj_weight.astype(BF))
    take_up = gather_relative(up_weight.astype(BF).T, by_z + by_second + by_first)
    take_down = gather_relative(down_weight.astype(BF), by_second + by_z + by_first)

    mask_row = jnp.pad(mask.astype(BF).T, ((0, 7), (0, D - count)))
    rounds.go([take_qkv, take_down])
    short_peer = rounds.go([take_qkv, take_proj], peer, jnp.concatenate([short_low, mask_row], axis=0))
    rounds.go([take_qkv, take_up, take_proj])

    def first_hats(mine, theirs):
        return normalised(mine.astype(F32))[0], normalised(theirs[:count].astype(F32))[0]

    (hat_mine, hat_peer), out_peer = rounds.go(
        [take_qkv, take_up, take_proj],
        lambda one, two, three: (block(first_hats, one, two), peer(three)),
        short_low,
        short_peer,
        out_low,
    )
    qkv_half = take_qkv.out
    wide_part = part + 8

    def slim(value):
        return value.reshape((chips, wide_part) + value.shape[1:])[:, :part].reshape((-1,) + value.shape[1:])

    def stout(value):
        value = value.reshape((chips, part) + value.shape[1:])
        return jnp.pad(value, ((0, 0), (0, 8)) + ((0, 0),) * (value.ndim - 2)).reshape((-1,) + value.shape[2:])

    def both_qkv(qkv_half, hat_mine, hat_peer, short_peer, mask):
        vec_half = qkv_half.reshape(chips, wide_part, D)[:, part, :spare]
        vec = join_halves(vec_half, peer(vec_half)).reshape(-1).astype(F32)
        bias_qkv = jnp.concatenate([vec[2 * D : 3 * D], jnp.zeros((D,), F32), vec[3 * D : 4 * D]])
        bias_qkv = stout(cut_half(bias_qkv, core))[:, None]
        live = short_peer[count, :count].astype(F32)[:, None]
        pad_peer = widen_slots(((hat_peer * vec[:D] + vec[D : 2 * D]) * live).astype(BF))
        theirs = (dot_nt(qkv_half, pad_peer) + bias_qkv).astype(BF)
        came = peer(theirs)
        pad_mine = widen_slots(((hat_mine * vec[:D] + vec[D : 2 * D]) * mask).astype(BF))
        mine = (dot_nt(qkv_half, pad_mine) + bias_qkv).astype(BF)
        return mine, came, vec, pad_mine, pad_peer

    qkv_mine, qkv_came, vec, pad_mine, pad_peer = rounds.go(
        [take_up, take_proj, take_down], both_qkv, qkv_half, hat_mine, hat_peer, short_peer, mask
    )
    proj_half = take_proj.out
    bias_down = vec[7 * D : 8 * D]
    rel_low = rel_pos.astype(BF)[:, ::-1]
    rel_rows = jnp.pad(rel_low, ((0, 0), (0, 5), (0, 0))).reshape(64, HD)
    rel_cols = jnp.concatenate([rel_rows, rel_rows], axis=0).T

    def to_attended(mine, came, proj_half, out_low, out_peer, vec):
        proj_came = peer(proj_half)
        qkv = join_halves(slim(mine), slim(came)).reshape(3, HEADS, HD, wide)
        attended, probs = attend(qkv, rel_rows)
        out_both = jnp.concatenate([out_low, out_peer], axis=0)
        bias_up = relative(cut_half(vec[8 * D :], core).reshape(chips, -1)).reshape(1, -1)
        table = vec[: 8 * D].reshape(8, D)
        middle_rows = jnp.concatenate([table[4:7], table[:1], table[:4]], axis=0)
        return join_halves(proj_half, proj_came), out_both, qkv, attended, probs, bias_up, middle_rows

    proj_full, out_both, qkv, attended, probs, bias_up, middle_rows = rounds.go(
        [take_up, take_down], to_attended, qkv_mine, qkv_came, proj_half, out_low, out_peer, vec
    )
    attended = attended.reshape(D, wide)
    up_halves = take_up.out
    width = up_halves[0].shape[0]

    def to_gelu(mine, came, up_full, out_both):
        both = jnp.concatenate([mine, came], axis=0)
        pre = dot_nt(both, up_full) + bias_up
        bell = jnp.exp(-0.5 * pre * pre)
        below = 0.5 * (1.0 + lax.erf(pre * (0.5**0.5)))
        gelu = (pre * below).astype(BF)
        slope = (below + pre * bell * (2.0 * math.pi) ** -0.5).astype(BF)
        send = dot_tn(gelu[:, width:], out_both).astype(BF)
        return both, gelu, slope, dot_tn(gelu[:, :width], out_both).astype(BF), send

    def to_hidden(attended, up_one, up_two):
        middle, normed = to_middle(attended, proj_full, short_low, mask, middle_rows)
        came = peer(normed)
        up_full = jnp.concatenate([up_one, up_two], axis=0)
        return middle, up_full, *to_gelu(normed, came, up_full, out_both)

    middle, up_full, normed_both, gelu_both, slope, keep_down, send_down = rounds.go(
        [take_down], to_hidden, attended, *up_halves
    )
    down_halves = take_down.out

    by_first, by_second, by_z = reduce_groups()
    mixed_order = by_first + by_z + by_second
    plane_last = by_first + by_second + by_z
    give_down = reduce_relative(lambda: keep_down, send_down, mixed_order)

    def to_pre(down_one, down_two, out_both, slope, up_full):
        down_full = jnp.concatenate([down_one, down_two], axis=0)
        pre = (dot_nt(out_both, down_full) * slope.astype(F32)).astype(BF)
        return down_full, pre, dot_nn(pre[count:], up_full).astype(BF)

    def second_mine(pre, up_full):
        return dot_nn(pre[:count], up_full)

    def up_back(pre, normed_both):
        send = dot_tn(pre[:, width:], normed_both).astype(BF)
        keep = dot_tn(pre[:, :width], normed_both).astype(BF)
        return keep, send, jnp.sum(pre, axis=0, dtype=F32)

    def to_branch(down_one, down_two, out_both, slope, up_full, normed_both, middle):
        down_full, pre, theirs = to_pre(down_one, down_two, out_both, slope, up_full)
        came = peer(theirs)
        keep_up, send_up, up_bias = block(up_back, pre, normed_both)
        given = (second_mine(pre, up_full), came, middle, out_low, mask, middle_rows)
        shapes = (((count, D), F32), ((wide, D), BF), ((8, D), F32))
        outs = [jax.ShapeDtypeStruct(*shape) for shape in shapes]
        return down_full, keep_up, send_up, up_bias, *by_slots(second_norm_kernel, "second_norm", given, outs)

    down_full, keep_up, send_up, up_bias, grad_total, branch_pad, second_sums = rounds.go(
        [give_down], to_branch, *down_halves, out_both, slope, up_full, normed_both, middle
    )
    give_up = reduce_relative(lambda: keep_up, send_up, plane_last)

    def attention_back(branch_pad, attended):
        grad_proj = dot_nn(attended, branch_pad).astype(BF)
        proj_came = peer(cut_half(grad_proj, 1 - core))
        grad_att = dot_nt(proj_full, branch_pad).astype(BF).reshape(HEADS, HD, wide)
        grad_qkv, grad_rel = attend_back(qkv, grad_att, probs, rel_cols)
        grad_qkv = grad_qkv.reshape(3 * D, wide)
        grad_proj = (cut_half(grad_proj, core).astype(F32) + proj_came.astype(F32)).astype(BF)
        halves = [stout(cut_half(grad_qkv, which)) for which in (core, 1 - core)]
        return grad_qkv, grad_rel, *halves, grad_proj

    grad_qkv, grad_rel, qkv_grad_mine, qkv_grad_theirs, grad_proj = rounds.go(
        [give_up, give_down], attention_back, branch_pad, attended
    )
    give_proj = reduce_half(grad_proj, plane_last)
    normed_pad = jnp.concatenate([pad_mine, pad_peer], axis=0)

    def qkv_back(mine, came, normed_pad):
        both = jnp.concatenate([mine, came], axis=1)
        return both, dot_nn(both, normed_pad).astype(BF)

    def to_qkv_grad(mine, theirs, normed_pad):
        return qkv_back(mine, peer(theirs), normed_pad)

    qkv_grad_both, grad_qkv_half = rounds.go(
        [give_up, give_down, give_proj], to_qkv_grad, qkv_grad_mine, qkv_grad_theirs, normed_pad
    )
    give_qkv = reduce_half(grad_qkv_half, plane_last)

    def first_theirs(both, weight):
        return narrow_slots(dot_tn(both[:, wide:], weight).astype(BF))

    def first_mine(both, weight):
        return dot_tn(both[:, :wide], weight)

    def mlp_theirs(gelu_both, down_full):
        return dot_nn(gelu_both[count:], down_full).astype(BF)

    def mlp_mine(gelu_both, down_full, came, middle):
        mlp_out = dot_nn(gelu_both[:count], down_full) + came.astype(F32) + bias_down
        return ((middle + mlp_out) * mask).astype(BF).reshape(slots, ROWS, D)[:, :tokens]

    def to_small(grad_qkv, branch_pad, second_sums, out_low, up_bias, grad_rel):
        up_bias = relative(up_bias.reshape(chips, -1))
        up_bias = [jnp.where(core == 0, up_bias, 0.0), turned(jnp.where(core == 0, 0.0, up_bias))]
        up_bias = jnp.stack(up_bias, axis=1).reshape(chips // planes, planes, 2, -1)
        up_bias = jnp.swapaxes(up_bias, 1, 2).reshape(-1, D)
        qkv_bias = jnp.sum(grad_qkv, axis=1, dtype=F32).reshape(3, D)
        rows = [
            jnp.zeros((2, D), F32),
            qkv_bias[:1],
            qkv_bias[2:],
            jnp.sum(branch_pad, axis=0, dtype=F32, keepdims=True),
            second_sums[:2],
            jnp.sum(out_low, axis=0, dtype=F32, keepdims=True),
            up_bias,
        ]
        rows = jnp.concatenate(rows).reshape(-1, SIDE), grad_rel.reshape(-1, SIDE)
        return jnp.concatenate(rows)

    def for_peer(both, weight, gelu_both, down_full, *values):
        ours = block(first_theirs, both, weight), block(mlp_theirs, gelu_both, down_full)
        return *ours, to_small(*values)

    first_sent, mlp_sent, small_early = rounds.go(
        [give_qkv, give_up, give_down, give_proj],
        for_peer,
        qkv_grad_both,
        qkv_half,
        gelu_both,
        down_full,
        grad_qkv,
        branch_pad,
        second_sums,
        out_low,
        up_bias,
        grad_rel,
    )

    stride = max(planes // 4, 1)
    homes = {"qkv": 0, "down": stride, "up": 2 * stride, "proj": 3 * stride}
    me_z = lax.axis_index("gy")
    room = max(up_weight.shape[1], down_weight.shape[0], part, proj_weight.shape[0])
    pieces = [[] for _ in range(planes)]

    def home(**lows):
        parts = []
        for far in range(planes):
            value = sum(
                jnp.where((me_z ^ far) == homes[name], low, jnp.zeros_like(low)) for name, low in lows.items()
            )
            if far:
                value = lax.ppermute(value, "gy", [(homes[name] ^ far, homes[name]) for name in lows])
            parts.append(value)
        return parts

    def arrive(parts):
        for row, piece in zip(pieces, parts):
            row.append(jnp.pad(piece, ((0, room - piece.shape[0]), (0, 0))))

    def moment(old, grad, flip):
        new = MOMENT_MATRIX * old + (grad.T if flip else grad)
        return new, (new.T if flip else new).astype(BF)

    first_came, mlp_came = rounds.go(
        [give_qkv, give_up, give_proj], lambda one, two: (peer(one), peer(two)), first_sent, mlp_sent
    )
    new_down, low_down = moment(down_moment, give_down.out, False)
    new_up, low_up = moment(up_moment, give_up.out, True)

    def to_ends(low_down, low_up, both, weight, first_came, grad_total, short_low):
        arrived = home(down=low_down, up=low_up)
        given = (block(first_mine, both, weight), first_came, short_low, grad_total, mask, middle_rows)
        outs = [jax.ShapeDtypeStruct((slots, tokens, D), F32), jax.ShapeDtypeStruct((8, D), F32)]
        return arrived, *by_slots(first_norm_kernel, "first_norm", given, outs)

    arrived, grad_input, first_sums = rounds.go(
        [give_qkv, give_proj],
        to_ends,
        low_down,
        low_up,
        qkv_grad_both,
        qkv_half,
        first_came,
        grad_total,
        short_low,
    )
    arrive(arrived)
    new_proj, low_proj = moment(proj_moment, give_proj.out, False)

    arrive(rounds.go([give_qkv, give_proj], lambda value: home(proj=value), low_proj))
    while not give_qkv.done:
        rounds.go([give_qkv])
    new_qkv, low_qkv = moment(qkv_moment, give_qkv.out[:part], True)
    arrive(rounds.go([], lambda value: home(qkv=value), low_qkv))
    held = jnp.concatenate([sum(row[1:], row[0]) for row in pieces], axis=0)
    first_rows = jnp.pad(first_sums[:2].reshape(-1, SIDE), ((0, small_early.shape[0] - 2 * D // SIDE), (0, 0)))
    small = small_early + first_rows
    blocks = upper_blocks(dot_tn(held, held))
    fill = -small.shape[0] % (8 * devices // planes)
    summed, block_out = plane_sum(
        rounds,
        jnp.concatenate([blocks, jnp.pad(small, ((0, fill), (0, 0)))], axis=0),
        lambda *values: block(mlp_mine, *values),
        gelu_both,
        down_full,
        mlp_came,
        middle,
    )
    gram = summed[: blocks.shape[0]]
    add_small = sum_whole(summed[blocks.shape[0] : blocks.shape[0] + small.shape[0]], deep)

    def send_back(ortho):
        back = [ortho[0]]
        for far in range(1, planes):
            back.append(lax.ppermute(ortho[far], "gy", [(place, place ^ far) for place in range(planes)]))
        return jnp.stack(back)

    (ortho,) = rounds.go([add_small], lambda *pair: (chain(*pair),), gram, held)
    back = rounds.go([add_small], send_back, ortho.reshape(planes, room, D))
    while not add_small.done:
        rounds.go([add_small])
    small = add_small.out.reshape(-1)
    rel_total = small[devices * spare :].reshape(2, 32, HD)
    vec_total = lax.dynamic_slice_in_dim(small, lax.axis_index(EVERY) * spare, spare)

    def part_of(name, rows):
        return lax.dynamic_index_in_dim(back, me_z ^ homes[name], 0, False)[:rows].astype(F32)

    parts = [
        part_of("qkv", qkv_weight.shape[1]),
        part_of("proj", proj_weight.shape[0]),
        part_of("up", up_weight.shape[1]),
        part_of("down", down_weight.shape[0]),
    ]

    scales = (math.sqrt(3.0), 1.0, math.sqrt(max(1.0, FF / D)), math.sqrt(max(1.0, D / FF)))
    masters = (qkv_weight, proj_weight, up_weight, down_weight)
    flipped = (True, False, True, False)
    new_weights = [
        master - RATE_MATRIX * factor * (part.T if turn else part)
        for master, factor, part, turn in zip(masters, scales, parts, flipped)
    ]

    rate_vec = 0.5 / math.sqrt(float(devices * slots * tokens))
    vec_moment_new = MOMENT_VECTOR * vector_moment + vec_total
    rel_grad = rel_total[:, : 2 * WIN - 1][:, ::-1]
    rel_moment_new = MOMENT_VECTOR * rel_moment + rel_grad
    return (
        block_out,
        grad_input,
        new_qkv,
        new_proj,
        new_up,
        new_down,
        new_weights[0],
        new_weights[1],
        new_weights[2],
        new_weights[3],
        vec_moment_new,
        vectors - rate_vec * vec_moment_new,
        rel_moment_new,
        rel_pos - 0.2 * rate_vec * rel_moment_new,
    )


def solution(mesh):
    size_x, size_y = mesh.shape["gx"], mesh.shape["gy"]
    side = math.isqrt(size_x // 2)
    assert side * side * 2 == size_x
    grid = (side, size_x // 2 // side, 2, size_y)
    split = Mesh(mesh.devices.reshape(grid), ("ga", "gb", "gc", "gy"))
    flat = ("ga", "gb", "gc", "gy")
    slab, cols, rows, line = P(flat, None, None), P(None, flat), P(flat, None), P(flat)
    return jax.shard_map(
        body,
        mesh=split,
        in_specs=(
            (slab, slab, rows, line) + (cols, rows, cols, rows) * 2 + (line, line, P(), P())
        ),
        out_specs=(
            (slab, slab) + (cols, rows, cols, rows) * 2 + (line, line, P(), P())
        ),
        check_vma=False,
    )
```

```python
from functools import partial
import math

import jax
import jax.numpy as jnp
from jax import lax
from jax.experimental import pallas as pl
from jax.experimental.pallas import tpu as pltpu
from jax.sharding import Mesh, PartitionSpec as P

D = 1280
FF = 5120
HEADS = 16
HD = 80
WIN = 14
GRID = 64
ITERS = 5
LANES = 256
ROWS = 208

NORM_EPSILON = 1e-06
ORTHO_EPSILON = 1e-07
COEFF_LINEAR = 3.4445
COEFF_CUBIC = -4.775
COEFF_QUINTIC = 2.0315
MOMENT_MATRIX = 0.95
MOMENT_VECTOR = 0.9
RATE_MATRIX = 0.5

BF = jnp.bfloat16
F32 = jnp.float32


def dot_nn(left, right):
    return jnp.dot(left, right, preferred_element_type=F32)


def dot_tn(left, right):
    return lax.dot_general(left, right, (((0,), (0,)), ((), ())), preferred_element_type=F32)


def dot_nt(left, right):
    return lax.dot_general(left, right, (((1,), (1,)), ((), ())), preferred_element_type=F32)


def split_low(value):
    high = value.astype(BF)
    return high, (value - high.astype(F32)).astype(BF)


GROUP = 8


def spots():
    row = lax.broadcasted_iota(jnp.int32, (32, LANES), 0)
    lane = lax.broadcasted_iota(jnp.int32, (32, LANES), 1)
    along = jnp.where(row < 16, lane // WIN, lane % WIN + 16)
    return jnp.where((along == row) & (lane < WIN * WIN), 1.0, 0.0).astype(BF)


def shifts():
    lane = lax.broadcasted_iota(jnp.int32, (32, LANES), 1)
    down_h = jnp.maximum(WIN - 1 - lane // WIN, 0)
    return down_h, WIN - 1 - lane % WIN


def barrel(value, amount, up):
    for bit in (1, 2, 4, 8):
        moved = pltpu.roll(value, 32 - bit if up else bit, 0)
        value = jnp.where((amount & bit) != 0, moved, value)
    return value


def attend_kernel(q_ref, k_ref, v_ref, rel_ref, out_ref, probs_ref):
    marks = spots()
    marks2 = jnp.concatenate([marks, marks], axis=0)
    shift_h, shift_w = shifts()
    tail_row = lax.broadcasted_iota(jnp.int32, (16, LANES), 0) + (ROWS - 16)
    pad = jnp.zeros((LANES - ROWS, LANES), BF)
    scale = HD ** (-0.5) / math.log(2.0)
    for head in range(GROUP):
        query = q_ref[0, head]
        rel_q = dot_nn(rel_ref[...], query) * (HD**0.5)
        along_h = barrel(rel_q[:32], shift_h, True)[:16]
        along_w = barrel(rel_q[32:], shift_w, True)[:16]
        high, rest = split_low(jnp.concatenate([along_h, along_w], axis=0))
        query_all = jnp.concatenate([query, high, rest], axis=0)
        key_all = jnp.concatenate([k_ref[0, head], marks2], axis=0)
        scores = dot_tn(key_all, query_all)[:ROWS]
        tail = jnp.where(tail_row < WIN * WIN, scores[ROWS - 16 :], -1e30)
        scores = jnp.concatenate([scores[: ROWS - 16], tail], axis=0)
        peak = jnp.max(scores, axis=0, keepdims=True)
        exponent = jnp.exp2((scores - peak) * scale)
        probs = (exponent * (1.0 / jnp.sum(exponent, axis=0, keepdims=True))).astype(BF)
        probs_ref[0, head] = probs
        out_ref[head] = dot_nn(v_ref[0, head], jnp.concatenate([probs, pad], axis=0)).astype(BF)


def attend(qkv, rel_rows):
    slots = qkv.shape[-1] // LANES
    cut = lambda part: pl.BlockSpec((1, GROUP, HD, LANES), lambda s, g, part=part: (part, g, 0, s))
    return pl.pallas_call(
        attend_kernel,
        grid=(slots, HEADS // GROUP),
        in_specs=[cut(0), cut(1), cut(2), pl.BlockSpec((64, HD), lambda s, g: (0, 0))],
        out_specs=[
            pl.BlockSpec((GROUP, HD, LANES), lambda s, g: (g, 0, s)),
            pl.BlockSpec((1, GROUP, ROWS, LANES), lambda s, g: (s, g, 0, 0)),
        ],
        out_shape=[
            jax.ShapeDtypeStruct((HEADS, HD, slots * LANES), BF),
            jax.ShapeDtypeStruct((slots, HEADS, ROWS, LANES), BF),
        ],
        compiler_params=pltpu.CompilerParams(vmem_limit_bytes=16 * 2**20),
        cost_estimate=cheap(slots * HEADS * 2 * LANES * LANES * 256),
        name="attend",
    )(qkv, qkv, qkv, rel_rows)


def attend_back_kernel(q_ref, k_ref, v_ref, g_ref, probs_ref, rel_ref, out_ref, drel_ref):
    marks = spots()
    shift_h, shift_w = shifts()
    pad = jnp.zeros((LANES - ROWS, LANES), BF)
    none = jnp.zeros((16, LANES), F32)
    scale = HD ** (-0.5)
    total = jnp.zeros((64, HD), F32)
    for head in range(GROUP):
        query = q_ref[0, head]
        grad = g_ref[head]
        probs_low = probs_ref[0, head]
        probs = probs_low.astype(F32)
        weighted = dot_tn(v_ref[0, head], grad)[:ROWS] * probs
        flow = jnp.sum(weighted, axis=0, keepdims=True)
        score_low = jnp.concatenate([(weighted - probs * flow).astype(BF), pad], axis=0)
        out_ref[2, head] = dot_nt(grad, jnp.concatenate([probs_low, pad], axis=0)).astype(BF)
        out_ref[1, head] = (dot_nt(query, score_low) * scale).astype(BF)
        mixed = dot_nn(jnp.concatenate([k_ref[0, head], marks], axis=0), score_low)
        rows_h = barrel(jnp.concatenate([mixed[HD : HD + 16], none], axis=0), shift_h, False)
        rows_w = barrel(jnp.concatenate([mixed[HD + 16 :], none], axis=0), shift_w, False)
        both = jnp.concatenate(split_low(jnp.concatenate([rows_h, rows_w], axis=0)), axis=0)
        out_ref[0, head] = (mixed[:HD] * scale + dot_nn(rel_ref[...], both)).astype(BF)
        parts = dot_nt(both, query)
        total = total + parts[:64] + parts[64:]

    @pl.when((pl.program_id(0) == 0) & (pl.program_id(1) == 0))
    def _():
        drel_ref[...] = jnp.zeros_like(drel_ref)

    drel_ref[...] += total


def attend_back(qkv, grad, probs, rel_cols):
    slots = qkv.shape[-1] // LANES
    cut = lambda part: pl.BlockSpec((1, GROUP, HD, LANES), lambda s, g, part=part: (part, g, 0, s))
    return pl.pallas_call(
        attend_back_kernel,
        grid=(slots, HEADS // GROUP),
        in_specs=[
            cut(0),
            cut(1),
            cut(2),
            pl.BlockSpec((GROUP, HD, LANES), lambda s, g: (g, 0, s)),
            pl.BlockSpec((1, GROUP, ROWS, LANES), lambda s, g: (s, g, 0, 0)),
            pl.BlockSpec((HD, 128), lambda s, g: (0, 0)),
        ],
        out_specs=[
            pl.BlockSpec((3, GROUP, HD, LANES), lambda s, g: (0, g, 0, s)),
            pl.BlockSpec((64, HD), lambda s, g: (0, 0)),
        ],
        out_shape=[
            jax.ShapeDtypeStruct((3, HEADS, HD, slots * LANES), BF),
            jax.ShapeDtypeStruct((64, HD), F32),
        ],
        compiler_params=pltpu.CompilerParams(vmem_limit_bytes=20 * 2**20),
        cost_estimate=cheap(slots * HEADS * 5 * LANES * LANES * 256),
        name="attend_back",
    )(qkv, qkv, qkv, grad, probs, rel_cols)


def resident(shape):
    return pl.BlockSpec(shape, lambda *_: (0,) * len(shape))


def cheap(flops):
    return pl.CostEstimate(flops=flops // 8, bytes_accessed=1_000_000, transcendentals=0)


def settings(mebibytes):
    return pltpu.CompilerParams(vmem_limit_bytes=mebibytes * 2**20)


def middle_kernel(att_ref, proj_ref, short_ref, mask_ref, rows_ref, middle_ref, normed_ref):
    branch = dot_tn(att_ref[...], proj_ref[...])[:ROWS] + rows_ref[0:1]
    middle = (short_ref[...].astype(F32) + branch) * mask_ref[...]
    middle_ref[...] = middle
    centred = middle - jnp.mean(middle, axis=1, keepdims=True)
    inverse = lax.rsqrt(jnp.mean(centred * centred, axis=1, keepdims=True) + NORM_EPSILON)
    normed_ref[...] = (centred * inverse * rows_ref[1:2] + rows_ref[2:3]).astype(BF)


def to_middle(attended, proj_full, short, mask, rows):
    slots = attended.shape[1] // LANES
    by_slot = lambda width: pl.BlockSpec((ROWS, width), lambda s: (s, 0))
    return pl.pallas_call(
        middle_kernel,
        grid=(slots,),
        in_specs=[
            pl.BlockSpec((D, LANES), lambda s: (0, s)),
            resident((D, D)),
            by_slot(D),
            by_slot(1),
            resident((8, D)),
        ],
        out_specs=[by_slot(D), by_slot(D)],
        out_shape=[
            jax.ShapeDtypeStruct((slots * ROWS, D), F32),
            jax.ShapeDtypeStruct((slots * ROWS, D), BF),
        ],
        compiler_params=settings(24),
        cost_estimate=cheap(2 * slots * LANES * D * D),
        name="middle",
    )(attended, proj_full, short, mask, rows)


def norm_parts(grad, value, gain):
    centred = value - jnp.mean(value, axis=1, keepdims=True)
    inverse = lax.rsqrt(jnp.mean(centred * centred, axis=1, keepdims=True) + NORM_EPSILON)
    hat = centred * inverse
    scaled = grad * gain
    mean_one = jnp.mean(scaled, axis=1, keepdims=True)
    mean_two = jnp.mean(scaled * hat, axis=1, keepdims=True)
    sums = [jnp.sum(grad * hat, axis=0, keepdims=True), jnp.sum(grad, axis=0, keepdims=True)]
    sums = jnp.concatenate(sums + [jnp.zeros((6, D), F32)], axis=0)
    return inverse * (scaled - mean_one - hat * mean_two), sums


def add_sums(sums_ref, sums):
    @pl.when(pl.program_id(0) == 0)
    def _():
        sums_ref[...] = jnp.zeros_like(sums_ref)

    sums_ref[...] += sums


def second_norm_kernel(grad_ref, came_ref, middle_ref, out_ref, mask_ref, rows_ref, total_ref, pad_ref, sums_ref):
    grad = grad_ref[...] + came_ref[...].astype(F32)
    back, sums = norm_parts(grad, middle_ref[...], rows_ref[1:2])
    total = (out_ref[...].astype(F32) + back) * mask_ref[...]
    total_ref[...] = total
    low = total.astype(BF)
    pad_ref[...] = jnp.concatenate([low, jnp.zeros((LANES - ROWS, D), BF)], axis=0)
    add_sums(sums_ref, sums)


def first_norm_kernel(grad_ref, came_ref, short_ref, total_ref, mask_ref, rows_ref, out_ref, sums_ref):
    mask = mask_ref[...]
    grad = (grad_ref[:ROWS] + came_ref[...].astype(F32)) * mask
    back, sums = norm_parts(grad, short_ref[...].astype(F32), rows_ref[3:4])
    out_ref[0] = ((total_ref[...] + back) * mask)[: WIN * WIN]
    add_sums(sums_ref, sums)


def by_slots(kernel, name, given, outs):
    slots = given[1].shape[0] // ROWS

    def spec(shape):
        if len(shape) == 3:
            return pl.BlockSpec((1,) + shape[1:], lambda s: (s, 0, 0))
        if shape[0] == 8:
            return resident(shape)
        return pl.BlockSpec((shape[0] // slots, shape[1]), lambda s: (s, 0))

    return pl.pallas_call(
        kernel,
        grid=(slots,),
        in_specs=[spec(item.shape) for item in given],
        out_specs=[spec(item.shape) for item in outs],
        out_shape=list(outs),
        compiler_params=settings(32),
        cost_estimate=cheap(1_000_000),
        name=name,
    )(*given)


SIDE = 256
SPOTS = [(row, column) for row in range(D // SIDE) for column in range(row, D // SIDE)]


def upper_blocks(gram):
    parts = [
        gram[row * SIDE : (row + 1) * SIDE, column * SIDE : (column + 1) * SIDE] for row, column in SPOTS
    ]
    return jnp.concatenate(parts, axis=0)


def chain_kernel(gram_ref, y_ref, out_ref, high_ref, rest_ref, b_ref, t_high, t_rest, z_high, z_rest):
    columns = [slice(start, start + SIDE) for start in range(0, D, SIDE)]
    row = lax.broadcasted_iota(jnp.int32, (SIDE, SIDE), 0)
    spot = row == lax.broadcasted_iota(jnp.int32, (SIDE, SIDE), 1)
    trace = jnp.zeros((), F32)
    for place, (row, column) in enumerate(SPOTS):
        if row == column:
            trace = trace + jnp.sum(jnp.where(spot, gram_ref[place * SIDE : (place + 1) * SIDE, :], 0.0))
    inverse = 1.0 / (jnp.sqrt(trace) + ORTHO_EPSILON)
    for place, (row, column) in enumerate(SPOTS):
        block = gram_ref[place * SIDE : (place + 1) * SIDE, :] * inverse * inverse
        for part, over, down in ((block, row, column), (block.T, column, row)):
            high, rest = split_low(part)
            high_ref[columns[over], columns[down]] = high
            rest_ref[columns[over], columns[down]] = rest
    z_high[0] = y_ref[...]

    def mirror(ref, values, place):
        cut = columns[place]
        ref[: (place + 1) * SIDE, cut] = values
        for over in range(place):
            ref[cut, columns[over]] = values[columns[over], :].T

    def polynomial():
        for place, cut in enumerate(columns):
            rows = slice(0, (place + 1) * SIDE)
            square = dot_nn(high_ref[rows, :], high_ref[:, cut])
            value = high_ref[rows, cut].astype(F32) + rest_ref[rows, cut].astype(F32)
            poly = COEFF_CUBIC * value + COEFF_QUINTIC * square
            line = lax.broadcasted_iota(jnp.int32, poly.shape, 0) - place * SIDE
            eye = line == lax.broadcasted_iota(jnp.int32, poly.shape, 1)
            mirror(b_ref, (poly + jnp.where(eye, COEFF_LINEAR, 0.0)).astype(BF), place)

    def follow(now, cut, fine):
        value = dot_nn(z_high[now], b_ref[:, cut])
        return value + dot_nn(z_rest[now], b_ref[:, cut]) if fine else value

    def advance(now, fine, z_fine, z_more):
        later = 1 - now
        polynomial()
        for cut in columns:
            value = dot_nn(b_ref[...], high_ref[:, cut])
            if fine:
                value = value + dot_nn(b_ref[...], rest_ref[:, cut])
            t_high[:, cut], rest = split_low(value)
            if fine:
                t_rest[:, cut] = rest
            z_high[later, :, cut], rest = split_low(follow(now, cut, z_fine))
            if z_more:
                z_rest[later, :, cut] = rest
        for place, cut in enumerate(columns):
            rows = slice(0, (place + 1) * SIDE)
            value = dot_nn(t_high[rows, :], b_ref[:, cut])
            if fine:
                value = value + dot_nn(t_rest[rows, :], b_ref[:, cut])
            high, rest = split_low(value)
            mirror(high_ref, high, place)
            mirror(rest_ref, rest, place)

    advance(0, True, False, True)

    @pl.loop(1, ITERS - 2)
    def _(step):
        advance(step % 2, True, True, True)

    advance((ITERS - 2) % 2, False, False, False)
    polynomial()
    for cut in columns:
        out_ref[:, cut] = (follow((ITERS - 1) % 2, cut, False) * inverse).astype(BF)


def chain(gram, rows):
    half = pltpu.VMEM((D, D), BF)
    flow = pltpu.VMEM((2,) + rows.shape, BF)
    whole = pl.BlockSpec(memory_space=pltpu.VMEM)
    return pl.pallas_call(
        chain_kernel,
        in_specs=[whole, whole],
        out_specs=whole,
        out_shape=jax.ShapeDtypeStruct(rows.shape, BF),
        scratch_shapes=[half] * 5 + [flow] * 2,
        compiler_params=settings(56),
        cost_estimate=pl.CostEstimate(flops=18 * 2 * D**3, bytes_accessed=6 * D * D, transcendentals=0),
        name="chain",
    )(gram, rows)


EVERY = ("ga", "gb", "gc", "gy")


def peer(value):
    return lax.ppermute(value, "gc", [(0, 1), (1, 0)])


def steps_of(axis):
    return lax.axis_size(axis).bit_length() - 1


def first_stages():
    return [("f", step) for step in reversed(range(steps_of("ga")))]


def second_stages():
    return [("s", step) for step in reversed(range(steps_of("gb")))]


def plane_stages():
    return [("z", step) for step in range(steps_of("gy"))]


def gather_groups():
    deep = plane_stages()
    return [deep[1:][::-1], deep[:1]], [second_stages()[::-1]], [first_stages()[::-1]]


def reduce_groups():
    deep = plane_stages()
    return [first_stages()], [second_stages()], [deep[:1], deep[1:]]


def half_stages():
    return first_stages() + second_stages() + plane_stages()


def bit_of(stage, core):
    kind, step = stage
    if kind == "z":
        return "gy", steps_of("gy") - 1 - step if core == 0 else step
    return ("ga" if (kind == "f") == (core == 0) else "gb"), step


def my_bit(stage):
    values = []
    for core in range(2):
        axis, step = bit_of(stage, core)
        values.append((lax.axis_index(axis) >> step) & 1)
    return jnp.where(lax.axis_index("gc") == 0, values[0], values[1])


def swap(value, stage):
    if stage == "c":
        return peer(value)
    sizes = [lax.axis_size(axis) for axis in EVERY]
    pairs = []
    for place in range(math.prod(sizes)):
        spot, rest = [], place
        for size in reversed(sizes):
            spot.insert(0, rest % size)
            rest //= size
        axis, step = bit_of(stage, spot[2])
        spot[EVERY.index(axis)] ^= 1 << step
        other = 0
        for size, at in zip(sizes, spot):
            other = other * size + at
        pairs.append((place, other))
    return lax.ppermute(value, EVERY, pairs)


class Rounds:
    def __init__(self):
        self.last = None

    def go(self, chains, work=None, *values):
        chains = [chain for chain in chains if not chain.done]
        while long := [chain for chain in chains if chain.left > 1]:
            self.once(long)
        out = self.once(chains, work, *values)
        for chain in chains:
            chain.left = chain.counts.pop(0) if chain.counts else 0
        return out

    def once(self, chains, work=None, *values):
        [chain.look() for chain in chains]
        marks = [] if self.last is None else [self.last]
        held = [lax.optimization_barrier((chain.value, *marks))[0] for chain in chains]
        came = [swap(value, chain.stage) for value, chain in zip(held, chains)]
        ready = lax.optimization_barrier((*values, *held, *marks))
        out = () if work is None else work(*ready[: len(values)])
        leaves, tree = jax.tree.flatten(out)
        ended = lax.optimization_barrier(tuple(came) + tuple(leaves))
        self.last = ended[0]
        for chain, value in zip(chains, ended):
            chain.take(value)
            chain.left -= 1
        return jax.tree.unflatten(tree, ended[len(chains) :])


class Chain:
    def __init__(self, work, groups):
        self.work, self.ended, self.result = work, False, None
        self.pending = [None]
        self.counts = [len(group) for group in groups if group]
        self.left = self.counts.pop(0)

    def take(self, came):
        self.pending = [came]

    def look(self):
        if self.pending:
            try:
                self.value, self.stage = self.work.send(self.pending.pop())
            except StopIteration as stop:
                self.ended, self.result = True, stop.value

    @property
    def done(self):
        self.look()
        return self.ended

    @property
    def out(self):
        self.look()
        return self.result


def gather_half(shard):
    groups = sum(gather_groups(), [])

    def work():
        held = shard[None]
        for stage in sum(groups, []):
            came = yield held, stage
            first = my_bit(stage) == 0
            held = jnp.concatenate([jnp.where(first, held, came), jnp.where(first, came, held)], axis=0)
        return held.reshape(-1, shard.shape[-1])

    return Chain(work(), groups)


def gather_relative(shard, groups):
    def work():
        order, canon = sum(groups, []), half_stages()
        held = shard
        for stage in order[:-1]:
            came = yield held, stage
            held = jnp.stack([held, came])
        came = yield held, order[-1]
        there = order[-2::-1]
        turn = [there.index(stage) for stage in canon[1:]] + [len(there), len(there) + 1]
        return tuple(half.transpose(turn).reshape(-1, shard.shape[-1]) for half in (held, came))

    return Chain(work(), groups)


def relative(value):
    stages = half_stages()
    place = sum(my_bit(stage) << (len(stages) - 1 - at) for at, stage in enumerate(stages))
    spots = jnp.arange(value.shape[0])
    picker = ((spots[:, None] ^ place) == spots[None, :]).astype(F32)
    return jnp.dot(picker, value, precision=lax.Precision.HIGHEST, preferred_element_type=F32)


def reduce_half(grad, groups, kind=BF):
    def work():
        live = half_stages()
        parts = [grad.reshape((2,) * len(live) + (-1, grad.shape[-1]))]
        for stage in sum(groups, []):
            place, mine = live.index(stage), my_bit(stage)
            live.remove(stage)

            def pick(which):
                cuts = [lax.dynamic_index_in_dim(part, which, place, False) for part in parts]
                return cuts[0] if len(cuts) == 1 else (cuts[0].astype(F32) + cuts[1].astype(F32)).astype(kind)

            send = pick(1 - mine)
            parts = list(lax.optimization_barrier((*parts, send))[:-1])
            keep = pick(mine)
            came = yield send, stage
            parts = [keep, came]
        return parts[0].astype(F32) + parts[1].astype(F32)

    return Chain(work(), groups)


def reduce_relative(keep, send, groups):
    def work():
        live, order = half_stages(), sum(groups, [])
        came = yield send, order[0]
        assert order[0] == live[0]
        live.remove(order[0])
        shape = (2,) * len(live) + (-1, send.shape[-1])
        parts = [keep().reshape(shape), came.reshape(shape)]
        for stage in order[1:]:
            place = live.index(stage)
            live.remove(stage)

            def pick(which):
                cuts = [lax.index_in_dim(part, which, place, False).astype(F32) for part in parts]
                return (cuts[0] + cuts[1]).astype(BF)

            away = pick(1)
            parts = list(lax.optimization_barrier((*parts, away))[:-1])
            kept = pick(0)
            came = yield away, stage
            parts = [kept, came]
        return parts[0].astype(F32) + parts[1].astype(F32)

    return Chain(work(), groups)


def turned(value):
    stages = half_stages()
    shape = value.shape
    value = value.reshape((2,) * len(stages) + shape[1:])
    side, deep = len(first_stages()), len(plane_stages())
    order = list(range(side, 2 * side)) + list(range(side)) + list(reversed(range(2 * side, 2 * side + deep)))
    order += list(range(2 * side + deep, value.ndim))
    return value.transpose(order).reshape(shape)


def join_halves(mine, theirs):
    chips = 1 << len(half_stages())
    planes = lax.axis_size("gy")
    first = lax.axis_index("gc") == 0
    shape = (chips, -1) + mine.shape[1:]
    mine, theirs = mine.reshape(shape), theirs.reshape(shape)
    both = [jnp.where(first, mine, theirs), turned(jnp.where(first, theirs, mine))]
    both = [half.reshape((chips // planes, planes) + half.shape[1:]) for half in both]
    return jnp.stack(both, axis=1).reshape((-1,) + mine.shape[2:])


def cut_half(value, which):
    chips = 1 << len(half_stages())
    planes = lax.axis_size("gy")
    shape = value.shape
    value = value.reshape((chips // planes, 2, planes, -1) + shape[1:])
    halves = [value[:, core].reshape((chips, -1) + shape[1:]) for core in range(2)]
    return jnp.where(which == 0, halves[0], turned(halves[1])).reshape((-1,) + shape[1:])


def sum_rows(value, stages):
    def work():
        held = value
        for stage in stages:
            halves = held.reshape((2, held.shape[0] // 2) + held.shape[1:])
            mine = my_bit(stage)
            keep = lax.dynamic_index_in_dim(halves, mine, 0, False)
            came = yield lax.dynamic_index_in_dim(halves, 1 - mine, 0, False), stage
            held = keep + came
        return held

    return Chain(work(), [[stage] for stage in stages])


def spread_rows(value, stages):
    def work():
        held = value
        for stage in stages:
            came = yield held, stage
            first = my_bit(stage) == 0
            held = jnp.concatenate([jnp.where(first, held, came), jnp.where(first, came, held)], axis=0)
        return held

    return Chain(work(), [[stage] for stage in stages])


def plane_sum(rounds, value, work, *values):
    core = lax.axis_index("gc")
    halves = value.reshape((2, value.shape[0] // 2) + value.shape[1:])

    def over_cores(mine, theirs):
        return mine + peer(theirs)

    held = rounds.go(
        [],
        over_cores,
        lax.dynamic_index_in_dim(halves, core, 0, False),
        lax.dynamic_index_in_dim(halves, 1 - core, 0, False),
    )
    stages = first_stages() + second_stages()
    chain = sum_rows(held, stages)
    out = rounds.go([chain], work, *values)
    while not chain.done:
        rounds.go([chain])
    chain = spread_rows(chain.out, stages[::-1])
    while not chain.done:
        rounds.go([chain])
    held = chain.out
    came = rounds.go([], peer, held)
    held = [jnp.where(core == 0, held, came), jnp.where(core == 0, came, held)]
    return jnp.concatenate(held, axis=0), out


def sum_whole(value, stages):
    def work():
        held = value
        for stage in stages:
            came = yield held, stage
            held = held + came
        return held

    return Chain(work(), [[stage] for stage in stages])


def token_mask(placement, counts):
    slot_count = placement.shape[0]
    live = (jnp.arange(slot_count, dtype=jnp.int32) < counts[0]).astype(F32)
    inner = jnp.arange(WIN * WIN, dtype=jnp.int32)
    row_pos = placement[:, 0:1] * WIN + inner[None, :] // WIN
    col_pos = placement[:, 1:2] * WIN + inner[None, :] % WIN
    inside = ((row_pos < GRID) & (col_pos < GRID)).astype(F32)
    return inside * live[:, None]


def normalised(value):
    centred = value - jnp.mean(value, axis=-1, keepdims=True)
    inverse = lax.rsqrt(jnp.mean(centred * centred, axis=-1, keepdims=True) + NORM_EPSILON)
    return centred * inverse, inverse


def norm_back(grad, hat, inverse, gain):
    scaled = grad * gain
    mean_one = jnp.mean(scaled, axis=-1, keepdims=True)
    mean_two = jnp.mean(scaled * hat, axis=-1, keepdims=True)
    return inverse * (scaled - mean_one - hat * mean_two)


def pad_slots(value, rows):
    slots, given, width = value.shape
    return jnp.pad(value, ((0, 0), (0, rows - given), (0, 0))).reshape(slots * rows, width)


def widen_slots(value):
    return pad_slots(value.reshape(-1, ROWS, value.shape[1]), LANES)


def narrow_slots(value):
    return value.reshape(-1, LANES, value.shape[1])[:, :ROWS].reshape(-1, value.shape[1])


def body(
    windows,
    cotangent,
    placement,
    counts,
    qkv_weight,
    proj_weight,
    up_weight,
    down_weight,
    qkv_moment,
    proj_moment,
    up_moment,
    down_moment,
    vectors,
    vector_moment,
    rel_pos,
    rel_moment,
):
    core = lax.axis_index("gc")
    planes = lax.axis_size("gy")
    chips = 1 << len(half_stages())
    devices = 2 * chips
    slots, tokens, _ = windows.shape
    wide = slots * LANES
    first, second, deep = first_stages(), second_stages(), plane_stages()
    rounds = Rounds()

    def block(work, *values):
        shapes = jax.eval_shape(work, *values)

        def idle(*_):
            return jax.tree.map(lambda item: jnp.zeros(item.shape, item.dtype), shapes)

        return lax.cond(counts[0] > 0, work, idle, *values)

    mask = pad_slots(token_mask(placement, counts)[:, :, None], ROWS)
    short_low = pad_slots(windows, ROWS) * mask.astype(BF)
    out_low = pad_slots(cotangent, ROWS) * mask.astype(BF)
    count = short_low.shape[0]
    by_z, by_second, by_first = gather_groups()
    part, spare = qkv_weight.shape[1], vectors.shape[0]
    vec_rows = jnp.pad(vectors.astype(BF)[None], ((0, 7), (0, D - spare)))
    take_qkv = gather_half(jnp.concatenate([qkv_weight.astype(BF).T, vec_rows], axis=0))
    take_proj = gather_half(proj_weight.astype(BF))
    take_up = gather_relative(up_weight.astype(BF).T, by_z + by_second + by_first)
    take_down = gather_relative(down_weight.astype(BF), by_second + by_z + by_first)

    mask_row = jnp.pad(mask.astype(BF).T, ((0, 7), (0, D - count)))
    rounds.go([take_qkv, take_down])
    short_peer = rounds.go([take_qkv, take_proj], peer, jnp.concatenate([short_low, mask_row], axis=0))
    rounds.go([take_qkv, take_up, take_proj])

    def first_hats(mine, theirs):
        return normalised(mine.astype(F32))[0], normalised(theirs[:count].astype(F32))[0]

    (hat_mine, hat_peer), out_peer = rounds.go(
        [take_qkv, take_up, take_proj],
        lambda one, two, three: (block(first_hats, one, two), peer(three)),
        short_low,
        short_peer,
        out_low,
    )
    qkv_half = take_qkv.out
    wide_part = part + 8

    def slim(value):
        return value.reshape((chips, wide_part) + value.shape[1:])[:, :part].reshape((-1,) + value.shape[1:])

    def stout(value):
        value = value.reshape((chips, part) + value.shape[1:])
        return jnp.pad(value, ((0, 0), (0, 8)) + ((0, 0),) * (value.ndim - 2)).reshape((-1,) + value.shape[2:])

    def both_qkv(qkv_half, hat_mine, hat_peer, short_peer, mask):
        vec_half = qkv_half.reshape(chips, wide_part, D)[:, part, :spare]
        vec = join_halves(vec_half, peer(vec_half)).reshape(-1).astype(F32)
        bias_qkv = jnp.concatenate([vec[2 * D : 3 * D], jnp.zeros((D,), F32), vec[3 * D : 4 * D]])
        bias_qkv = stout(cut_half(bias_qkv, core))[:, None]
        live = short_peer[count, :count].astype(F32)[:, None]
        pad_peer = widen_slots(((hat_peer * vec[:D] + vec[D : 2 * D]) * live).astype(BF))
        theirs = (dot_nt(qkv_half, pad_peer) + bias_qkv).astype(BF)
        came = peer(theirs)
        pad_mine = widen_slots(((hat_mine * vec[:D] + vec[D : 2 * D]) * mask).astype(BF))
        mine = (dot_nt(qkv_half, pad_mine) + bias_qkv).astype(BF)
        return mine, came, vec, pad_mine, pad_peer

    qkv_mine, qkv_came, vec, pad_mine, pad_peer = rounds.go(
        [take_up, take_proj, take_down], both_qkv, qkv_half, hat_mine, hat_peer, short_peer, mask
    )
    proj_half = take_proj.out
    bias_down = vec[7 * D : 8 * D]
    rel_low = rel_pos.astype(BF)[:, ::-1]
    rel_rows = jnp.pad(rel_low, ((0, 0), (0, 5), (0, 0))).reshape(64, HD)
    rel_cols = jnp.concatenate([rel_rows, rel_rows], axis=0).T

    def to_attended(mine, came, proj_half, out_low, out_peer, vec):
        proj_came = peer(proj_half)
        qkv = join_halves(slim(mine), slim(came)).reshape(3, HEADS, HD, wide)
        attended, probs = attend(qkv, rel_rows)
        out_both = jnp.concatenate([out_low, out_peer], axis=0)
        bias_up = relative(cut_half(vec[8 * D :], core).reshape(chips, -1)).reshape(1, -1)
        table = vec[: 8 * D].reshape(8, D)
        middle_rows = jnp.concatenate([table[4:7], table[:1], table[:4]], axis=0)
        return join_halves(proj_half, proj_came), out_both, qkv, attended, probs, bias_up, middle_rows

    proj_full, out_both, qkv, attended, probs, bias_up, middle_rows = rounds.go(
        [take_up, take_down], to_attended, qkv_mine, qkv_came, proj_half, out_low, out_peer, vec
    )
    attended = attended.reshape(D, wide)
    up_halves = take_up.out
    width = up_halves[0].shape[0]

    def to_gelu(mine, came, up_full, out_both):
        both = jnp.concatenate([mine, came], axis=0)
        pre = dot_nt(both, up_full) + bias_up
        bell = jnp.exp(-0.5 * pre * pre)
        below = 0.5 * (1.0 + lax.erf(pre * (0.5**0.5)))
        gelu = (pre * below).astype(BF)
        slope = (below + pre * bell * (2.0 * math.pi) ** -0.5).astype(BF)
        send = dot_tn(gelu[:, width:], out_both).astype(BF)
        return both, gelu, slope, dot_tn(gelu[:, :width], out_both).astype(BF), send

    def to_hidden(attended, up_one, up_two):
        middle, normed = to_middle(attended, proj_full, short_low, mask, middle_rows)
        came = peer(normed)
        up_full = jnp.concatenate([up_one, up_two], axis=0)
        return middle, up_full, *to_gelu(normed, came, up_full, out_both)

    middle, up_full, normed_both, gelu_both, slope, keep_down, send_down = rounds.go(
        [take_down], to_hidden, attended, *up_halves
    )
    down_halves = take_down.out

    by_first, by_second, by_z = reduce_groups()
    mixed_order = by_first + by_z + by_second
    plane_last = by_first + by_second + by_z
    give_down = reduce_relative(lambda: keep_down, send_down, mixed_order)

    def to_pre(down_one, down_two, out_both, slope, up_full):
        down_full = jnp.concatenate([down_one, down_two], axis=0)
        pre = (dot_nt(out_both, down_full) * slope.astype(F32)).astype(BF)
        return down_full, pre, dot_nn(pre[count:], up_full).astype(BF)

    def second_mine(pre, up_full):
        return dot_nn(pre[:count], up_full)

    def up_back(pre, normed_both):
        send = dot_tn(pre[:, width:], normed_both).astype(BF)
        keep = dot_tn(pre[:, :width], normed_both).astype(BF)
        return keep, send, jnp.sum(pre, axis=0, dtype=F32)

    def to_branch(down_one, down_two, out_both, slope, up_full, normed_both, middle):
        down_full, pre, theirs = to_pre(down_one, down_two, out_both, slope, up_full)
        came = peer(theirs)
        keep_up, send_up, up_bias = block(up_back, pre, normed_both)
        given = (second_mine(pre, up_full), came, middle, out_low, mask, middle_rows)
        shapes = (((count, D), F32), ((wide, D), BF), ((8, D), F32))
        outs = [jax.ShapeDtypeStruct(*shape) for shape in shapes]
        return down_full, keep_up, send_up, up_bias, *by_slots(second_norm_kernel, "second_norm", given, outs)

    down_full, keep_up, send_up, up_bias, grad_total, branch_pad, second_sums = rounds.go(
        [give_down], to_branch, *down_halves, out_both, slope, up_full, normed_both, middle
    )
    give_up = reduce_relative(lambda: keep_up, send_up, plane_last)

    def attention_back(branch_pad, attended):
        grad_proj = dot_nn(attended, branch_pad).astype(BF)
        proj_came = peer(cut_half(grad_proj, 1 - core))
        grad_att = dot_nt(proj_full, branch_pad).astype(BF).reshape(HEADS, HD, wide)
        grad_qkv, grad_rel = attend_back(qkv, grad_att, probs, rel_cols)
        grad_qkv = grad_qkv.reshape(3 * D, wide)
        grad_proj = (cut_half(grad_proj, core).astype(F32) + proj_came.astype(F32)).astype(BF)
        halves = [stout(cut_half(grad_qkv, which)) for which in (core, 1 - core)]
        return grad_qkv, grad_rel, *halves, grad_proj

    grad_qkv, grad_rel, qkv_grad_mine, qkv_grad_theirs, grad_proj = rounds.go(
        [give_up, give_down], attention_back, branch_pad, attended
    )
    give_proj = reduce_half(grad_proj, plane_last)
    normed_pad = jnp.concatenate([pad_mine, pad_peer], axis=0)

    def qkv_back(mine, came, normed_pad):
        both = jnp.concatenate([mine, came], axis=1)
        return both, dot_nn(both, normed_pad).astype(BF)

    def to_qkv_grad(mine, theirs, normed_pad):
        return qkv_back(mine, peer(theirs), normed_pad)

    qkv_grad_both, grad_qkv_half = rounds.go(
        [give_up, give_down, give_proj], to_qkv_grad, qkv_grad_mine, qkv_grad_theirs, normed_pad
    )
    give_qkv = reduce_half(grad_qkv_half, plane_last)

    def first_theirs(both, weight):
        return narrow_slots(dot_tn(both[:, wide:], weight).astype(BF))

    def first_mine(both, weight):
        return dot_tn(both[:, :wide], weight)

    def mlp_theirs(gelu_both, down_full):
        return dot_nn(gelu_both[count:], down_full).astype(BF)

    def mlp_mine(gelu_both, down_full, came, middle):
        mlp_out = dot_nn(gelu_both[:count], down_full) + came.astype(F32) + bias_down
        return ((middle + mlp_out) * mask).astype(BF).reshape(slots, ROWS, D)[:, :tokens]

    def to_small(grad_qkv, branch_pad, second_sums, out_low, up_bias, grad_rel):
        up_bias = relative(up_bias.reshape(chips, -1))
        up_bias = [jnp.where(core == 0, up_bias, 0.0), turned(jnp.where(core == 0, 0.0, up_bias))]
        up_bias = jnp.stack(up_bias, axis=1).reshape(chips // planes, planes, 2, -1)
        up_bias = jnp.swapaxes(up_bias, 1, 2).reshape(-1, D)
        qkv_bias = jnp.sum(grad_qkv, axis=1, dtype=F32).reshape(3, D)
        rows = [
            jnp.zeros((2, D), F32),
            qkv_bias[:1],
            qkv_bias[2:],
            jnp.sum(branch_pad, axis=0, dtype=F32, keepdims=True),
            second_sums[:2],
            jnp.sum(out_low, axis=0, dtype=F32, keepdims=True),
            up_bias,
        ]
        rows = jnp.concatenate(rows).reshape(-1, SIDE), grad_rel.reshape(-1, SIDE)
        return jnp.concatenate(rows)

    def for_peer(both, weight, gelu_both, down_full, *values):
        ours = block(first_theirs, both, weight), block(mlp_theirs, gelu_both, down_full)
        return *ours, to_small(*values)

    first_sent, mlp_sent, small_early = rounds.go(
        [give_qkv, give_up, give_down, give_proj],
        for_peer,
        qkv_grad_both,
        qkv_half,
        gelu_both,
        down_full,
        grad_qkv,
        branch_pad,
        second_sums,
        out_low,
        up_bias,
        grad_rel,
    )

    stride = max(planes // 4, 1)
    homes = {"qkv": 0, "down": stride, "up": 2 * stride, "proj": 3 * stride}
    me_z = lax.axis_index("gy")
    room = max(up_weight.shape[1], down_weight.shape[0], part, proj_weight.shape[0])
    pieces = [[] for _ in range(planes)]

    def home(**lows):
        parts = []
        for far in range(planes):
            value = sum(
                jnp.where((me_z ^ far) == homes[name], low, jnp.zeros_like(low)) for name, low in lows.items()
            )
            if far:
                value = lax.ppermute(value, "gy", [(homes[name] ^ far, homes[name]) for name in lows])
            parts.append(value)
        return parts

    def arrive(parts):
        for row, piece in zip(pieces, parts):
            row.append(jnp.pad(piece, ((0, room - piece.shape[0]), (0, 0))))

    def moment(old, grad, flip):
        new = MOMENT_MATRIX * old + (grad.T if flip else grad)
        return new, (new.T if flip else new).astype(BF)

    first_came, mlp_came = rounds.go(
        [give_qkv, give_up, give_proj], lambda one, two: (peer(one), peer(two)), first_sent, mlp_sent
    )
    new_down, low_down = moment(down_moment, give_down.out, False)
    new_up, low_up = moment(up_moment, give_up.out, True)

    def to_ends(low_down, low_up, both, weight, first_came, grad_total, short_low):
        arrived = home(down=low_down, up=low_up)
        given = (block(first_mine, both, weight), first_came, short_low, grad_total, mask, middle_rows)
        outs = [jax.ShapeDtypeStruct((slots, tokens, D), F32), jax.ShapeDtypeStruct((8, D), F32)]
        return arrived, *by_slots(first_norm_kernel, "first_norm", given, outs)

    arrived, grad_input, first_sums = rounds.go(
        [give_qkv, give_proj],
        to_ends,
        low_down,
        low_up,
        qkv_grad_both,
        qkv_half,
        first_came,
        grad_total,
        short_low,
    )
    arrive(arrived)
    new_proj, low_proj = moment(proj_moment, give_proj.out, False)

    arrive(rounds.go([give_qkv, give_proj], lambda value: home(proj=value), low_proj))
    while not give_qkv.done:
        rounds.go([give_qkv])
    new_qkv, low_qkv = moment(qkv_moment, give_qkv.out[:part], True)
    arrive(rounds.go([], lambda value: home(qkv=value), low_qkv))
    held = jnp.concatenate([sum(row[1:], row[0]) for row in pieces], axis=0)
    first_rows = jnp.pad(first_sums[:2].reshape(-1, SIDE), ((0, small_early.shape[0] - 2 * D // SIDE), (0, 0)))
    small = small_early + first_rows
    blocks = upper_blocks(dot_tn(held, held))
    fill = -small.shape[0] % (8 * devices // planes)
    summed, block_out = plane_sum(
        rounds,
        jnp.concatenate([blocks, jnp.pad(small, ((0, fill), (0, 0)))], axis=0),
        lambda *values: block(mlp_mine, *values),
        gelu_both,
        down_full,
        mlp_came,
        middle,
    )
    gram = summed[: blocks.shape[0]]
    add_small = sum_whole(summed[blocks.shape[0] : blocks.shape[0] + small.shape[0]], deep)

    def send_back(ortho):
        back = [ortho[0]]
        for far in range(1, planes):
            back.append(lax.ppermute(ortho[far], "gy", [(place, place ^ far) for place in range(planes)]))
        return jnp.stack(back)

    (ortho,) = rounds.go([add_small], lambda *pair: (chain(*pair),), gram, held)
    back = rounds.go([add_small], send_back, ortho.reshape(planes, room, D))
    while not add_small.done:
        rounds.go([add_small])
    small = add_small.out.reshape(-1)
    rel_total = small[devices * spare :].reshape(2, 32, HD)
    vec_total = lax.dynamic_slice_in_dim(small, lax.axis_index(EVERY) * spare, spare)

    def part_of(name, rows):
        return lax.dynamic_index_in_dim(back, me_z ^ homes[name], 0, False)[:rows].astype(F32)

    parts = [
        part_of("qkv", qkv_weight.shape[1]),
        part_of("proj", proj_weight.shape[0]),
        part_of("up", up_weight.shape[1]),
        part_of("down", down_weight.shape[0]),
    ]

    scales = (math.sqrt(3.0), 1.0, math.sqrt(max(1.0, FF / D)), math.sqrt(max(1.0, D / FF)))
    masters = (qkv_weight, proj_weight, up_weight, down_weight)
    flipped = (True, False, True, False)
    new_weights = [
        master - RATE_MATRIX * factor * (part.T if turn else part)
        for master, factor, part, turn in zip(masters, scales, parts, flipped)
    ]

    rate_vec = 0.5 / math.sqrt(float(devices * slots * tokens))
    vec_moment_new = MOMENT_VECTOR * vector_moment + vec_total
    rel_grad = rel_total[:, : 2 * WIN - 1][:, ::-1]
    rel_moment_new = MOMENT_VECTOR * rel_moment + rel_grad
    return (
        block_out,
        grad_input,
        new_qkv,
        new_proj,
        new_up,
        new_down,
        new_weights[0],
        new_weights[1],
        new_weights[2],
        new_weights[3],
        vec_moment_new,
        vectors - rate_vec * vec_moment_new,
        rel_moment_new,
        rel_pos - 0.2 * rate_vec * rel_moment_new,
    )


def solution(mesh):
    size_x, size_y = mesh.shape["gx"], mesh.shape["gy"]
    side = math.isqrt(size_x // 2)
    assert side * side * 2 == size_x
    grid = (side, size_x // 2 // side, 2, size_y)
    split = Mesh(mesh.devices.reshape(grid), ("ga", "gb", "gc", "gy"))
    flat = ("ga", "gb", "gc", "gy")
    slab, cols, rows, line = P(flat, None, None), P(None, flat), P(flat, None), P(flat)
    return jax.shard_map(
        body,
        mesh=split,
        in_specs=(
            (slab, slab, rows, line) + (cols, rows, cols, rows) * 2 + (line, line, P(), P())
        ),
        out_specs=(
            (slab, slab) + (cols, rows, cols, rows) * 2 + (line, line, P(), P())
        ),
        check_vma=False,
    )
```

```python
from functools import partial
import math

import jax
import jax.numpy as jnp
from jax import lax
from jax.experimental import pallas as pl
from jax.experimental.pallas import tpu as pltpu
from jax.experimental.layout import Layout, with_layout_constraint
from jax.sharding import Mesh, PartitionSpec as P

D = 1280
FF = 5120
HEADS = 16
HD = 80
WIN = 14
GRID = 64
ITERS = 5
LANES = 256
ROWS = 208

NORM_EPSILON = 1e-06
ORTHO_EPSILON = 1e-07
COEFF_LINEAR = 3.4445
COEFF_CUBIC = -4.775
COEFF_QUINTIC = 2.0315
MOMENT_MATRIX = 0.95
MOMENT_VECTOR = 0.9
RATE_MATRIX = 0.5

BF = jnp.bfloat16
F32 = jnp.float32


def dot_nn(left, right):
    return jnp.dot(left, right, preferred_element_type=F32)


def dot_tn(left, right):
    return lax.dot_general(left, right, (((0,), (0,)), ((), ())), preferred_element_type=F32)


def dot_nt(left, right):
    return lax.dot_general(left, right, (((1,), (1,)), ((), ())), preferred_element_type=F32)


def split_low(value):
    high = value.astype(BF)
    return high, (value - high.astype(F32)).astype(BF)


GROUP = 8


def spots():
    row = lax.broadcasted_iota(jnp.int32, (32, LANES), 0)
    lane = lax.broadcasted_iota(jnp.int32, (32, LANES), 1)
    along = jnp.where(row < 16, lane // WIN, lane % WIN + 16)
    return jnp.where((along == row) & (lane < WIN * WIN), 1.0, 0.0).astype(BF)


def shifts():
    lane = lax.broadcasted_iota(jnp.int32, (32, LANES), 1)
    down_h = jnp.maximum(WIN - 1 - lane // WIN, 0)
    return down_h, WIN - 1 - lane % WIN


def barrel(value, amount, up):
    for bit in (1, 2, 4, 8):
        moved = pltpu.roll(value, 32 - bit if up else bit, 0)
        value = jnp.where((amount & bit) != 0, moved, value)
    return value


def attend_kernel(q_ref, k_ref, v_ref, rel_ref, out_ref, probs_ref):
    marks = spots()
    marks2 = jnp.concatenate([marks, marks], axis=0)
    shift_h, shift_w = shifts()
    tail_row = lax.broadcasted_iota(jnp.int32, (16, LANES), 0) + (ROWS - 16)
    pad = jnp.zeros((LANES - ROWS, LANES), BF)
    scale = HD ** (-0.5) / math.log(2.0)
    for head in range(GROUP):
        query = q_ref[0, head]
        rel_q = dot_nn(rel_ref[...], query) * (HD**0.5)
        along_h = barrel(rel_q[:32], shift_h, True)[:16]
        along_w = barrel(rel_q[32:], shift_w, True)[:16]
        high, rest = split_low(jnp.concatenate([along_h, along_w], axis=0))
        query_all = jnp.concatenate([query, high, rest], axis=0)
        key_all = jnp.concatenate([k_ref[0, head], marks2], axis=0)
        scores = dot_tn(key_all, query_all)[:ROWS]
        tail = jnp.where(tail_row < WIN * WIN, scores[ROWS - 16 :], -1e30)
        scores = jnp.concatenate([scores[: ROWS - 16], tail], axis=0)
        peak = jnp.max(scores, axis=0, keepdims=True)
        exponent = jnp.exp2((scores - peak) * scale)
        probs = (exponent * (1.0 / jnp.sum(exponent, axis=0, keepdims=True))).astype(BF)
        probs_ref[0, head] = probs
        out_ref[head] = dot_nn(v_ref[0, head], jnp.concatenate([probs, pad], axis=0)).astype(BF)


def attend(qkv, rel_rows):
    slots = qkv.shape[-1] // LANES
    cut = lambda part: pl.BlockSpec((1, GROUP, HD, LANES), lambda s, g, part=part: (part, g, 0, s))
    return pl.pallas_call(
        attend_kernel,
        grid=(slots, HEADS // GROUP),
        in_specs=[cut(0), cut(1), cut(2), pl.BlockSpec((64, HD), lambda s, g: (0, 0))],
        out_specs=[
            pl.BlockSpec((GROUP, HD, LANES), lambda s, g: (g, 0, s)),
            pl.BlockSpec((1, GROUP, ROWS, LANES), lambda s, g: (s, g, 0, 0)),
        ],
        out_shape=[
            jax.ShapeDtypeStruct((HEADS, HD, slots * LANES), BF),
            jax.ShapeDtypeStruct((slots, HEADS, ROWS, LANES), BF),
        ],
        compiler_params=pltpu.CompilerParams(vmem_limit_bytes=16 * 2**20),
        cost_estimate=cheap(slots * HEADS * 2 * LANES * LANES * 256),
        name="attend",
    )(qkv, qkv, qkv, rel_rows)


def attend_back_kernel(q_ref, k_ref, v_ref, g_ref, probs_ref, rel_ref, out_ref, drel_ref):
    marks = spots()
    shift_h, shift_w = shifts()
    pad = jnp.zeros((LANES - ROWS, LANES), BF)
    none = jnp.zeros((16, LANES), F32)
    scale = HD ** (-0.5)
    total = jnp.zeros((64, HD), F32)
    for head in range(GROUP):
        query = q_ref[0, head]
        grad = g_ref[head]
        probs_low = probs_ref[0, head]
        probs = probs_low.astype(F32)
        weighted = dot_tn(v_ref[0, head], grad)[:ROWS] * probs
        flow = jnp.sum(weighted, axis=0, keepdims=True)
        score_low = jnp.concatenate([(weighted - probs * flow).astype(BF), pad], axis=0)
        out_ref[2, head] = dot_nt(grad, jnp.concatenate([probs_low, pad], axis=0)).astype(BF)
        out_ref[1, head] = (dot_nt(query, score_low) * scale).astype(BF)
        mixed = dot_nn(jnp.concatenate([k_ref[0, head], marks], axis=0), score_low)
        rows_h = barrel(jnp.concatenate([mixed[HD : HD + 16], none], axis=0), shift_h, False)
        rows_w = barrel(jnp.concatenate([mixed[HD + 16 :], none], axis=0), shift_w, False)
        both = jnp.concatenate(split_low(jnp.concatenate([rows_h, rows_w], axis=0)), axis=0)
        out_ref[0, head] = (mixed[:HD] * scale + dot_nn(rel_ref[...], both)).astype(BF)
        parts = dot_nt(both, query)
        total = total + parts[:64] + parts[64:]

    @pl.when((pl.program_id(0) == 0) & (pl.program_id(1) == 0))
    def _():
        drel_ref[...] = jnp.zeros_like(drel_ref)

    drel_ref[...] += total


def attend_back(qkv, grad, probs, rel_cols):
    slots = qkv.shape[-1] // LANES
    cut = lambda part: pl.BlockSpec((1, GROUP, HD, LANES), lambda s, g, part=part: (part, g, 0, s))
    return pl.pallas_call(
        attend_back_kernel,
        grid=(slots, HEADS // GROUP),
        in_specs=[
            cut(0),
            cut(1),
            cut(2),
            pl.BlockSpec((GROUP, HD, LANES), lambda s, g: (g, 0, s)),
            pl.BlockSpec((1, GROUP, ROWS, LANES), lambda s, g: (s, g, 0, 0)),
            pl.BlockSpec((HD, 128), lambda s, g: (0, 0)),
        ],
        out_specs=[
            pl.BlockSpec((3, GROUP, HD, LANES), lambda s, g: (0, g, 0, s)),
            pl.BlockSpec((64, HD), lambda s, g: (0, 0)),
        ],
        out_shape=[
            jax.ShapeDtypeStruct((3, HEADS, HD, slots * LANES), BF),
            jax.ShapeDtypeStruct((64, HD), F32),
        ],
        compiler_params=pltpu.CompilerParams(vmem_limit_bytes=20 * 2**20),
        cost_estimate=cheap(slots * HEADS * 5 * LANES * LANES * 256),
        name="attend_back",
    )(qkv, qkv, qkv, grad, probs, rel_cols)


def resident(shape):
    return pl.BlockSpec(shape, lambda *_: (0,) * len(shape))


def cheap(flops):
    return pl.CostEstimate(flops=flops // 8, bytes_accessed=1_000_000, transcendentals=0)


def settings(mebibytes):
    return pltpu.CompilerParams(vmem_limit_bytes=mebibytes * 2**20)


def middle_kernel(att_ref, proj_ref, short_ref, mask_ref, rows_ref, middle_ref, normed_ref):
    branch = dot_tn(att_ref[...], proj_ref[...])[:ROWS] + rows_ref[0:1]
    middle = (short_ref[...].astype(F32) + branch) * mask_ref[...]
    middle_ref[...] = middle
    centred = middle - jnp.mean(middle, axis=1, keepdims=True)
    inverse = lax.rsqrt(jnp.mean(centred * centred, axis=1, keepdims=True) + NORM_EPSILON)
    normed_ref[...] = (centred * inverse * rows_ref[1:2] + rows_ref[2:3]).astype(BF)


def to_middle(attended, proj_full, short, mask, rows):
    slots = attended.shape[1] // LANES
    by_slot = lambda width: pl.BlockSpec((ROWS, width), lambda s: (s, 0))
    return pl.pallas_call(
        middle_kernel,
        grid=(slots,),
        in_specs=[
            pl.BlockSpec((D, LANES), lambda s: (0, s)),
            resident((D, D)),
            by_slot(D),
            by_slot(1),
            resident((8, D)),
        ],
        out_specs=[by_slot(D), by_slot(D)],
        out_shape=[
            jax.ShapeDtypeStruct((slots * ROWS, D), F32),
            jax.ShapeDtypeStruct((slots * ROWS, D), BF),
        ],
        compiler_params=settings(24),
        cost_estimate=cheap(2 * slots * LANES * D * D),
        name="middle",
    )(attended, proj_full, short, mask, rows)


def norm_parts(grad, value, gain):
    centred = value - jnp.mean(value, axis=1, keepdims=True)
    inverse = lax.rsqrt(jnp.mean(centred * centred, axis=1, keepdims=True) + NORM_EPSILON)
    hat = centred * inverse
    scaled = grad * gain
    mean_one = jnp.mean(scaled, axis=1, keepdims=True)
    mean_two = jnp.mean(scaled * hat, axis=1, keepdims=True)
    sums = [jnp.sum(grad * hat, axis=0, keepdims=True), jnp.sum(grad, axis=0, keepdims=True)]
    sums = jnp.concatenate(sums + [jnp.zeros((6, D), F32)], axis=0)
    return inverse * (scaled - mean_one - hat * mean_two), sums


def add_sums(sums_ref, sums):
    @pl.when(pl.program_id(0) == 0)
    def _():
        sums_ref[...] = jnp.zeros_like(sums_ref)

    sums_ref[...] += sums


def second_norm_kernel(grad_ref, came_ref, middle_ref, out_ref, mask_ref, rows_ref, total_ref, pad_ref, sums_ref):
    grad = grad_ref[...] + came_ref[...].astype(F32)
    back, sums = norm_parts(grad, middle_ref[...], rows_ref[1:2])
    total = (out_ref[...].astype(F32) + back) * mask_ref[...]
    total_ref[...] = total
    low = total.astype(BF)
    pad_ref[...] = jnp.concatenate([low, jnp.zeros((LANES - ROWS, D), BF)], axis=0)
    add_sums(sums_ref, sums)


def first_norm_kernel(grad_ref, came_ref, short_ref, total_ref, mask_ref, rows_ref, out_ref, sums_ref):
    mask = mask_ref[...]
    grad = (grad_ref[:ROWS] + came_ref[...].astype(F32)) * mask
    back, sums = norm_parts(grad, short_ref[...].astype(F32), rows_ref[3:4])
    out_ref[0] = ((total_ref[...] + back) * mask)[: WIN * WIN]
    add_sums(sums_ref, sums)


def by_slots(kernel, name, given, outs):
    slots = given[1].shape[0] // ROWS

    def spec(shape):
        if len(shape) == 3:
            return pl.BlockSpec((1,) + shape[1:], lambda s: (s, 0, 0))
        if shape[0] == 8:
            return resident(shape)
        return pl.BlockSpec((shape[0] // slots, shape[1]), lambda s: (s, 0))

    return pl.pallas_call(
        kernel,
        grid=(slots,),
        in_specs=[spec(item.shape) for item in given],
        out_specs=[spec(item.shape) for item in outs],
        out_shape=list(outs),
        compiler_params=settings(32),
        cost_estimate=cheap(1_000_000),
        name=name,
    )(*given)


SIDE = 256
SPOTS = [(row, column) for row in range(D // SIDE) for column in range(row, D // SIDE)]


def upper_blocks(gram):
    parts = [
        gram[row * SIDE : (row + 1) * SIDE, column * SIDE : (column + 1) * SIDE] for row, column in SPOTS
    ]
    return jnp.concatenate(parts, axis=0)


def chain_kernel(count, gram_ref, y_ref, *refs):
    outs, (high_ref, rest_ref, b_ref, t_high, t_rest, z_high, z_rest) = refs[:count], refs[count:]
    columns = [slice(start, start + SIDE) for start in range(0, D, SIDE)]
    row = lax.broadcasted_iota(jnp.int32, (SIDE, SIDE), 0)
    spot = row == lax.broadcasted_iota(jnp.int32, (SIDE, SIDE), 1)
    trace = jnp.zeros((), F32)
    for place, (row, column) in enumerate(SPOTS):
        if row == column:
            trace = trace + jnp.sum(jnp.where(spot, gram_ref[place * SIDE : (place + 1) * SIDE, :], 0.0))
    inverse = 1.0 / (jnp.sqrt(trace) + ORTHO_EPSILON)
    for place, (row, column) in enumerate(SPOTS):
        block = gram_ref[place * SIDE : (place + 1) * SIDE, :] * inverse * inverse
        for part, over, down in ((block, row, column), (block.T, column, row)):
            high, rest = split_low(part)
            high_ref[columns[over], columns[down]] = high
            rest_ref[columns[over], columns[down]] = rest
    z_high[0] = y_ref[...]

    def mirror(ref, values, place):
        cut = columns[place]
        ref[: (place + 1) * SIDE, cut] = values
        for over in range(place):
            ref[cut, columns[over]] = values[columns[over], :].T

    def polynomial():
        for place, cut in enumerate(columns):
            rows = slice(0, (place + 1) * SIDE)
            square = dot_nn(high_ref[rows, :], high_ref[:, cut])
            value = high_ref[rows, cut].astype(F32) + rest_ref[rows, cut].astype(F32)
            poly = COEFF_CUBIC * value + COEFF_QUINTIC * square
            line = lax.broadcasted_iota(jnp.int32, poly.shape, 0) - place * SIDE
            eye = line == lax.broadcasted_iota(jnp.int32, poly.shape, 1)
            mirror(b_ref, (poly + jnp.where(eye, COEFF_LINEAR, 0.0)).astype(BF), place)

    def follow(now, cut, fine):
        value = dot_nn(z_high[now], b_ref[:, cut])
        return value + dot_nn(z_rest[now], b_ref[:, cut]) if fine else value

    def advance(now, fine, z_fine, z_more):
        later = 1 - now
        polynomial()
        for cut in columns:
            value = dot_nn(b_ref[...], high_ref[:, cut])
            if fine:
                value = value + dot_nn(b_ref[...], rest_ref[:, cut])
            t_high[:, cut], rest = split_low(value)
            if fine:
                t_rest[:, cut] = rest
            z_high[later, :, cut], rest = split_low(follow(now, cut, z_fine))
            if z_more:
                z_rest[later, :, cut] = rest
        for place, cut in enumerate(columns):
            rows = slice(0, (place + 1) * SIDE)
            value = dot_nn(t_high[rows, :], b_ref[:, cut])
            if fine:
                value = value + dot_nn(t_rest[rows, :], b_ref[:, cut])
            high, rest = split_low(value)
            mirror(high_ref, high, place)
            mirror(rest_ref, rest, place)

    advance(0, True, False, True)

    @pl.loop(1, ITERS - 2)
    def _(step):
        advance(step % 2, True, True, True)

    advance((ITERS - 2) % 2, False, False, False)
    polynomial()
    for cut in columns:
        value = (follow((ITERS - 1) % 2, cut, False) * inverse).astype(BF)
        for place, out_ref in enumerate(outs):
            rows = out_ref.shape[0]
            out_ref[:, cut] = value[place * rows : (place + 1) * rows]


def chain(gram, rows, count):
    half = pltpu.VMEM((D, D), BF)
    flow = pltpu.VMEM((2,) + rows.shape, BF)
    whole = pl.BlockSpec(memory_space=pltpu.VMEM)
    part = rows.shape[0] // count
    pieces = count if part % 16 == 0 else 1
    out = pl.pallas_call(
        partial(chain_kernel, pieces),
        in_specs=[whole, whole],
        out_specs=[whole] * pieces,
        out_shape=[jax.ShapeDtypeStruct((rows.shape[0] // pieces, D), BF)] * pieces,
        scratch_shapes=[half] * 5 + [flow] * 2,
        compiler_params=settings(56),
        cost_estimate=pl.CostEstimate(flops=18 * 2 * D**3, bytes_accessed=6 * D * D, transcendentals=0),
        name="chain",
    )(gram, rows)
    return out if pieces == count else [out[0][at * part : (at + 1) * part] for at in range(count)]


EVERY = ("ga", "gb", "gc", "gy")


def peer(value):
    return lax.ppermute(value, "gc", [(0, 1), (1, 0)])


def steps_of(axis):
    return lax.axis_size(axis).bit_length() - 1


def first_stages():
    return [("f", step) for step in reversed(range(steps_of("ga")))]


def second_stages():
    return [("s", step) for step in reversed(range(steps_of("gb")))]


def plane_stages():
    return [("z", step) for step in range(steps_of("gy"))]


def gather_groups():
    deep = plane_stages()
    return [deep[1:][::-1], deep[:1]], [second_stages()[::-1]], [first_stages()[::-1]]


def reduce_groups():
    deep = plane_stages()
    return [first_stages()], [second_stages()], [deep[:1], deep[1:]]


def half_stages():
    return first_stages() + second_stages() + plane_stages()


def bit_of(stage, core):
    kind, step = stage
    if kind == "z":
        return "gy", steps_of("gy") - 1 - step if core == 0 else step
    return ("ga" if (kind == "f") == (core == 0) else "gb"), step


def my_bit(stage):
    values = []
    for core in range(2):
        axis, step = bit_of(stage, core)
        values.append((lax.axis_index(axis) >> step) & 1)
    return jnp.where(lax.axis_index("gc") == 0, values[0], values[1])


def swap(value, stage):
    if stage == "c":
        return peer(value)
    sizes = [lax.axis_size(axis) for axis in EVERY]
    pairs = []
    for place in range(math.prod(sizes)):
        spot, rest = [], place
        for size in reversed(sizes):
            spot.insert(0, rest % size)
            rest //= size
        axis, step = bit_of(stage, spot[2])
        spot[EVERY.index(axis)] ^= 1 << step
        other = 0
        for size, at in zip(sizes, spot):
            other = other * size + at
        pairs.append((place, other))
    return lax.ppermute(value, EVERY, pairs)


class Rounds:
    def __init__(self):
        self.last = None

    def go(self, chains, work=None, *values):
        chains = [chain for chain in chains if not chain.done]
        while long := [chain for chain in chains if chain.left > 1]:
            self.once(long)
        out = self.once(chains, work, *values)
        for chain in chains:
            chain.left = chain.counts.pop(0) if chain.counts else 0
        return out

    def once(self, chains, work=None, *values):
        [chain.look() for chain in chains]
        marks = [] if self.last is None else [self.last]
        held = [lax.optimization_barrier((chain.value, *marks))[0] for chain in chains]
        came = [swap(value, chain.stage) for value, chain in zip(held, chains)]
        ready = lax.optimization_barrier((*values, *held, *marks))
        out = () if work is None else work(*ready[: len(values)])
        leaves, tree = jax.tree.flatten(out)
        ended = lax.optimization_barrier(tuple(came) + tuple(leaves))
        self.last = ended[0]
        for chain, value in zip(chains, ended):
            chain.take(value)
            chain.left -= 1
        return jax.tree.unflatten(tree, ended[len(chains) :])


class Chain:
    def __init__(self, work, groups):
        self.work, self.ended, self.result = work, False, None
        self.pending = [None]
        self.counts = [len(group) for group in groups if group]
        self.left = self.counts.pop(0)

    def take(self, came):
        self.pending = [came]

    def look(self):
        if self.pending:
            try:
                self.value, self.stage = self.work.send(self.pending.pop())
            except StopIteration as stop:
                self.ended, self.result = True, stop.value

    @property
    def done(self):
        self.look()
        return self.ended

    @property
    def out(self):
        self.look()
        return self.result


def gather_half(shard):
    groups = sum(gather_groups(), [])

    def work():
        held = shard[None]
        for stage in sum(groups, []):
            came = yield held, stage
            first = my_bit(stage) == 0
            held = jnp.concatenate([jnp.where(first, held, came), jnp.where(first, came, held)], axis=0)
        return held.reshape(-1, shard.shape[-1])

    return Chain(work(), groups)


def gather_relative(shard, groups):
    def work():
        order, canon = sum(groups, []), half_stages()
        held = shard
        for stage in order[:-1]:
            came = yield held, stage
            held = jnp.stack([held, came])
        came = yield held, order[-1]
        there = order[-2::-1]
        turn = [there.index(stage) for stage in canon[1:]] + [len(there), len(there) + 1]
        return tuple(half.transpose(turn).reshape(-1, shard.shape[-1]) for half in (held, came))

    return Chain(work(), groups)


def relative(value):
    stages = half_stages()
    place = sum(my_bit(stage) << (len(stages) - 1 - at) for at, stage in enumerate(stages))
    spots = jnp.arange(value.shape[0])
    picker = ((spots[:, None] ^ place) == spots[None, :]).astype(F32)
    return jnp.dot(picker, value, precision=lax.Precision.HIGHEST, preferred_element_type=F32)


def reduce_half(grad, groups, kind=BF):
    def work():
        live = half_stages()
        parts = [grad.reshape((2,) * len(live) + (-1, grad.shape[-1]))]
        for stage in sum(groups, []):
            place, mine = live.index(stage), my_bit(stage)
            live.remove(stage)

            def pick(which):
                cuts = [lax.dynamic_index_in_dim(part, which, place, False) for part in parts]
                return cuts[0] if len(cuts) == 1 else (cuts[0].astype(F32) + cuts[1].astype(F32)).astype(kind)

            send = pick(1 - mine)
            parts = list(lax.optimization_barrier((*parts, send))[:-1])
            keep = pick(mine)
            came = yield send, stage
            parts = [keep, came]
        return parts[0].astype(F32) + parts[1].astype(F32)

    return Chain(work(), groups)


def reduce_relative(keep, send, groups):
    def work():
        live, order = half_stages(), sum(groups, [])
        came = yield send, order[0]
        assert order[0] == live[0]
        live.remove(order[0])
        shape = (2,) * len(live) + (-1, send.shape[-1])
        parts = [keep().reshape(shape), came.reshape(shape)]
        for stage in order[1:]:
            place = live.index(stage)
            live.remove(stage)

            def pick(which):
                cuts = [lax.index_in_dim(part, which, place, False).astype(F32) for part in parts]
                return (cuts[0] + cuts[1]).astype(BF)

            away = pick(1)
            parts = list(lax.optimization_barrier((*parts, away))[:-1])
            kept = pick(0)
            came = yield away, stage
            parts = [kept, came]
        return parts[0].astype(F32) + parts[1].astype(F32)

    return Chain(work(), groups)


def turned(value):
    stages = half_stages()
    shape = value.shape
    value = value.reshape((2,) * len(stages) + shape[1:])
    side, deep = len(first_stages()), len(plane_stages())
    order = list(range(side, 2 * side)) + list(range(side)) + list(reversed(range(2 * side, 2 * side + deep)))
    order += list(range(2 * side + deep, value.ndim))
    return value.transpose(order).reshape(shape)


def join_halves(mine, theirs):
    chips = 1 << len(half_stages())
    planes = lax.axis_size("gy")
    first = lax.axis_index("gc") == 0
    shape = (chips, -1) + mine.shape[1:]
    mine, theirs = mine.reshape(shape), theirs.reshape(shape)
    both = [jnp.where(first, mine, theirs), turned(jnp.where(first, theirs, mine))]
    both = [half.reshape((chips // planes, planes) + half.shape[1:]) for half in both]
    return jnp.stack(both, axis=1).reshape((-1,) + mine.shape[2:])


def cut_half(value, which):
    chips = 1 << len(half_stages())
    planes = lax.axis_size("gy")
    shape = value.shape
    value = value.reshape((chips // planes, 2, planes, -1) + shape[1:])
    halves = [value[:, core].reshape((chips, -1) + shape[1:]) for core in range(2)]
    return jnp.where(which == 0, halves[0], turned(halves[1])).reshape((-1,) + shape[1:])


def sum_rows(value, stages):
    def work():
        held = value
        for stage in stages:
            halves = held.reshape((2, held.shape[0] // 2) + held.shape[1:])
            mine = my_bit(stage)
            keep = lax.dynamic_index_in_dim(halves, mine, 0, False)
            came = yield lax.dynamic_index_in_dim(halves, 1 - mine, 0, False), stage
            held = keep + came
        return held

    return Chain(work(), [[stage] for stage in stages])


def spread_rows(value, stages):
    def work():
        held = value
        for stage in stages:
            came = yield held, stage
            first = my_bit(stage) == 0
            held = jnp.concatenate([jnp.where(first, held, came), jnp.where(first, came, held)], axis=0)
        return held

    return Chain(work(), [[stage] for stage in stages])


def plane_sum(rounds, value, work, *values):
    core = lax.axis_index("gc")
    halves = value.reshape((2, value.shape[0] // 2) + value.shape[1:])

    def over_cores(mine, theirs):
        return mine + peer(theirs)

    held = rounds.go(
        [],
        over_cores,
        lax.dynamic_index_in_dim(halves, core, 0, False),
        lax.dynamic_index_in_dim(halves, 1 - core, 0, False),
    )
    stages = first_stages() + second_stages()
    chain = sum_rows(held, stages)
    out = rounds.go([chain], work, *values)
    while not chain.done:
        rounds.go([chain])
    chain = spread_rows(chain.out, stages[::-1])
    while not chain.done:
        rounds.go([chain])
    held = chain.out
    came = rounds.go([], peer, held)
    held = [jnp.where(core == 0, held, came), jnp.where(core == 0, came, held)]
    return jnp.concatenate(held, axis=0), out


def sum_whole(value, stages):
    def work():
        held = value
        for stage in stages:
            came = yield held, stage
            held = held + came
        return held

    return Chain(work(), [[stage] for stage in stages])


def token_mask(placement, counts):
    slot_count = placement.shape[0]
    live = (jnp.arange(slot_count, dtype=jnp.int32) < counts[0]).astype(F32)
    inner = jnp.arange(WIN * WIN, dtype=jnp.int32)
    row_pos = placement[:, 0:1] * WIN + inner[None, :] // WIN
    col_pos = placement[:, 1:2] * WIN + inner[None, :] % WIN
    inside = ((row_pos < GRID) & (col_pos < GRID)).astype(F32)
    return inside * live[:, None]


def normalised(value):
    centred = value - jnp.mean(value, axis=-1, keepdims=True)
    inverse = lax.rsqrt(jnp.mean(centred * centred, axis=-1, keepdims=True) + NORM_EPSILON)
    return centred * inverse, inverse


def norm_back(grad, hat, inverse, gain):
    scaled = grad * gain
    mean_one = jnp.mean(scaled, axis=-1, keepdims=True)
    mean_two = jnp.mean(scaled * hat, axis=-1, keepdims=True)
    return inverse * (scaled - mean_one - hat * mean_two)


def pad_slots(value, rows):
    slots, given, width = value.shape
    return jnp.pad(value, ((0, 0), (0, rows - given), (0, 0))).reshape(slots * rows, width)


def widen_slots(value):
    return pad_slots(value.reshape(-1, ROWS, value.shape[1]), LANES)


def narrow_slots(value):
    return value.reshape(-1, LANES, value.shape[1])[:, :ROWS].reshape(-1, value.shape[1])


def body(
    windows,
    cotangent,
    placement,
    counts,
    qkv_weight,
    proj_weight,
    up_weight,
    down_weight,
    qkv_moment,
    proj_moment,
    up_moment,
    down_moment,
    vectors,
    vector_moment,
    rel_pos,
    rel_moment,
):
    core = lax.axis_index("gc")
    planes = lax.axis_size("gy")
    chips = 1 << len(half_stages())
    devices = 2 * chips
    slots, tokens, _ = windows.shape
    wide = slots * LANES
    first, second, deep = first_stages(), second_stages(), plane_stages()
    rounds = Rounds()

    def block(work, *values):
        shapes = jax.eval_shape(work, *values)

        def idle(*_):
            return jax.tree.map(lambda item: jnp.zeros(item.shape, item.dtype), shapes)

        return lax.cond(counts[0] > 0, work, idle, *values)

    mask = pad_slots(token_mask(placement, counts)[:, :, None], ROWS)
    short_low = pad_slots(windows, ROWS) * mask.astype(BF)
    out_low = pad_slots(cotangent, ROWS) * mask.astype(BF)
    count = short_low.shape[0]
    by_z, by_second, by_first = gather_groups()
    part, spare = qkv_weight.shape[1], vectors.shape[0]
    vec_rows = jnp.pad(vectors.astype(BF)[None], ((0, 7), (0, D - spare)))
    take_qkv = gather_half(jnp.concatenate([qkv_weight.astype(BF).T, vec_rows], axis=0))
    take_proj = gather_half(proj_weight.astype(BF))
    take_up = gather_relative(up_weight.astype(BF).T, by_z + by_second + by_first)
    take_down = gather_relative(down_weight.astype(BF), by_second + by_z + by_first)

    mask_row = jnp.pad(mask.astype(BF).T, ((0, 7), (0, D - count)))
    rounds.go([take_qkv, take_down])
    short_peer = rounds.go([take_qkv, take_proj], peer, jnp.concatenate([short_low, mask_row], axis=0))
    rounds.go([take_qkv, take_up, take_proj])

    def first_hats(mine, theirs):
        return normalised(mine.astype(F32))[0], normalised(theirs[:count].astype(F32))[0]

    (hat_mine, hat_peer), out_peer = rounds.go(
        [take_qkv, take_up, take_proj],
        lambda one, two, three: (block(first_hats, one, two), peer(three)),
        short_low,
        short_peer,
        out_low,
    )
    qkv_half = take_qkv.out
    wide_part = part + 8

    def slim(value):
        return value.reshape((chips, wide_part) + value.shape[1:])[:, :part].reshape((-1,) + value.shape[1:])

    def stout(value):
        value = value.reshape((chips, part) + value.shape[1:])
        return jnp.pad(value, ((0, 0), (0, 8)) + ((0, 0),) * (value.ndim - 2)).reshape((-1,) + value.shape[2:])

    def to_qkv(qkv_half, hat, vec, live, bias):
        rows = widen_slots(((hat * vec[:D] + vec[D : 2 * D]) * live).astype(BF))
        return with_layout_constraint((dot_nt(qkv_half, rows) + bias).astype(BF), Layout((0, 1))), rows

    def both_qkv(qkv_half, hat_mine, hat_peer, short_peer, mask):
        vec_half = qkv_half.reshape(chips, wide_part, D)[:, part, :spare]
        vec = join_halves(vec_half, peer(vec_half)).reshape(-1).astype(F32)
        bias_qkv = jnp.concatenate([vec[2 * D : 3 * D], jnp.zeros((D,), F32), vec[3 * D : 4 * D]])
        bias_qkv = stout(cut_half(bias_qkv, core))[:, None]
        live = short_peer[count, :count].astype(F32)[:, None]
        theirs, pad_peer = block(to_qkv, qkv_half, hat_peer, vec, live, bias_qkv)
        came = tuple(peer(piece) for piece in jnp.split(theirs, 4, axis=0))
        mine, pad_mine = block(to_qkv, qkv_half, hat_mine, vec, mask, bias_qkv)
        return mine, came, vec, pad_mine, pad_peer

    qkv_mine, qkv_came, vec, pad_mine, pad_peer = rounds.go(
        [take_up, take_proj, take_down], both_qkv, qkv_half, hat_mine, hat_peer, short_peer, mask
    )
    proj_half = take_proj.out
    bias_down = vec[7 * D : 8 * D]
    rel_low = rel_pos.astype(BF)[:, ::-1]
    rel_rows = jnp.pad(rel_low, ((0, 0), (0, 5), (0, 0))).reshape(64, HD)
    rel_cols = jnp.concatenate([rel_rows, rel_rows], axis=0).T

    def to_attended(mine, came, proj_half, out_low, out_peer, vec):
        proj_came = peer(proj_half)
        qkv = join_halves(slim(mine), slim(jnp.concatenate(came, axis=0))).reshape(3, HEADS, HD, wide)
        attended, probs = attend(qkv, rel_rows)
        out_both = jnp.concatenate([out_low, out_peer], axis=0)
        bias_up = relative(cut_half(vec[8 * D :], core).reshape(chips, -1)).reshape(1, -1)
        table = vec[: 8 * D].reshape(8, D)
        middle_rows = jnp.concatenate([table[4:7], table[:1], table[:4]], axis=0)
        return join_halves(proj_half, proj_came), out_both, qkv, attended, probs, bias_up, middle_rows

    proj_full, out_both, qkv, attended, probs, bias_up, middle_rows = rounds.go(
        [take_up, take_down], to_attended, qkv_mine, qkv_came, proj_half, out_low, out_peer, vec
    )
    attended = attended.reshape(D, wide)
    up_halves = take_up.out
    width = up_halves[0].shape[0]

    def to_gelu(mine, came, up_full, out_both):
        both = jnp.concatenate([mine, came], axis=0)
        pre = dot_nt(both, up_full) + bias_up
        bell = jnp.exp(-0.5 * pre * pre)
        below = 0.5 * (1.0 + lax.erf(pre * (0.5**0.5)))
        gelu = (pre * below).astype(BF)
        slope = (below + pre * bell * (2.0 * math.pi) ** -0.5).astype(BF)
        send = dot_tn(gelu[:, width:], out_both).astype(BF)
        return both, gelu, slope, dot_tn(gelu[:, :width], out_both).astype(BF), send

    def to_hidden(attended, up_one, up_two):
        middle, normed = to_middle(attended, proj_full, short_low, mask, middle_rows)
        came = peer(normed)
        up_full = jnp.concatenate([up_one, up_two], axis=0)
        return middle, up_full, *to_gelu(normed, came, up_full, out_both)

    middle, up_full, normed_both, gelu_both, slope, keep_down, send_down = rounds.go(
        [take_down], to_hidden, attended, *up_halves
    )
    down_halves = take_down.out

    by_first, by_second, by_z = reduce_groups()
    mixed_order = by_first + by_z + by_second
    plane_last = by_first + by_second + by_z
    give_down = reduce_relative(lambda: keep_down, send_down, mixed_order)

    def to_pre(down_one, down_two, out_both, slope, up_full):
        down_full = jnp.concatenate([down_one, down_two], axis=0)
        pre = (dot_nt(out_both, down_full) * slope.astype(F32)).astype(BF)
        return down_full, pre, dot_nn(pre[count:], up_full).astype(BF)

    def second_mine(pre, up_full):
        return dot_nn(pre[:count], up_full)

    def up_back(pre, normed_both):
        send = dot_tn(pre[:, width:], normed_both).astype(BF)
        return send, jnp.sum(pre, axis=0, dtype=F32)

    def to_branch(down_one, down_two, out_both, slope, up_full, normed_both, middle):
        down_full, pre, theirs = to_pre(down_one, down_two, out_both, slope, up_full)
        came = peer(theirs)
        send_up, up_bias = block(up_back, pre, normed_both)
        given = (second_mine(pre, up_full), came, middle, out_low, mask, middle_rows)
        shapes = (((count, D), F32), ((wide, D), BF), ((8, D), F32))
        outs = [jax.ShapeDtypeStruct(*shape) for shape in shapes]
        return down_full, pre, send_up, up_bias, *by_slots(second_norm_kernel, "second_norm", given, outs)

    down_full, pre, send_up, up_bias, grad_total, branch_pad, second_sums = rounds.go(
        [give_down], to_branch, *down_halves, out_both, slope, up_full, normed_both, middle
    )
    kept = {"up": lambda: dot_tn(pre[:, :width], normed_both).astype(BF)}
    give_up = reduce_relative(lambda: kept["up"](), send_up, plane_last)

    def attention_back(branch_pad, attended, pre, normed_both):
        keep_up = dot_tn(pre[:, :width], normed_both).astype(BF)
        grad_proj = dot_nn(attended, branch_pad).astype(BF)
        proj_came = peer(cut_half(grad_proj, 1 - core))
        grad_att = dot_nt(proj_full, branch_pad).astype(BF).reshape(HEADS, HD, wide)
        grad_qkv, grad_rel = attend_back(qkv, grad_att, probs, rel_cols)
        grad_qkv = grad_qkv.reshape(3 * D, wide)
        grad_proj = (cut_half(grad_proj, core).astype(F32) + proj_came.astype(F32)).astype(BF)
        halves = [stout(cut_half(grad_qkv, which)) for which in (core, 1 - core)]
        halves[0] = jnp.pad(halves[0], ((0, 0), (0, wide)))
        return grad_qkv, grad_rel, *halves, grad_proj, keep_up

    grad_qkv, grad_rel, qkv_grad_mine, qkv_grad_theirs, grad_proj, keep_up = rounds.go(
        [give_up, give_down], attention_back, branch_pad, attended, pre, normed_both
    )
    kept["up"] = lambda: keep_up
    give_proj = reduce_half(grad_proj, plane_last)
    normed_pad = jnp.concatenate([pad_mine, pad_peer], axis=0)

    def qkv_back(mine, came, normed_pad):
        both = lax.dynamic_update_slice(mine, came, (0, wide))
        return both, dot_nn(both, normed_pad).astype(BF)

    def to_qkv_grad(mine, theirs, normed_pad):
        return qkv_back(mine, peer(theirs), normed_pad)

    qkv_grad_both, grad_qkv_half = rounds.go(
        [give_up, give_down, give_proj], to_qkv_grad, qkv_grad_mine, qkv_grad_theirs, normed_pad
    )
    give_qkv = reduce_half(grad_qkv_half, plane_last)

    def first_theirs(both, weight):
        return narrow_slots(dot_tn(both[:, wide:], weight).astype(BF))

    def first_mine(both, weight):
        return dot_tn(both[:, :wide], weight)

    def mlp_theirs(gelu_both, down_full):
        return dot_nn(gelu_both[count:], down_full).astype(BF)

    def mlp_mine(gelu_both, down_full, came, middle):
        mlp_out = dot_nn(gelu_both[:count], down_full) + came.astype(F32) + bias_down
        return ((middle + mlp_out) * mask).astype(BF).reshape(slots, ROWS, D)[:, :tokens]

    def to_small(grad_qkv, branch_pad, second_sums, out_low, up_bias, grad_rel):
        up_bias = relative(up_bias.reshape(chips, -1))
        up_bias = [jnp.where(core == 0, up_bias, 0.0), turned(jnp.where(core == 0, 0.0, up_bias))]
        up_bias = jnp.stack(up_bias, axis=1).reshape(chips // planes, planes, 2, -1)
        up_bias = jnp.swapaxes(up_bias, 1, 2).reshape(-1, D)
        qkv_bias = jnp.sum(grad_qkv, axis=1, dtype=F32).reshape(3, D)
        rows = [
            jnp.zeros((2, D), F32),
            qkv_bias[:1],
            qkv_bias[2:],
            jnp.sum(branch_pad, axis=0, dtype=F32, keepdims=True),
            second_sums[:2],
            jnp.sum(out_low, axis=0, dtype=F32, keepdims=True),
            up_bias,
        ]
        rows = jnp.concatenate(rows).reshape(-1, SIDE), grad_rel.reshape(-1, SIDE)
        return jnp.concatenate(rows)

    def for_peer(both, weight, gelu_both, down_full, *values):
        ours = block(first_theirs, both, weight), block(mlp_theirs, gelu_both, down_full)
        return *ours, to_small(*values)

    first_sent, mlp_sent, small_early = rounds.go(
        [give_qkv, give_up, give_down, give_proj],
        for_peer,
        qkv_grad_both,
        qkv_half,
        gelu_both,
        down_full,
        grad_qkv,
        branch_pad,
        second_sums,
        out_low,
        up_bias,
        grad_rel,
    )

    stride = max(planes // 4, 1)
    homes = {"qkv": 0, "down": stride, "up": 2 * stride, "proj": 3 * stride}
    me_z = lax.axis_index("gy")
    room = max(up_weight.shape[1], down_weight.shape[0], part, proj_weight.shape[0])
    pieces = [[] for _ in range(planes)]

    def home(**lows):
        parts = []
        for far in range(planes):
            value = sum(
                jnp.where((me_z ^ far) == homes[name], low, jnp.zeros_like(low)) for name, low in lows.items()
            )
            if far:
                value = lax.ppermute(value, "gy", [(homes[name] ^ far, homes[name]) for name in lows])
            parts.append(value)
        return parts

    def arrive(parts):
        for row, piece in zip(pieces, parts):
            row.append(jnp.pad(piece, ((0, room - piece.shape[0]), (0, 0))))

    def moment(old, grad, flip):
        new = MOMENT_MATRIX * old + (grad.T if flip else grad)
        return new, (new.T if flip else new).astype(BF)

    first_came, mlp_came = rounds.go(
        [give_qkv, give_up, give_proj], lambda one, two: (peer(one), peer(two)), first_sent, mlp_sent
    )
    new_down, low_down = moment(down_moment, give_down.out, False)
    new_up, low_up = moment(up_moment, give_up.out, True)

    def to_ends(low_down, low_up, both, weight, first_came, grad_total, short_low):
        arrived = home(down=low_down, up=low_up)
        given = (block(first_mine, both, weight), first_came, short_low, grad_total, mask, middle_rows)
        outs = [jax.ShapeDtypeStruct((slots, tokens, D), F32), jax.ShapeDtypeStruct((8, D), F32)]
        return arrived, *by_slots(first_norm_kernel, "first_norm", given, outs)

    arrived, grad_input, first_sums = rounds.go(
        [give_qkv, give_proj],
        to_ends,
        low_down,
        low_up,
        qkv_grad_both,
        qkv_half,
        first_came,
        grad_total,
        short_low,
    )
    arrive(arrived)
    new_proj, low_proj = moment(proj_moment, give_proj.out, False)

    arrive(rounds.go([give_qkv, give_proj], lambda value: home(proj=value), low_proj))
    while not give_qkv.done:
        rounds.go([give_qkv])
    new_qkv, low_qkv = moment(qkv_moment, give_qkv.out[:part], True)
    arrive(rounds.go([], lambda value: home(qkv=value), low_qkv))
    held = jnp.concatenate([sum(row[1:], row[0]) for row in pieces], axis=0)
    first_rows = jnp.pad(first_sums[:2].reshape(-1, SIDE), ((0, small_early.shape[0] - 2 * D // SIDE), (0, 0)))
    small = small_early + first_rows
    blocks = upper_blocks(dot_tn(held, held))
    fill = -small.shape[0] % (8 * devices // planes)
    summed, block_out = plane_sum(
        rounds,
        jnp.concatenate([blocks, jnp.pad(small, ((0, fill), (0, 0)))], axis=0),
        lambda *values: block(mlp_mine, *values),
        gelu_both,
        down_full,
        mlp_came,
        middle,
    )
    gram = summed[: blocks.shape[0]]
    add_small = sum_whole(summed[blocks.shape[0] : blocks.shape[0] + small.shape[0]], deep)

    def send_back(ortho):
        back = [ortho[0]]
        for far in range(1, planes):
            back.append(lax.ppermute(ortho[far], "gy", [(place, place ^ far) for place in range(planes)]))
        return jnp.stack(back)

    ortho = rounds.go([add_small], lambda *pair: chain(*pair, planes), gram, held)
    back = rounds.go([add_small], lambda *parts: send_back(parts), *ortho)
    while not add_small.done:
        rounds.go([add_small])
    small = add_small.out.reshape(-1)
    rel_total = small[devices * spare :].reshape(2, 32, HD)
    vec_total = lax.dynamic_slice_in_dim(small, lax.axis_index(EVERY) * spare, spare)

    def part_of(name, rows):
        return lax.dynamic_index_in_dim(back, me_z ^ homes[name], 0, False)[:rows].astype(F32)

    parts = [
        part_of("qkv", qkv_weight.shape[1]),
        part_of("proj", proj_weight.shape[0]),
        part_of("up", up_weight.shape[1]),
        part_of("down", down_weight.shape[0]),
    ]

    scales = (math.sqrt(3.0), 1.0, math.sqrt(max(1.0, FF / D)), math.sqrt(max(1.0, D / FF)))
    masters = (qkv_weight, proj_weight, up_weight, down_weight)
    flipped = (True, False, True, False)
    new_weights = [
        master - RATE_MATRIX * factor * (part.T if turn else part)
        for master, factor, part, turn in zip(masters, scales, parts, flipped)
    ]

    rate_vec = 0.5 / math.sqrt(float(devices * slots * tokens))
    vec_moment_new = MOMENT_VECTOR * vector_moment + vec_total
    rel_grad = rel_total[:, : 2 * WIN - 1][:, ::-1]
    rel_moment_new = MOMENT_VECTOR * rel_moment + rel_grad
    return (
        block_out,
        grad_input,
        new_qkv,
        new_proj,
        new_up,
        new_down,
        new_weights[0],
        new_weights[1],
        new_weights[2],
        new_weights[3],
        vec_moment_new,
        vectors - rate_vec * vec_moment_new,
        rel_moment_new,
        rel_pos - 0.2 * rate_vec * rel_moment_new,
    )


def solution(mesh):
    size_x, size_y = mesh.shape["gx"], mesh.shape["gy"]
    side = math.isqrt(size_x // 2)
    assert side * side * 2 == size_x
    grid = (side, size_x // 2 // side, 2, size_y)
    split = Mesh(mesh.devices.reshape(grid), ("ga", "gb", "gc", "gy"))
    flat = ("ga", "gb", "gc", "gy")
    slab, cols, rows, line = P(flat, None, None), P(None, flat), P(flat, None), P(flat)
    return jax.shard_map(
        body,
        mesh=split,
        in_specs=(
            (slab, slab, rows, line) + (cols, rows, cols, rows) * 2 + (line, line, P(), P())
        ),
        out_specs=(
            (slab, slab) + (cols, rows, cols, rows) * 2 + (line, line, P(), P())
        ),
        check_vma=False,
    )
```

```python
from functools import partial
import math

import jax
import jax.numpy as jnp
from jax import lax
from jax.experimental import pallas as pl
from jax.experimental.pallas import tpu as pltpu
from jax.experimental.layout import Layout, with_layout_constraint
from jax.sharding import Mesh, PartitionSpec as P

D = 1280
FF = 5120
HEADS = 16
HD = 80
WIN = 14
GRID = 64
ITERS = 5
LANES = 256
ROWS = 208

NORM_EPSILON = 1e-06
ORTHO_EPSILON = 1e-07
COEFF_LINEAR = 3.4445
COEFF_CUBIC = -4.775
COEFF_QUINTIC = 2.0315
MOMENT_MATRIX = 0.95
MOMENT_VECTOR = 0.9
RATE_MATRIX = 0.5

BF = jnp.bfloat16
F32 = jnp.float32


def dot_nn(left, right):
    return jnp.dot(left, right, preferred_element_type=F32)


def dot_tn(left, right):
    return lax.dot_general(left, right, (((0,), (0,)), ((), ())), preferred_element_type=F32)


def dot_nt(left, right):
    return lax.dot_general(left, right, (((1,), (1,)), ((), ())), preferred_element_type=F32)


def split_low(value):
    high = value.astype(BF)
    return high, (value - high.astype(F32)).astype(BF)


GROUP = 8


def spots():
    row = lax.broadcasted_iota(jnp.int32, (32, LANES), 0)
    lane = lax.broadcasted_iota(jnp.int32, (32, LANES), 1)
    along = jnp.where(row < 16, lane // WIN, lane % WIN + 16)
    return jnp.where((along == row) & (lane < WIN * WIN), 1.0, 0.0).astype(BF)


def shifts():
    lane = lax.broadcasted_iota(jnp.int32, (32, LANES), 1)
    down_h = jnp.maximum(WIN - 1 - lane // WIN, 0)
    return down_h, WIN - 1 - lane % WIN


def barrel(value, amount, up):
    for bit in (1, 2, 4, 8):
        moved = pltpu.roll(value, 32 - bit if up else bit, 0)
        value = jnp.where((amount & bit) != 0, moved, value)
    return value


def attend_kernel(q_ref, k_ref, v_ref, rel_ref, out_ref, probs_ref):
    marks = spots()
    marks2 = jnp.concatenate([marks, marks], axis=0)
    shift_h, shift_w = shifts()
    tail_row = lax.broadcasted_iota(jnp.int32, (16, LANES), 0) + (ROWS - 16)
    pad = jnp.zeros((LANES - ROWS, LANES), BF)
    scale = HD ** (-0.5) / math.log(2.0)
    for head in range(GROUP):
        query = q_ref[0, head]
        rel_q = dot_nn(rel_ref[...], query) * (HD**0.5)
        along_h = barrel(rel_q[:32], shift_h, True)[:16]
        along_w = barrel(rel_q[32:], shift_w, True)[:16]
        high, rest = split_low(jnp.concatenate([along_h, along_w], axis=0))
        query_all = jnp.concatenate([query, high, rest], axis=0)
        key_all = jnp.concatenate([k_ref[0, head], marks2], axis=0)
        scores = dot_tn(key_all, query_all)[:ROWS]
        tail = jnp.where(tail_row < WIN * WIN, scores[ROWS - 16 :], -1e30)
        scores = jnp.concatenate([scores[: ROWS - 16], tail], axis=0)
        peak = jnp.max(scores, axis=0, keepdims=True)
        exponent = jnp.exp2((scores - peak) * scale)
        probs = (exponent * (1.0 / jnp.sum(exponent, axis=0, keepdims=True))).astype(BF)
        probs_ref[0, head] = probs
        out_ref[head] = dot_nn(v_ref[0, head], jnp.concatenate([probs, pad], axis=0)).astype(BF)


def attend(qkv, rel_rows):
    slots = qkv.shape[-1] // LANES
    cut = lambda part: pl.BlockSpec((1, GROUP, HD, LANES), lambda s, g, part=part: (part, g, 0, s))
    return pl.pallas_call(
        attend_kernel,
        grid=(slots, HEADS // GROUP),
        in_specs=[cut(0), cut(1), cut(2), pl.BlockSpec((64, HD), lambda s, g: (0, 0))],
        out_specs=[
            pl.BlockSpec((GROUP, HD, LANES), lambda s, g: (g, 0, s)),
            pl.BlockSpec((1, GROUP, ROWS, LANES), lambda s, g: (s, g, 0, 0)),
        ],
        out_shape=[
            jax.ShapeDtypeStruct((HEADS, HD, slots * LANES), BF),
            jax.ShapeDtypeStruct((slots, HEADS, ROWS, LANES), BF),
        ],
        compiler_params=pltpu.CompilerParams(vmem_limit_bytes=16 * 2**20),
        cost_estimate=cheap(slots * HEADS * 2 * LANES * LANES * 256),
        name="attend",
    )(qkv, qkv, qkv, rel_rows)


def attend_back_kernel(q_ref, k_ref, v_ref, g_ref, probs_ref, rel_ref, out_ref, drel_ref):
    marks = spots()
    shift_h, shift_w = shifts()
    pad = jnp.zeros((LANES - ROWS, LANES), BF)
    none = jnp.zeros((16, LANES), F32)
    scale = HD ** (-0.5)
    total = jnp.zeros((64, HD), F32)
    for head in range(GROUP):
        query = q_ref[0, head]
        grad = g_ref[head]
        probs_low = probs_ref[0, head]
        probs = probs_low.astype(F32)
        weighted = dot_tn(v_ref[0, head], grad)[:ROWS] * probs
        flow = jnp.sum(weighted, axis=0, keepdims=True)
        score_low = jnp.concatenate([(weighted - probs * flow).astype(BF), pad], axis=0)
        out_ref[2, head] = dot_nt(grad, jnp.concatenate([probs_low, pad], axis=0)).astype(BF)
        out_ref[1, head] = (dot_nt(query, score_low) * scale).astype(BF)
        mixed = dot_nn(jnp.concatenate([k_ref[0, head], marks], axis=0), score_low)
        rows_h = barrel(jnp.concatenate([mixed[HD : HD + 16], none], axis=0), shift_h, False)
        rows_w = barrel(jnp.concatenate([mixed[HD + 16 :], none], axis=0), shift_w, False)
        both = jnp.concatenate(split_low(jnp.concatenate([rows_h, rows_w], axis=0)), axis=0)
        out_ref[0, head] = (mixed[:HD] * scale + dot_nn(rel_ref[...], both)).astype(BF)
        parts = dot_nt(both, query)
        total = total + parts[:64] + parts[64:]

    @pl.when((pl.program_id(0) == 0) & (pl.program_id(1) == 0))
    def _():
        drel_ref[...] = jnp.zeros_like(drel_ref)

    drel_ref[...] += total


def attend_back(qkv, grad, probs, rel_cols):
    slots = qkv.shape[-1] // LANES
    cut = lambda part: pl.BlockSpec((1, GROUP, HD, LANES), lambda s, g, part=part: (part, g, 0, s))
    return pl.pallas_call(
        attend_back_kernel,
        grid=(slots, HEADS // GROUP),
        in_specs=[
            cut(0),
            cut(1),
            cut(2),
            pl.BlockSpec((GROUP, HD, LANES), lambda s, g: (g, 0, s)),
            pl.BlockSpec((1, GROUP, ROWS, LANES), lambda s, g: (s, g, 0, 0)),
            pl.BlockSpec((HD, 128), lambda s, g: (0, 0)),
        ],
        out_specs=[
            pl.BlockSpec((3, GROUP, HD, LANES), lambda s, g: (0, g, 0, s)),
            pl.BlockSpec((64, HD), lambda s, g: (0, 0)),
        ],
        out_shape=[
            jax.ShapeDtypeStruct((3, HEADS, HD, slots * LANES), BF),
            jax.ShapeDtypeStruct((64, HD), F32),
        ],
        compiler_params=pltpu.CompilerParams(vmem_limit_bytes=20 * 2**20),
        cost_estimate=cheap(slots * HEADS * 5 * LANES * LANES * 256),
        name="attend_back",
    )(qkv, qkv, qkv, grad, probs, rel_cols)


def resident(shape):
    return pl.BlockSpec(shape, lambda *_: (0,) * len(shape))


def cheap(flops):
    return pl.CostEstimate(flops=flops // 8, bytes_accessed=1_000_000, transcendentals=0)


def settings(mebibytes):
    return pltpu.CompilerParams(vmem_limit_bytes=mebibytes * 2**20)


def middle_kernel(att_ref, proj_ref, short_ref, mask_ref, rows_ref, middle_ref, normed_ref):
    branch = dot_tn(att_ref[...], proj_ref[...])[:ROWS] + rows_ref[0:1]
    middle = (short_ref[...].astype(F32) + branch) * mask_ref[...]
    middle_ref[...] = middle
    centred = middle - jnp.mean(middle, axis=1, keepdims=True)
    inverse = lax.rsqrt(jnp.mean(centred * centred, axis=1, keepdims=True) + NORM_EPSILON)
    normed_ref[...] = (centred * inverse * rows_ref[1:2] + rows_ref[2:3]).astype(BF)


def to_middle(attended, proj_full, short, mask, rows):
    slots = attended.shape[1] // LANES
    by_slot = lambda width: pl.BlockSpec((ROWS, width), lambda s: (s, 0))
    return pl.pallas_call(
        middle_kernel,
        grid=(slots,),
        in_specs=[
            pl.BlockSpec((D, LANES), lambda s: (0, s)),
            resident((D, D)),
            by_slot(D),
            by_slot(1),
            resident((8, D)),
        ],
        out_specs=[by_slot(D), by_slot(D)],
        out_shape=[
            jax.ShapeDtypeStruct((slots * ROWS, D), F32),
            jax.ShapeDtypeStruct((slots * ROWS, D), BF),
        ],
        compiler_params=settings(24),
        cost_estimate=cheap(2 * slots * LANES * D * D),
        name="middle",
    )(attended, proj_full, short, mask, rows)


def norm_parts(grad, value, gain):
    centred = value - jnp.mean(value, axis=1, keepdims=True)
    inverse = lax.rsqrt(jnp.mean(centred * centred, axis=1, keepdims=True) + NORM_EPSILON)
    hat = centred * inverse
    scaled = grad * gain
    mean_one = jnp.mean(scaled, axis=1, keepdims=True)
    mean_two = jnp.mean(scaled * hat, axis=1, keepdims=True)
    sums = [jnp.sum(grad * hat, axis=0, keepdims=True), jnp.sum(grad, axis=0, keepdims=True)]
    sums = jnp.concatenate(sums + [jnp.zeros((6, D), F32)], axis=0)
    return inverse * (scaled - mean_one - hat * mean_two), sums


def add_sums(sums_ref, sums):
    @pl.when(pl.program_id(0) == 0)
    def _():
        sums_ref[...] = jnp.zeros_like(sums_ref)

    sums_ref[...] += sums


def second_norm_kernel(grad_ref, came_ref, middle_ref, out_ref, mask_ref, rows_ref, total_ref, pad_ref, sums_ref):
    grad = grad_ref[...] + came_ref[...].astype(F32)
    back, sums = norm_parts(grad, middle_ref[...], rows_ref[1:2])
    total = (out_ref[...].astype(F32) + back) * mask_ref[...]
    total_ref[...] = total
    low = total.astype(BF)
    pad_ref[...] = jnp.concatenate([low, jnp.zeros((LANES - ROWS, D), BF)], axis=0)
    add_sums(sums_ref, sums)


def first_norm_kernel(grad_ref, came_ref, short_ref, total_ref, mask_ref, rows_ref, out_ref, sums_ref):
    mask = mask_ref[...]
    grad = (grad_ref[:ROWS] + came_ref[...].astype(F32)) * mask
    back, sums = norm_parts(grad, short_ref[...].astype(F32), rows_ref[3:4])
    out_ref[0] = ((total_ref[...] + back) * mask)[: WIN * WIN]
    add_sums(sums_ref, sums)


def by_slots(kernel, name, given, outs):
    slots = given[1].shape[0] // ROWS

    def spec(shape):
        if len(shape) == 3:
            return pl.BlockSpec((1,) + shape[1:], lambda s: (s, 0, 0))
        if shape[0] == 8:
            return resident(shape)
        return pl.BlockSpec((shape[0] // slots, shape[1]), lambda s: (s, 0))

    return pl.pallas_call(
        kernel,
        grid=(slots,),
        in_specs=[spec(item.shape) for item in given],
        out_specs=[spec(item.shape) for item in outs],
        out_shape=list(outs),
        compiler_params=settings(32),
        cost_estimate=cheap(1_000_000),
        name=name,
    )(*given)


SIDE = 256
SPOTS = [(row, column) for row in range(D // SIDE) for column in range(row, D // SIDE)]


def upper_blocks(gram):
    parts = [
        gram[row * SIDE : (row + 1) * SIDE, column * SIDE : (column + 1) * SIDE] for row, column in SPOTS
    ]
    return jnp.concatenate(parts, axis=0)


def chain_kernel(count, gram_ref, y_ref, *refs):
    outs, (high_ref, rest_ref, b_ref, t_high, t_rest, z_high, z_rest) = refs[:count], refs[count:]
    columns = [slice(start, start + SIDE) for start in range(0, D, SIDE)]
    row = lax.broadcasted_iota(jnp.int32, (SIDE, SIDE), 0)
    spot = row == lax.broadcasted_iota(jnp.int32, (SIDE, SIDE), 1)
    trace = jnp.zeros((), F32)
    for place, (row, column) in enumerate(SPOTS):
        if row == column:
            trace = trace + jnp.sum(jnp.where(spot, gram_ref[place * SIDE : (place + 1) * SIDE, :], 0.0))
    inverse = 1.0 / (jnp.sqrt(trace) + ORTHO_EPSILON)
    for place, (row, column) in enumerate(SPOTS):
        block = gram_ref[place * SIDE : (place + 1) * SIDE, :] * inverse * inverse
        for part, over, down in ((block, row, column), (block.T, column, row)):
            high, rest = split_low(part)
            high_ref[columns[over], columns[down]] = high
            rest_ref[columns[over], columns[down]] = rest
    z_high[0] = y_ref[...]

    def mirror(ref, values, place):
        cut = columns[place]
        ref[: (place + 1) * SIDE, cut] = values
        for over in range(place):
            ref[cut, columns[over]] = values[columns[over], :].T

    def polynomial():
        for place, cut in enumerate(columns):
            rows = slice(0, (place + 1) * SIDE)
            square = dot_nn(high_ref[rows, :], high_ref[:, cut])
            value = high_ref[rows, cut].astype(F32) + rest_ref[rows, cut].astype(F32)
            poly = COEFF_CUBIC * value + COEFF_QUINTIC * square
            line = lax.broadcasted_iota(jnp.int32, poly.shape, 0) - place * SIDE
            eye = line == lax.broadcasted_iota(jnp.int32, poly.shape, 1)
            mirror(b_ref, (poly + jnp.where(eye, COEFF_LINEAR, 0.0)).astype(BF), place)

    def follow(now, cut, fine):
        value = dot_nn(z_high[now], b_ref[:, cut])
        return value + dot_nn(z_rest[now], b_ref[:, cut]) if fine else value

    def advance(now, fine, z_fine, z_more):
        later = 1 - now
        polynomial()
        for cut in columns:
            value = dot_nn(b_ref[...], high_ref[:, cut])
            if fine:
                value = value + dot_nn(b_ref[...], rest_ref[:, cut])
            t_high[:, cut], rest = split_low(value)
            if fine:
                t_rest[:, cut] = rest
            z_high[later, :, cut], rest = split_low(follow(now, cut, z_fine))
            if z_more:
                z_rest[later, :, cut] = rest
        for place, cut in enumerate(columns):
            rows = slice(0, (place + 1) * SIDE)
            value = dot_nn(t_high[rows, :], b_ref[:, cut])
            if fine:
                value = value + dot_nn(t_rest[rows, :], b_ref[:, cut])
            high, rest = split_low(value)
            mirror(high_ref, high, place)
            mirror(rest_ref, rest, place)

    advance(0, True, False, True)

    @pl.loop(1, ITERS - 2)
    def _(step):
        advance(step % 2, True, True, True)

    advance((ITERS - 2) % 2, False, False, False)
    polynomial()
    for cut in columns:
        value = (follow((ITERS - 1) % 2, cut, False) * inverse).astype(BF)
        for place, out_ref in enumerate(outs):
            rows = out_ref.shape[0]
            out_ref[:, cut] = value[place * rows : (place + 1) * rows]


def chain(gram, rows, count):
    half = pltpu.VMEM((D, D), BF)
    flow = pltpu.VMEM((2,) + rows.shape, BF)
    whole = pl.BlockSpec(memory_space=pltpu.VMEM)
    part = rows.shape[0] // count
    pieces = count if part % 16 == 0 else 1
    out = pl.pallas_call(
        partial(chain_kernel, pieces),
        in_specs=[whole, whole],
        out_specs=[whole] * pieces,
        out_shape=[jax.ShapeDtypeStruct((rows.shape[0] // pieces, D), BF)] * pieces,
        scratch_shapes=[half] * 5 + [flow] * 2,
        compiler_params=settings(56),
        cost_estimate=pl.CostEstimate(flops=18 * 2 * D**3, bytes_accessed=6 * D * D, transcendentals=0),
        name="chain",
    )(gram, rows)
    return out if pieces == count else [out[0][at * part : (at + 1) * part] for at in range(count)]


EVERY = ("ga", "gb", "gc", "gy")


def peer(value):
    return lax.ppermute(value, "gc", [(0, 1), (1, 0)])


def steps_of(axis):
    return lax.axis_size(axis).bit_length() - 1


def first_stages():
    return [("f", step) for step in reversed(range(steps_of("ga")))]


def second_stages():
    return [("s", step) for step in reversed(range(steps_of("gb")))]


def plane_stages():
    return [("z", step) for step in range(steps_of("gy"))]


def gather_groups():
    deep = plane_stages()
    return [deep[1:][::-1], deep[:1]], [second_stages()[::-1]], [first_stages()[::-1]]


def reduce_groups():
    deep = plane_stages()
    return [first_stages()], [second_stages()], [deep[:1], deep[1:]]


def half_stages():
    return first_stages() + second_stages() + plane_stages()


def bit_of(stage, core):
    kind, step = stage
    if kind == "z":
        return "gy", steps_of("gy") - 1 - step if core == 0 else step
    return ("ga" if (kind == "f") == (core == 0) else "gb"), step


def my_bit(stage):
    values = []
    for core in range(2):
        axis, step = bit_of(stage, core)
        values.append((lax.axis_index(axis) >> step) & 1)
    return jnp.where(lax.axis_index("gc") == 0, values[0], values[1])


def swap(value, stage):
    if stage == "c":
        return peer(value)
    sizes = [lax.axis_size(axis) for axis in EVERY]
    pairs = []
    for place in range(math.prod(sizes)):
        spot, rest = [], place
        for size in reversed(sizes):
            spot.insert(0, rest % size)
            rest //= size
        axis, step = bit_of(stage, spot[2])
        spot[EVERY.index(axis)] ^= 1 << step
        other = 0
        for size, at in zip(sizes, spot):
            other = other * size + at
        pairs.append((place, other))
    return lax.ppermute(value, EVERY, pairs)


class Rounds:
    def __init__(self):
        self.last = None

    def go(self, chains, work=None, *values):
        chains = [chain for chain in chains if not chain.done]
        while long := [chain for chain in chains if chain.left > 1]:
            self.once(long)
        out = self.once(chains, work, *values)
        for chain in chains:
            chain.left = chain.counts.pop(0) if chain.counts else 0
        return out

    def once(self, chains, work=None, *values):
        marks = [] if self.last is None else [self.last]
        held = []
        for chain in chains:
            chain.wait_for(held[-1:])
            chain.look()
            held.append(lax.optimization_barrier((chain.value, *marks))[0])
        came = [swap(value, chain.stage) for value, chain in zip(held, chains)]
        ready = lax.optimization_barrier((*values, *held, *marks))
        out = () if work is None else work(*ready[: len(values)])
        leaves, tree = jax.tree.flatten(out)
        ended = lax.optimization_barrier(tuple(came) + tuple(leaves))
        self.last = ended[0]
        for chain, value in zip(chains, ended):
            chain.take(value)
            chain.left -= 1
        return jax.tree.unflatten(tree, ended[len(chains) :])


class Chain:
    def __init__(self, work, groups):
        self.work, self.result = work, None
        self.steps = sum(len(group) for group in groups)
        self.pending = [None]
        self.counts = [len(group) for group in groups if group]
        self.left = self.counts.pop(0)

    def take(self, came):
        self.pending = [came]
        self.steps -= 1

    def look(self):
        if self.pending:
            try:
                self.value, self.stage = self.work.send(self.pending.pop())
            except StopIteration as stop:
                self.result = stop.value

    def wait_for(self, others):
        if others and self.pending and self.pending[0] is not None:
            self.pending = [lax.optimization_barrier((self.pending[0], *others))[0]]

    @property
    def done(self):
        return self.steps == 0

    @property
    def out(self):
        self.look()
        return self.result


def gather_half(shard):
    groups = sum(gather_groups(), [])

    def work():
        held = shard[None]
        for stage in sum(groups, []):
            came = yield held, stage
            first = my_bit(stage) == 0
            held = jnp.concatenate([jnp.where(first, held, came), jnp.where(first, came, held)], axis=0)
        return held.reshape(-1, shard.shape[-1])

    return Chain(work(), groups)


def gather_relative(shard, groups):
    def work():
        order, canon = sum(groups, []), half_stages()
        held = shard
        for stage in order[:-1]:
            came = yield held, stage
            held = jnp.stack([held, came])
        came = yield held, order[-1]
        there = order[-2::-1]
        turn = [there.index(stage) for stage in canon[1:]] + [len(there), len(there) + 1]
        return tuple(half.transpose(turn).reshape(-1, shard.shape[-1]) for half in (held, came))

    return Chain(work(), groups)


def relative(value):
    stages = half_stages()
    place = sum(my_bit(stage) << (len(stages) - 1 - at) for at, stage in enumerate(stages))
    spots = jnp.arange(value.shape[0])
    picker = ((spots[:, None] ^ place) == spots[None, :]).astype(F32)
    return jnp.dot(picker, value, precision=lax.Precision.HIGHEST, preferred_element_type=F32)


def reduce_half(grad, groups, kind=BF):
    def work():
        live = half_stages()
        parts = [grad.reshape((2,) * len(live) + (-1, grad.shape[-1]))]
        for stage in sum(groups, []):
            place, mine = live.index(stage), my_bit(stage)
            live.remove(stage)

            def pick(which):
                cuts = [lax.dynamic_index_in_dim(part, which, place, False) for part in parts]
                return cuts[0] if len(cuts) == 1 else (cuts[0].astype(F32) + cuts[1].astype(F32)).astype(kind)

            send = pick(1 - mine)
            parts = list(lax.optimization_barrier((*parts, send))[:-1])
            keep = pick(mine)
            came = yield send, stage
            parts = [keep, came]
        return parts[0].astype(F32) + parts[1].astype(F32)

    return Chain(work(), groups)


def reduce_relative(keep, send, groups):
    def work():
        live, order = half_stages(), sum(groups, [])
        came = yield send, order[0]
        assert order[0] == live[0]
        live.remove(order[0])
        shape = (2,) * len(live) + (-1, send.shape[-1])
        parts = [keep().reshape(shape), came.reshape(shape)]
        for stage in order[1:]:
            place = live.index(stage)
            live.remove(stage)

            def pick(which):
                cuts = [lax.index_in_dim(part, which, place, False).astype(F32) for part in parts]
                return (cuts[0] + cuts[1]).astype(BF)

            away = pick(1)
            parts = list(lax.optimization_barrier((*parts, away))[:-1])
            kept = pick(0)
            came = yield away, stage
            parts = [kept, came]
        return parts[0].astype(F32) + parts[1].astype(F32)

    return Chain(work(), groups)


def turned(value):
    stages = half_stages()
    shape = value.shape
    value = value.reshape((2,) * len(stages) + shape[1:])
    side, deep = len(first_stages()), len(plane_stages())
    order = list(range(side, 2 * side)) + list(range(side)) + list(reversed(range(2 * side, 2 * side + deep)))
    order += list(range(2 * side + deep, value.ndim))
    return value.transpose(order).reshape(shape)


def join_halves(mine, theirs):
    chips = 1 << len(half_stages())
    planes = lax.axis_size("gy")
    first = lax.axis_index("gc") == 0
    shape = (chips, -1) + mine.shape[1:]
    mine, theirs = mine.reshape(shape), theirs.reshape(shape)
    both = [jnp.where(first, mine, theirs), turned(jnp.where(first, theirs, mine))]
    both = [half.reshape((chips // planes, planes) + half.shape[1:]) for half in both]
    return jnp.stack(both, axis=1).reshape((-1,) + mine.shape[2:])


def cut_half(value, which):
    chips = 1 << len(half_stages())
    planes = lax.axis_size("gy")
    shape = value.shape
    value = value.reshape((chips // planes, 2, planes, -1) + shape[1:])
    halves = [value[:, core].reshape((chips, -1) + shape[1:]) for core in range(2)]
    return jnp.where(which == 0, halves[0], turned(halves[1])).reshape((-1,) + shape[1:])


def sum_rows(value, stages):
    def work():
        held = value
        for stage in stages:
            halves = held.reshape((2, held.shape[0] // 2) + held.shape[1:])
            mine = my_bit(stage)
            keep = lax.dynamic_index_in_dim(halves, mine, 0, False)
            came = yield lax.dynamic_index_in_dim(halves, 1 - mine, 0, False), stage
            held = keep + came
        return held

    return Chain(work(), [[stage] for stage in stages])


def spread_rows(value, stages):
    def work():
        held = value
        for stage in stages:
            came = yield held, stage
            first = my_bit(stage) == 0
            held = jnp.concatenate([jnp.where(first, held, came), jnp.where(first, came, held)], axis=0)
        return held

    return Chain(work(), [[stage] for stage in stages])


def plane_sum(rounds, value, work, *values):
    core = lax.axis_index("gc")
    halves = value.reshape((2, value.shape[0] // 2) + value.shape[1:])

    def over_cores(mine, theirs):
        return mine + peer(theirs)

    held = rounds.go(
        [],
        over_cores,
        lax.dynamic_index_in_dim(halves, core, 0, False),
        lax.dynamic_index_in_dim(halves, 1 - core, 0, False),
    )
    stages = first_stages() + second_stages()
    chain = sum_rows(held, stages)
    out = rounds.go([chain], work, *values)
    while not chain.done:
        rounds.go([chain])
    chain = spread_rows(chain.out, stages[::-1])
    while not chain.done:
        rounds.go([chain])
    held = chain.out
    came = rounds.go([], peer, held)
    held = [jnp.where(core == 0, held, came), jnp.where(core == 0, came, held)]
    return jnp.concatenate(held, axis=0), out


def sum_whole(value, stages):
    def work():
        held = value
        for stage in stages:
            came = yield held, stage
            held = held + came
        return held

    return Chain(work(), [[stage] for stage in stages])


def token_mask(placement, counts):
    slot_count = placement.shape[0]
    live = (jnp.arange(slot_count, dtype=jnp.int32) < counts[0]).astype(F32)
    inner = jnp.arange(WIN * WIN, dtype=jnp.int32)
    row_pos = placement[:, 0:1] * WIN + inner[None, :] // WIN
    col_pos = placement[:, 1:2] * WIN + inner[None, :] % WIN
    inside = ((row_pos < GRID) & (col_pos < GRID)).astype(F32)
    return inside * live[:, None]


def normalised(value):
    centred = value - jnp.mean(value, axis=-1, keepdims=True)
    inverse = lax.rsqrt(jnp.mean(centred * centred, axis=-1, keepdims=True) + NORM_EPSILON)
    return centred * inverse, inverse


def norm_back(grad, hat, inverse, gain):
    scaled = grad * gain
    mean_one = jnp.mean(scaled, axis=-1, keepdims=True)
    mean_two = jnp.mean(scaled * hat, axis=-1, keepdims=True)
    return inverse * (scaled - mean_one - hat * mean_two)


def pad_slots(value, rows):
    slots, given, width = value.shape
    return jnp.pad(value, ((0, 0), (0, rows - given), (0, 0))).reshape(slots * rows, width)


def widen_slots(value):
    return pad_slots(value.reshape(-1, ROWS, value.shape[1]), LANES)


def narrow_slots(value):
    return value.reshape(-1, LANES, value.shape[1])[:, :ROWS].reshape(-1, value.shape[1])


def body(
    windows,
    cotangent,
    placement,
    counts,
    qkv_weight,
    proj_weight,
    up_weight,
    down_weight,
    qkv_moment,
    proj_moment,
    up_moment,
    down_moment,
    vectors,
    vector_moment,
    rel_pos,
    rel_moment,
):
    core = lax.axis_index("gc")
    planes = lax.axis_size("gy")
    chips = 1 << len(half_stages())
    devices = 2 * chips
    slots, tokens, _ = windows.shape
    wide = slots * LANES
    first, second, deep = first_stages(), second_stages(), plane_stages()
    rounds = Rounds()

    def block(work, *values):
        shapes = jax.eval_shape(work, *values)

        def idle(*_):
            return jax.tree.map(lambda item: jnp.zeros(item.shape, item.dtype), shapes)

        return lax.cond(counts[0] > 0, work, idle, *values)

    mask = pad_slots(token_mask(placement, counts)[:, :, None], ROWS)
    short_low = pad_slots(windows, ROWS) * mask.astype(BF)
    out_low = pad_slots(cotangent, ROWS) * mask.astype(BF)
    count = short_low.shape[0]
    by_z, by_second, by_first = gather_groups()
    part, spare = qkv_weight.shape[1], vectors.shape[0]
    vec_rows = jnp.pad(vectors.astype(BF)[None], ((0, 7), (0, D - spare)))
    take_qkv = gather_half(jnp.concatenate([qkv_weight.astype(BF).T, vec_rows], axis=0))
    take_proj = gather_half(proj_weight.astype(BF))
    take_up = gather_relative(up_weight.astype(BF).T, by_z + by_second + by_first)
    take_down = gather_relative(down_weight.astype(BF), by_second + by_z + by_first)

    mask_row = jnp.pad(mask.astype(BF).T, ((0, 7), (0, D - count)))
    rounds.go([take_qkv, take_down])
    short_peer = rounds.go([take_qkv, take_proj], peer, jnp.concatenate([short_low, mask_row], axis=0))
    rounds.go([take_qkv, take_up, take_proj])

    def first_hats(mine, theirs):
        return normalised(mine.astype(F32))[0], normalised(theirs[:count].astype(F32))[0]

    (hat_mine, hat_peer), out_peer = rounds.go(
        [take_qkv, take_up, take_proj],
        lambda one, two, three: (block(first_hats, one, two), peer(three)),
        short_low,
        short_peer,
        out_low,
    )
    qkv_half = take_qkv.out
    wide_part = part + 8

    def slim(value):
        return value.reshape((chips, wide_part) + value.shape[1:])[:, :part].reshape((-1,) + value.shape[1:])

    def stout(value):
        value = value.reshape((chips, part) + value.shape[1:])
        return jnp.pad(value, ((0, 0), (0, 8)) + ((0, 0),) * (value.ndim - 2)).reshape((-1,) + value.shape[2:])

    def to_qkv(qkv_half, hat, vec, live, bias):
        rows = widen_slots(((hat * vec[:D] + vec[D : 2 * D]) * live).astype(BF))
        return with_layout_constraint((dot_nt(qkv_half, rows) + bias).astype(BF), Layout((0, 1))), rows

    def both_qkv(qkv_half, hat_mine, hat_peer, short_peer, mask):
        vec_half = qkv_half.reshape(chips, wide_part, D)[:, part, :spare]
        vec = join_halves(vec_half, peer(vec_half)).reshape(-1).astype(F32)
        bias_qkv = jnp.concatenate([vec[2 * D : 3 * D], jnp.zeros((D,), F32), vec[3 * D : 4 * D]])
        bias_qkv = stout(cut_half(bias_qkv, core))[:, None]
        live = short_peer[count, :count].astype(F32)[:, None]
        theirs, pad_peer = block(to_qkv, qkv_half, hat_peer, vec, live, bias_qkv)
        came = tuple(peer(piece) for piece in jnp.split(theirs, 4, axis=0))
        mine, pad_mine = block(to_qkv, qkv_half, hat_mine, vec, mask, bias_qkv)
        return mine, came, vec, pad_mine, pad_peer

    qkv_mine, qkv_came, vec, pad_mine, pad_peer = rounds.go(
        [take_up, take_proj, take_down], both_qkv, qkv_half, hat_mine, hat_peer, short_peer, mask
    )
    proj_half = take_proj.out
    bias_down = vec[7 * D : 8 * D]
    rel_low = rel_pos.astype(BF)[:, ::-1]
    rel_rows = jnp.pad(rel_low, ((0, 0), (0, 5), (0, 0))).reshape(64, HD)
    rel_cols = jnp.concatenate([rel_rows, rel_rows], axis=0).T

    def to_attended(mine, came, proj_half, out_low, out_peer, vec):
        proj_came = peer(proj_half)
        qkv = join_halves(slim(mine), slim(jnp.concatenate(came, axis=0))).reshape(3, HEADS, HD, wide)
        attended, probs = attend(qkv, rel_rows)
        out_both = jnp.concatenate([out_low, out_peer], axis=0)
        bias_up = relative(cut_half(vec[8 * D :], core).reshape(chips, -1)).reshape(1, -1)
        table = vec[: 8 * D].reshape(8, D)
        middle_rows = jnp.concatenate([table[4:7], table[:1], table[:4]], axis=0)
        return join_halves(proj_half, proj_came), out_both, qkv, attended, probs, bias_up, middle_rows

    proj_full, out_both, qkv, attended, probs, bias_up, middle_rows = rounds.go(
        [take_up, take_down], to_attended, qkv_mine, qkv_came, proj_half, out_low, out_peer, vec
    )
    attended = attended.reshape(D, wide)
    up_halves = take_up.out
    width = up_halves[0].shape[0]

    def to_gelu(mine, came, up_full, out_both):
        both = jnp.concatenate([mine, came], axis=0)
        pre = dot_nt(both, up_full) + bias_up
        bell = jnp.exp(-0.5 * pre * pre)
        below = 0.5 * (1.0 + lax.erf(pre * (0.5**0.5)))
        gelu = (pre * below).astype(BF)
        slope = (below + pre * bell * (2.0 * math.pi) ** -0.5).astype(BF)
        send = dot_tn(gelu[:, width:], out_both).astype(BF)
        return both, gelu, slope, dot_tn(gelu[:, :width], out_both).astype(BF), send

    def to_hidden(attended, up_one, up_two):
        middle, normed = to_middle(attended, proj_full, short_low, mask, middle_rows)
        came = peer(normed)
        up_full = jnp.concatenate([up_one, up_two], axis=0)
        return middle, up_full, *to_gelu(normed, came, up_full, out_both)

    middle, up_full, normed_both, gelu_both, slope, keep_down, send_down = rounds.go(
        [take_down], to_hidden, attended, *up_halves
    )
    down_halves = take_down.out

    by_first, by_second, by_z = reduce_groups()
    mixed_order = by_first + by_z + by_second
    plane_last = by_first + by_second + by_z
    give_down = reduce_relative(lambda: keep_down, send_down, mixed_order)

    def to_pre(down_one, down_two, out_both, slope, up_full):
        down_full = jnp.concatenate([down_one, down_two], axis=0)
        pre = (dot_nt(out_both, down_full) * slope.astype(F32)).astype(BF)
        return down_full, pre, dot_nn(pre[count:], up_full).astype(BF)

    def second_mine(pre, up_full):
        return dot_nn(pre[:count], up_full)

    def up_back(pre, normed_both):
        send = dot_tn(pre[:, width:], normed_both).astype(BF)
        return send, jnp.sum(pre, axis=0, dtype=F32)

    def to_branch(down_one, down_two, out_both, slope, up_full, normed_both, middle):
        down_full, pre, theirs = to_pre(down_one, down_two, out_both, slope, up_full)
        came = peer(theirs)
        send_up, up_bias = block(up_back, pre, normed_both)
        given = (second_mine(pre, up_full), came, middle, out_low, mask, middle_rows)
        shapes = (((count, D), F32), ((wide, D), BF), ((8, D), F32))
        outs = [jax.ShapeDtypeStruct(*shape) for shape in shapes]
        return down_full, pre, send_up, up_bias, *by_slots(second_norm_kernel, "second_norm", given, outs)

    down_full, pre, send_up, up_bias, grad_total, branch_pad, second_sums = rounds.go(
        [give_down], to_branch, *down_halves, out_both, slope, up_full, normed_both, middle
    )
    kept = {"up": lambda: dot_tn(pre[:, :width], normed_both).astype(BF)}
    give_up = reduce_relative(lambda: kept["up"](), send_up, plane_last)

    def attention_back(branch_pad, attended, pre, normed_both):
        keep_up = dot_tn(pre[:, :width], normed_both).astype(BF)
        grad_proj = dot_nn(attended, branch_pad).astype(BF)
        proj_came = peer(cut_half(grad_proj, 1 - core))
        grad_att = dot_nt(proj_full, branch_pad).astype(BF).reshape(HEADS, HD, wide)
        grad_qkv, grad_rel = attend_back(qkv, grad_att, probs, rel_cols)
        grad_qkv = grad_qkv.reshape(3 * D, wide)
        grad_proj = (cut_half(grad_proj, core).astype(F32) + proj_came.astype(F32)).astype(BF)
        halves = [stout(cut_half(grad_qkv, which)) for which in (core, 1 - core)]
        return grad_qkv, grad_rel, *halves, grad_proj, keep_up

    grad_qkv, grad_rel, qkv_grad_mine, qkv_grad_theirs, grad_proj, keep_up = rounds.go(
        [give_up, give_down], attention_back, branch_pad, attended, pre, normed_both
    )
    kept["up"] = lambda: keep_up
    give_proj = reduce_half(grad_proj, plane_last)
    normed_pad = jnp.concatenate([pad_mine, pad_peer], axis=0)

    def qkv_back(mine, came, normed_pad):
        both = jnp.concatenate([mine, came], axis=1)
        return both, dot_nn(both, normed_pad).astype(BF)

    def to_qkv_grad(mine, theirs, normed_pad):
        return qkv_back(mine, peer(theirs), normed_pad)

    qkv_grad_both, grad_qkv_half = rounds.go(
        [give_up, give_down, give_proj], to_qkv_grad, qkv_grad_mine, qkv_grad_theirs, normed_pad
    )
    give_qkv = reduce_half(grad_qkv_half, plane_last)

    def first_theirs(both, weight):
        return narrow_slots(dot_tn(both[:, wide:], weight).astype(BF))

    def first_mine(both, weight):
        return dot_tn(both[:, :wide], weight)

    def mlp_theirs(gelu_both, down_full):
        return dot_nn(gelu_both[count:], down_full).astype(BF)

    def mlp_mine(gelu_both, down_full, came, middle):
        mlp_out = dot_nn(gelu_both[:count], down_full) + came.astype(F32) + bias_down
        return ((middle + mlp_out) * mask).astype(BF).reshape(slots, ROWS, D)[:, :tokens]

    def to_small(grad_qkv, branch_pad, second_sums, out_low, up_bias, grad_rel):
        up_bias = relative(up_bias.reshape(chips, -1))
        up_bias = [jnp.where(core == 0, up_bias, 0.0), turned(jnp.where(core == 0, 0.0, up_bias))]
        up_bias = jnp.stack(up_bias, axis=1).reshape(chips // planes, planes, 2, -1)
        up_bias = jnp.swapaxes(up_bias, 1, 2).reshape(-1, D)
        qkv_bias = jnp.sum(grad_qkv, axis=1, dtype=F32).reshape(3, D)
        rows = [
            jnp.zeros((2, D), F32),
            qkv_bias[:1],
            qkv_bias[2:],
            jnp.sum(branch_pad, axis=0, dtype=F32, keepdims=True),
            second_sums[:2],
            jnp.sum(out_low, axis=0, dtype=F32, keepdims=True),
            up_bias,
        ]
        rows = jnp.concatenate(rows).reshape(-1, SIDE), grad_rel.reshape(-1, SIDE)
        return jnp.concatenate(rows)

    def for_peer(both, weight, gelu_both, down_full, *values):
        ours = block(first_theirs, both, weight), block(mlp_theirs, gelu_both, down_full)
        return *ours, to_small(*values)

    first_sent, mlp_sent, small_early = rounds.go(
        [give_qkv, give_up, give_down, give_proj],
        for_peer,
        qkv_grad_both,
        qkv_half,
        gelu_both,
        down_full,
        grad_qkv,
        branch_pad,
        second_sums,
        out_low,
        up_bias,
        grad_rel,
    )

    stride = max(planes // 4, 1)
    homes = {"qkv": 0, "down": stride, "up": 2 * stride, "proj": 3 * stride}
    me_z = lax.axis_index("gy")
    room = max(up_weight.shape[1], down_weight.shape[0], part, proj_weight.shape[0])
    pieces = [[] for _ in range(planes)]

    def home(**lows):
        parts = []
        for far in range(planes):
            value = sum(
                jnp.where((me_z ^ far) == homes[name], low, jnp.zeros_like(low)) for name, low in lows.items()
            )
            if far:
                value = lax.ppermute(value, "gy", [(homes[name] ^ far, homes[name]) for name in lows])
            parts.append(value)
        return parts

    def arrive(parts):
        for row, piece in zip(pieces, parts):
            row.append(jnp.pad(piece, ((0, room - piece.shape[0]), (0, 0))))

    def moment(old, grad, flip):
        new = MOMENT_MATRIX * old + (grad.T if flip else grad)
        return new, (new.T if flip else new).astype(BF)

    first_came, mlp_came = rounds.go(
        [give_qkv, give_up, give_proj], lambda one, two: (peer(one), peer(two)), first_sent, mlp_sent
    )
    new_down, low_down = moment(down_moment, give_down.out, False)
    new_up, low_up = moment(up_moment, give_up.out, True)

    def to_ends(low_down, low_up, both, weight, first_came, grad_total, short_low):
        arrived = home(down=low_down, up=low_up)
        given = (block(first_mine, both, weight), first_came, short_low, grad_total, mask, middle_rows)
        outs = [jax.ShapeDtypeStruct((slots, tokens, D), F32), jax.ShapeDtypeStruct((8, D), F32)]
        return arrived, *by_slots(first_norm_kernel, "first_norm", given, outs)

    arrived, grad_input, first_sums = rounds.go(
        [give_qkv, give_proj],
        to_ends,
        low_down,
        low_up,
        qkv_grad_both,
        qkv_half,
        first_came,
        grad_total,
        short_low,
    )
    arrive(arrived)
    new_proj, low_proj = moment(proj_moment, give_proj.out, False)

    arrive(rounds.go([give_qkv, give_proj], lambda value: home(proj=value), low_proj))
    while not give_qkv.done:
        rounds.go([give_qkv])
    new_qkv, low_qkv = moment(qkv_moment, give_qkv.out[:part], True)
    arrive(rounds.go([], lambda value: home(qkv=value), low_qkv))
    held = jnp.concatenate([sum(row[1:], row[0]) for row in pieces], axis=0)
    first_rows = jnp.pad(first_sums[:2].reshape(-1, SIDE), ((0, small_early.shape[0] - 2 * D // SIDE), (0, 0)))
    small = small_early + first_rows
    blocks = upper_blocks(dot_tn(held, held))
    fill = -small.shape[0] % (8 * devices // planes)
    summed, block_out = plane_sum(
        rounds,
        jnp.concatenate([blocks, jnp.pad(small, ((0, fill), (0, 0)))], axis=0),
        lambda *values: block(mlp_mine, *values),
        gelu_both,
        down_full,
        mlp_came,
        middle,
    )
    gram = summed[: blocks.shape[0]]
    add_small = sum_whole(summed[blocks.shape[0] : blocks.shape[0] + small.shape[0]], deep)

    def send_back(ortho):
        back = [ortho[0]]
        for far in range(1, planes):
            back.append(lax.ppermute(ortho[far], "gy", [(place, place ^ far) for place in range(planes)]))
        return jnp.stack(back)

    ortho = rounds.go([add_small], lambda *pair: chain(*pair, planes), gram, held)
    back = rounds.go([add_small], lambda *parts: send_back(parts), *ortho)
    while not add_small.done:
        rounds.go([add_small])
    small = add_small.out.reshape(-1)
    rel_total = small[devices * spare :].reshape(2, 32, HD)
    vec_total = lax.dynamic_slice_in_dim(small, lax.axis_index(EVERY) * spare, spare)

    def part_of(name, rows):
        return lax.dynamic_index_in_dim(back, me_z ^ homes[name], 0, False)[:rows].astype(F32)

    parts = [
        part_of("qkv", qkv_weight.shape[1]),
        part_of("proj", proj_weight.shape[0]),
        part_of("up", up_weight.shape[1]),
        part_of("down", down_weight.shape[0]),
    ]

    scales = (math.sqrt(3.0), 1.0, math.sqrt(max(1.0, FF / D)), math.sqrt(max(1.0, D / FF)))
    masters = (qkv_weight, proj_weight, up_weight, down_weight)
    flipped = (True, False, True, False)
    new_weights = [
        master - RATE_MATRIX * factor * (part.T if turn else part)
        for master, factor, part, turn in zip(masters, scales, parts, flipped)
    ]

    rate_vec = 0.5 / math.sqrt(float(devices * slots * tokens))
    vec_moment_new = MOMENT_VECTOR * vector_moment + vec_total
    rel_grad = rel_total[:, : 2 * WIN - 1][:, ::-1]
    rel_moment_new = MOMENT_VECTOR * rel_moment + rel_grad
    return (
        block_out,
        grad_input,
        new_qkv,
        new_proj,
        new_up,
        new_down,
        new_weights[0],
        new_weights[1],
        new_weights[2],
        new_weights[3],
        vec_moment_new,
        vectors - rate_vec * vec_moment_new,
        rel_moment_new,
        rel_pos - 0.2 * rate_vec * rel_moment_new,
    )


def solution(mesh):
    size_x, size_y = mesh.shape["gx"], mesh.shape["gy"]
    side = math.isqrt(size_x // 2)
    assert side * side * 2 == size_x
    grid = (side, size_x // 2 // side, 2, size_y)
    split = Mesh(mesh.devices.reshape(grid), ("ga", "gb", "gc", "gy"))
    flat = ("ga", "gb", "gc", "gy")
    slab, cols, rows, line = P(flat, None, None), P(None, flat), P(flat, None), P(flat)
    return jax.shard_map(
        body,
        mesh=split,
        in_specs=(
            (slab, slab, rows, line) + (cols, rows, cols, rows) * 2 + (line, line, P(), P())
        ),
        out_specs=(
            (slab, slab) + (cols, rows, cols, rows) * 2 + (line, line, P(), P())
        ),
        check_vma=False,
    )
```

```python
from functools import partial
import math

import jax
import jax.numpy as jnp
from jax import lax
from jax.experimental import pallas as pl
from jax.experimental.pallas import tpu as pltpu
from jax.experimental.layout import Layout, with_layout_constraint
from jax.sharding import Mesh, PartitionSpec as P

D = 1280
FF = 5120
HEADS = 16
HD = 80
WIN = 14
GRID = 64
ITERS = 5
LANES = 256
ROWS = 208

NORM_EPSILON = 1e-06
ORTHO_EPSILON = 1e-07
COEFF_LINEAR = 3.4445
COEFF_CUBIC = -4.775
COEFF_QUINTIC = 2.0315
MOMENT_MATRIX = 0.95
MOMENT_VECTOR = 0.9
RATE_MATRIX = 0.5

BF = jnp.bfloat16
F32 = jnp.float32


def dot_nn(left, right):
    return jnp.dot(left, right, preferred_element_type=F32)


def dot_tn(left, right):
    return lax.dot_general(left, right, (((0,), (0,)), ((), ())), preferred_element_type=F32)


def dot_nt(left, right):
    return lax.dot_general(left, right, (((1,), (1,)), ((), ())), preferred_element_type=F32)


def split_low(value):
    high = value.astype(BF)
    return high, (value - high.astype(F32)).astype(BF)


GROUP = 8


def spots():
    row = lax.broadcasted_iota(jnp.int32, (32, LANES), 0)
    lane = lax.broadcasted_iota(jnp.int32, (32, LANES), 1)
    along = jnp.where(row < 16, lane // WIN, lane % WIN + 16)
    return jnp.where((along == row) & (lane < WIN * WIN), 1.0, 0.0).astype(BF)


def shifts():
    lane = lax.broadcasted_iota(jnp.int32, (32, LANES), 1)
    down_h = jnp.maximum(WIN - 1 - lane // WIN, 0)
    return down_h, WIN - 1 - lane % WIN


def barrel(value, amount, up):
    for bit in (1, 2, 4, 8):
        moved = pltpu.roll(value, 32 - bit if up else bit, 0)
        value = jnp.where((amount & bit) != 0, moved, value)
    return value


def attend_kernel(q_ref, k_ref, v_ref, rel_ref, out_ref, probs_ref):
    marks = spots()
    marks2 = jnp.concatenate([marks, marks], axis=0)
    shift_h, shift_w = shifts()
    tail_row = lax.broadcasted_iota(jnp.int32, (16, LANES), 0) + (ROWS - 16)
    pad = jnp.zeros((LANES - ROWS, LANES), BF)
    scale = HD ** (-0.5) / math.log(2.0)
    for head in range(GROUP):
        query = q_ref[0, head]
        rel_q = dot_nn(rel_ref[...], query) * (HD**0.5)
        along_h = barrel(rel_q[:32], shift_h, True)[:16]
        along_w = barrel(rel_q[32:], shift_w, True)[:16]
        high, rest = split_low(jnp.concatenate([along_h, along_w], axis=0))
        query_all = jnp.concatenate([query, high, rest], axis=0)
        key_all = jnp.concatenate([k_ref[0, head], marks2], axis=0)
        scores = dot_tn(key_all, query_all)[:ROWS]
        tail = jnp.where(tail_row < WIN * WIN, scores[ROWS - 16 :], -1e30)
        scores = jnp.concatenate([scores[: ROWS - 16], tail], axis=0)
        peak = jnp.max(scores, axis=0, keepdims=True)
        exponent = jnp.exp2((scores - peak) * scale)
        probs = (exponent * (1.0 / jnp.sum(exponent, axis=0, keepdims=True))).astype(BF)
        probs_ref[0, head] = probs
        out_ref[head] = dot_nn(v_ref[0, head], jnp.concatenate([probs, pad], axis=0)).astype(BF)


def attend(qkv, rel_rows):
    slots = qkv.shape[-1] // LANES
    cut = lambda part: pl.BlockSpec((1, GROUP, HD, LANES), lambda s, g, part=part: (part, g, 0, s))
    return pl.pallas_call(
        attend_kernel,
        grid=(slots, HEADS // GROUP),
        in_specs=[cut(0), cut(1), cut(2), pl.BlockSpec((64, HD), lambda s, g: (0, 0))],
        out_specs=[
            pl.BlockSpec((GROUP, HD, LANES), lambda s, g: (g, 0, s)),
            pl.BlockSpec((1, GROUP, ROWS, LANES), lambda s, g: (s, g, 0, 0)),
        ],
        out_shape=[
            jax.ShapeDtypeStruct((HEADS, HD, slots * LANES), BF),
            jax.ShapeDtypeStruct((slots, HEADS, ROWS, LANES), BF),
        ],
        compiler_params=pltpu.CompilerParams(vmem_limit_bytes=16 * 2**20),
        cost_estimate=cheap(slots * HEADS * 2 * LANES * LANES * 256),
        name="attend",
    )(qkv, qkv, qkv, rel_rows)


def attend_back_kernel(q_ref, k_ref, v_ref, g_ref, probs_ref, rel_ref, out_ref, drel_ref):
    marks = spots()
    shift_h, shift_w = shifts()
    pad = jnp.zeros((LANES - ROWS, LANES), BF)
    none = jnp.zeros((16, LANES), F32)
    scale = HD ** (-0.5)
    total = jnp.zeros((64, HD), F32)
    for head in range(GROUP):
        query = q_ref[0, head]
        grad = g_ref[head]
        probs_low = probs_ref[0, head]
        probs = probs_low.astype(F32)
        weighted = dot_tn(v_ref[0, head], grad)[:ROWS] * probs
        flow = jnp.sum(weighted, axis=0, keepdims=True)
        score_low = jnp.concatenate([(weighted - probs * flow).astype(BF), pad], axis=0)
        out_ref[2, head] = dot_nt(grad, jnp.concatenate([probs_low, pad], axis=0)).astype(BF)
        out_ref[1, head] = (dot_nt(query, score_low) * scale).astype(BF)
        mixed = dot_nn(jnp.concatenate([k_ref[0, head], marks], axis=0), score_low)
        rows_h = barrel(jnp.concatenate([mixed[HD : HD + 16], none], axis=0), shift_h, False)
        rows_w = barrel(jnp.concatenate([mixed[HD + 16 :], none], axis=0), shift_w, False)
        both = jnp.concatenate(split_low(jnp.concatenate([rows_h, rows_w], axis=0)), axis=0)
        out_ref[0, head] = (mixed[:HD] * scale + dot_nn(rel_ref[...], both)).astype(BF)
        parts = dot_nt(both, query)
        total = total + parts[:64] + parts[64:]

    @pl.when((pl.program_id(0) == 0) & (pl.program_id(1) == 0))
    def _():
        drel_ref[...] = jnp.zeros_like(drel_ref)

    drel_ref[...] += total


def attend_back(qkv, grad, probs, rel_cols):
    slots = qkv.shape[-1] // LANES
    cut = lambda part: pl.BlockSpec((1, GROUP, HD, LANES), lambda s, g, part=part: (part, g, 0, s))
    return pl.pallas_call(
        attend_back_kernel,
        grid=(slots, HEADS // GROUP),
        in_specs=[
            cut(0),
            cut(1),
            cut(2),
            pl.BlockSpec((GROUP, HD, LANES), lambda s, g: (g, 0, s)),
            pl.BlockSpec((1, GROUP, ROWS, LANES), lambda s, g: (s, g, 0, 0)),
            pl.BlockSpec((HD, 128), lambda s, g: (0, 0)),
        ],
        out_specs=[
            pl.BlockSpec((3, GROUP, HD, LANES), lambda s, g: (0, g, 0, s)),
            pl.BlockSpec((64, HD), lambda s, g: (0, 0)),
        ],
        out_shape=[
            jax.ShapeDtypeStruct((3, HEADS, HD, slots * LANES), BF),
            jax.ShapeDtypeStruct((64, HD), F32),
        ],
        compiler_params=pltpu.CompilerParams(vmem_limit_bytes=20 * 2**20),
        cost_estimate=cheap(slots * HEADS * 5 * LANES * LANES * 256),
        name="attend_back",
    )(qkv, qkv, qkv, grad, probs, rel_cols)


def resident(shape):
    return pl.BlockSpec(shape, lambda *_: (0,) * len(shape))


def cheap(flops):
    return pl.CostEstimate(flops=flops // 8, bytes_accessed=1_000_000, transcendentals=0)


def settings(mebibytes):
    return pltpu.CompilerParams(vmem_limit_bytes=mebibytes * 2**20)


def middle_kernel(att_ref, proj_ref, short_ref, mask_ref, rows_ref, middle_ref, normed_ref):
    branch = dot_tn(att_ref[...], proj_ref[...])[:ROWS] + rows_ref[0:1]
    middle = (short_ref[...].astype(F32) + branch) * mask_ref[...]
    middle_ref[...] = middle
    centred = middle - jnp.mean(middle, axis=1, keepdims=True)
    inverse = lax.rsqrt(jnp.mean(centred * centred, axis=1, keepdims=True) + NORM_EPSILON)
    normed_ref[...] = (centred * inverse * rows_ref[1:2] + rows_ref[2:3]).astype(BF)


def to_middle(attended, proj_full, short, mask, rows):
    slots = attended.shape[1] // LANES
    by_slot = lambda width: pl.BlockSpec((ROWS, width), lambda s: (s, 0))
    return pl.pallas_call(
        middle_kernel,
        grid=(slots,),
        in_specs=[
            pl.BlockSpec((D, LANES), lambda s: (0, s)),
            resident((D, D)),
            by_slot(D),
            by_slot(1),
            resident((8, D)),
        ],
        out_specs=[by_slot(D), by_slot(D)],
        out_shape=[
            jax.ShapeDtypeStruct((slots * ROWS, D), F32),
            jax.ShapeDtypeStruct((slots * ROWS, D), BF),
        ],
        compiler_params=settings(24),
        cost_estimate=cheap(2 * slots * LANES * D * D),
        name="middle",
    )(attended, proj_full, short, mask, rows)


def norm_parts(grad, value, gain):
    centred = value - jnp.mean(value, axis=1, keepdims=True)
    inverse = lax.rsqrt(jnp.mean(centred * centred, axis=1, keepdims=True) + NORM_EPSILON)
    hat = centred * inverse
    scaled = grad * gain
    mean_one = jnp.mean(scaled, axis=1, keepdims=True)
    mean_two = jnp.mean(scaled * hat, axis=1, keepdims=True)
    sums = [jnp.sum(grad * hat, axis=0, keepdims=True), jnp.sum(grad, axis=0, keepdims=True)]
    sums = jnp.concatenate(sums + [jnp.zeros((6, D), F32)], axis=0)
    return inverse * (scaled - mean_one - hat * mean_two), sums


def add_sums(sums_ref, sums):
    @pl.when(pl.program_id(0) == 0)
    def _():
        sums_ref[...] = jnp.zeros_like(sums_ref)

    sums_ref[...] += sums


def second_norm_kernel(grad_ref, came_ref, middle_ref, out_ref, mask_ref, rows_ref, total_ref, pad_ref, sums_ref):
    grad = grad_ref[...] + came_ref[...].astype(F32)
    back, sums = norm_parts(grad, middle_ref[...], rows_ref[1:2])
    total = (out_ref[...].astype(F32) + back) * mask_ref[...]
    total_ref[...] = total
    low = total.astype(BF)
    pad_ref[...] = jnp.concatenate([low, jnp.zeros((LANES - ROWS, D), BF)], axis=0)
    add_sums(sums_ref, sums)


def first_norm_kernel(grad_ref, came_ref, short_ref, total_ref, mask_ref, rows_ref, out_ref, sums_ref):
    mask = mask_ref[...]
    grad = (grad_ref[:ROWS] + came_ref[...].astype(F32)) * mask
    back, sums = norm_parts(grad, short_ref[...].astype(F32), rows_ref[3:4])
    out_ref[0] = ((total_ref[...] + back) * mask)[: WIN * WIN]
    add_sums(sums_ref, sums)


def by_slots(kernel, name, given, outs):
    slots = given[1].shape[0] // ROWS

    def spec(shape):
        if len(shape) == 3:
            return pl.BlockSpec((1,) + shape[1:], lambda s: (s, 0, 0))
        if shape[0] == 8:
            return resident(shape)
        return pl.BlockSpec((shape[0] // slots, shape[1]), lambda s: (s, 0))

    return pl.pallas_call(
        kernel,
        grid=(slots,),
        in_specs=[spec(item.shape) for item in given],
        out_specs=[spec(item.shape) for item in outs],
        out_shape=list(outs),
        compiler_params=settings(32),
        cost_estimate=cheap(1_000_000),
        name=name,
    )(*given)


SIDE = 256
SPOTS = [(row, column) for row in range(D // SIDE) for column in range(row, D // SIDE)]


def upper_blocks(gram):
    parts = [
        gram[row * SIDE : (row + 1) * SIDE, column * SIDE : (column + 1) * SIDE] for row, column in SPOTS
    ]
    return jnp.concatenate(parts, axis=0)


def chain_kernel(count, gram_ref, y_ref, *refs):
    outs, (high_ref, rest_ref, b_ref, t_high, t_rest, z_high, z_rest) = refs[:count], refs[count:]
    columns = [slice(start, start + SIDE) for start in range(0, D, SIDE)]
    row = lax.broadcasted_iota(jnp.int32, (SIDE, SIDE), 0)
    spot = row == lax.broadcasted_iota(jnp.int32, (SIDE, SIDE), 1)
    trace = jnp.zeros((), F32)
    for place, (row, column) in enumerate(SPOTS):
        if row == column:
            trace = trace + jnp.sum(jnp.where(spot, gram_ref[place * SIDE : (place + 1) * SIDE, :], 0.0))
    inverse = 1.0 / (jnp.sqrt(trace) + ORTHO_EPSILON)
    for place, (row, column) in enumerate(SPOTS):
        block = gram_ref[place * SIDE : (place + 1) * SIDE, :] * inverse * inverse
        for part, over, down in ((block, row, column), (block.T, column, row)):
            high, rest = split_low(part)
            high_ref[columns[over], columns[down]] = high
            rest_ref[columns[over], columns[down]] = rest
    z_high[0] = y_ref[...]

    def mirror(ref, values, place):
        cut = columns[place]
        ref[: (place + 1) * SIDE, cut] = values
        for over in range(place):
            ref[cut, columns[over]] = values[columns[over], :].T

    def polynomial():
        for place, cut in enumerate(columns):
            rows = slice(0, (place + 1) * SIDE)
            square = dot_nn(high_ref[rows, :], high_ref[:, cut])
            value = high_ref[rows, cut].astype(F32) + rest_ref[rows, cut].astype(F32)
            poly = COEFF_CUBIC * value + COEFF_QUINTIC * square
            line = lax.broadcasted_iota(jnp.int32, poly.shape, 0) - place * SIDE
            eye = line == lax.broadcasted_iota(jnp.int32, poly.shape, 1)
            mirror(b_ref, (poly + jnp.where(eye, COEFF_LINEAR, 0.0)).astype(BF), place)

    def follow(now, cut, fine):
        value = dot_nn(z_high[now], b_ref[:, cut])
        return value + dot_nn(z_rest[now], b_ref[:, cut]) if fine else value

    def advance(now, fine, z_fine, z_more):
        later = 1 - now
        polynomial()
        for cut in columns:
            value = dot_nn(b_ref[...], high_ref[:, cut])
            if fine:
                value = value + dot_nn(b_ref[...], rest_ref[:, cut])
            t_high[:, cut], rest = split_low(value)
            if fine:
                t_rest[:, cut] = rest
            z_high[later, :, cut], rest = split_low(follow(now, cut, z_fine))
            if z_more:
                z_rest[later, :, cut] = rest
        for place, cut in enumerate(columns):
            rows = slice(0, (place + 1) * SIDE)
            value = dot_nn(t_high[rows, :], b_ref[:, cut])
            if fine:
                value = value + dot_nn(t_rest[rows, :], b_ref[:, cut])
            high, rest = split_low(value)
            mirror(high_ref, high, place)
            mirror(rest_ref, rest, place)

    advance(0, True, False, True)

    @pl.loop(1, ITERS - 2)
    def _(step):
        advance(step % 2, True, True, True)

    advance((ITERS - 2) % 2, False, False, False)
    polynomial()
    for cut in columns:
        value = (follow((ITERS - 1) % 2, cut, False) * inverse).astype(BF)
        for place, out_ref in enumerate(outs):
            rows = out_ref.shape[0]
            out_ref[:, cut] = value[place * rows : (place + 1) * rows]


def chain(gram, rows, count):
    half = pltpu.VMEM((D, D), BF)
    flow = pltpu.VMEM((2,) + rows.shape, BF)
    whole = pl.BlockSpec(memory_space=pltpu.VMEM)
    part = rows.shape[0] // count
    pieces = count if part % 16 == 0 else 1
    out = pl.pallas_call(
        partial(chain_kernel, pieces),
        in_specs=[whole, whole],
        out_specs=[whole] * pieces,
        out_shape=[jax.ShapeDtypeStruct((rows.shape[0] // pieces, D), BF)] * pieces,
        scratch_shapes=[half] * 5 + [flow] * 2,
        compiler_params=settings(56),
        cost_estimate=pl.CostEstimate(flops=18 * 2 * D**3, bytes_accessed=6 * D * D, transcendentals=0),
        name="chain",
    )(gram, rows)
    return out if pieces == count else [out[0][at * part : (at + 1) * part] for at in range(count)]


EVERY = ("ga", "gb", "gc", "gy")


def peer(value):
    return lax.ppermute(value, "gc", [(0, 1), (1, 0)])


def steps_of(axis):
    return lax.axis_size(axis).bit_length() - 1


def first_stages():
    return [("f", step) for step in reversed(range(steps_of("ga")))]


def second_stages():
    return [("s", step) for step in reversed(range(steps_of("gb")))]


def plane_stages():
    return [("z", step) for step in range(steps_of("gy"))]


def gather_groups():
    deep = plane_stages()
    return [deep[1:][::-1], deep[:1]], [second_stages()[::-1]], [first_stages()[::-1]]


def reduce_groups():
    deep = plane_stages()
    return [first_stages()], [second_stages()], [deep[:1], deep[1:]]


def half_stages():
    return first_stages() + second_stages() + plane_stages()


def bit_of(stage, core):
    kind, step = stage
    if kind == "z":
        return "gy", steps_of("gy") - 1 - step if core == 0 else step
    return ("ga" if (kind == "f") == (core == 0) else "gb"), step


def my_bit(stage):
    values = []
    for core in range(2):
        axis, step = bit_of(stage, core)
        values.append((lax.axis_index(axis) >> step) & 1)
    return jnp.where(lax.axis_index("gc") == 0, values[0], values[1])


def swap(value, stage):
    if stage == "c":
        return peer(value)
    sizes = [lax.axis_size(axis) for axis in EVERY]
    pairs = []
    for place in range(math.prod(sizes)):
        spot, rest = [], place
        for size in reversed(sizes):
            spot.insert(0, rest % size)
            rest //= size
        axis, step = bit_of(stage, spot[2])
        spot[EVERY.index(axis)] ^= 1 << step
        other = 0
        for size, at in zip(sizes, spot):
            other = other * size + at
        pairs.append((place, other))
    return lax.ppermute(value, EVERY, pairs)


class Rounds:
    def __init__(self):
        self.last = None

    def go(self, chains, work=None, *values):
        chains = [chain for chain in chains if not chain.done]
        while long := [chain for chain in chains if chain.left > 1]:
            self.once(long)
        out = self.once(chains, work, *values)
        for chain in chains:
            chain.left = chain.counts.pop(0) if chain.counts else 0
        return out

    def once(self, chains, work=None, *values):
        marks = [] if self.last is None else [self.last]
        held = []
        for chain in chains:
            chain.wait_for(held[-1:])
            chain.look()
            held.append(lax.optimization_barrier((chain.value, *marks))[0])
        came = [swap(value, chain.stage) for value, chain in zip(held, chains)]
        ready = lax.optimization_barrier((*values, *held, *marks))
        out = () if work is None else work(*ready[: len(values)])
        leaves, tree = jax.tree.flatten(out)
        ended = lax.optimization_barrier(tuple(came) + tuple(leaves))
        self.last = ended[0]
        for chain, value in zip(chains, ended):
            chain.take(value)
            chain.left -= 1
        return jax.tree.unflatten(tree, ended[len(chains) :])


class Chain:
    def __init__(self, work, groups):
        self.work, self.result = work, None
        self.steps = sum(len(group) for group in groups)
        self.pending = [None]
        self.counts = [len(group) for group in groups if group]
        self.left = self.counts.pop(0)

    def take(self, came):
        self.pending = [came]
        self.steps -= 1

    def look(self):
        if self.pending:
            try:
                self.value, self.stage = self.work.send(self.pending.pop())
            except StopIteration as stop:
                self.result = stop.value

    def wait_for(self, others):
        if others and self.pending and self.pending[0] is not None:
            self.pending = [lax.optimization_barrier((self.pending[0], *others))[0]]

    @property
    def done(self):
        return self.steps == 0

    @property
    def out(self):
        self.look()
        return self.result


def gather_half(shard):
    groups = sum(gather_groups(), [])

    def work():
        held = shard[None]
        for stage in sum(groups, []):
            came = yield held, stage
            first = my_bit(stage) == 0
            held = jnp.concatenate([jnp.where(first, held, came), jnp.where(first, came, held)], axis=0)
        return held.reshape(-1, shard.shape[-1])

    return Chain(work(), groups)


def gather_relative(shard, groups):
    def work():
        order, canon = sum(groups, []), half_stages()
        held = shard
        for stage in order[:-1]:
            came = yield held, stage
            held = jnp.stack([held, came])
        came = yield held, order[-1]
        there = order[-2::-1]
        turn = [there.index(stage) for stage in canon[1:]] + [len(there), len(there) + 1]
        return tuple(half.transpose(turn).reshape(-1, shard.shape[-1]) for half in (held, came))

    return Chain(work(), groups)


def relative(value):
    stages = half_stages()
    place = sum(my_bit(stage) << (len(stages) - 1 - at) for at, stage in enumerate(stages))
    spots = jnp.arange(value.shape[0])
    picker = ((spots[:, None] ^ place) == spots[None, :]).astype(F32)
    return jnp.dot(picker, value, precision=lax.Precision.HIGHEST, preferred_element_type=F32)


def reduce_half(grad, groups, kind=BF):
    def work():
        live = half_stages()
        parts = [grad.reshape((2,) * len(live) + (-1, grad.shape[-1]))]
        for stage in sum(groups, []):
            place, mine = live.index(stage), my_bit(stage)
            live.remove(stage)

            def pick(which):
                cuts = [lax.dynamic_index_in_dim(part, which, place, False) for part in parts]
                return cuts[0] if len(cuts) == 1 else (cuts[0].astype(F32) + cuts[1].astype(F32)).astype(kind)

            send = pick(1 - mine)
            parts = list(lax.optimization_barrier((*parts, send))[:-1])
            keep = pick(mine)
            came = yield send, stage
            parts = [keep, came]
        return parts[0].astype(F32) + parts[1].astype(F32)

    return Chain(work(), groups)


def reduce_relative(keep, send, groups):
    def work():
        live, order = half_stages(), sum(groups, [])
        came = yield send, order[0]
        assert order[0] == live[0]
        live.remove(order[0])
        shape = (2,) * len(live) + (-1, send.shape[-1])
        parts = [keep().reshape(shape), came.reshape(shape)]
        for stage in order[1:]:
            place = live.index(stage)
            live.remove(stage)

            def pick(which):
                cuts = [lax.index_in_dim(part, which, place, False).astype(F32) for part in parts]
                return (cuts[0] + cuts[1]).astype(BF)

            away = pick(1)
            parts = list(lax.optimization_barrier((*parts, away))[:-1])
            kept = pick(0)
            came = yield away, stage
            parts = [kept, came]
        return parts[0].astype(F32) + parts[1].astype(F32)

    return Chain(work(), groups)


def turned(value):
    stages = half_stages()
    shape = value.shape
    value = value.reshape((2,) * len(stages) + shape[1:])
    side, deep = len(first_stages()), len(plane_stages())
    order = list(range(side, 2 * side)) + list(range(side)) + list(reversed(range(2 * side, 2 * side + deep)))
    order += list(range(2 * side + deep, value.ndim))
    return value.transpose(order).reshape(shape)


def join_halves(mine, theirs):
    chips = 1 << len(half_stages())
    planes = lax.axis_size("gy")
    first = lax.axis_index("gc") == 0
    shape = (chips, -1) + mine.shape[1:]
    mine, theirs = mine.reshape(shape), theirs.reshape(shape)
    both = [jnp.where(first, mine, theirs), turned(jnp.where(first, theirs, mine))]
    both = [half.reshape((chips // planes, planes) + half.shape[1:]) for half in both]
    return jnp.stack(both, axis=1).reshape((-1,) + mine.shape[2:])


def cut_half(value, which):
    chips = 1 << len(half_stages())
    planes = lax.axis_size("gy")
    shape = value.shape
    value = value.reshape((chips // planes, 2, planes, -1) + shape[1:])
    halves = [value[:, core].reshape((chips, -1) + shape[1:]) for core in range(2)]
    return jnp.where(which == 0, halves[0], turned(halves[1])).reshape((-1,) + shape[1:])


def sum_rows(value, stages):
    def work():
        held = value
        for stage in stages:
            halves = held.reshape((2, held.shape[0] // 2) + held.shape[1:])
            mine = my_bit(stage)
            keep = lax.dynamic_index_in_dim(halves, mine, 0, False)
            came = yield lax.dynamic_index_in_dim(halves, 1 - mine, 0, False), stage
            held = keep + came
        return held

    return Chain(work(), [[stage] for stage in stages])


def spread_rows(value, stages):
    def work():
        held = value
        for stage in stages:
            came = yield held, stage
            first = my_bit(stage) == 0
            held = jnp.concatenate([jnp.where(first, held, came), jnp.where(first, came, held)], axis=0)
        return held

    return Chain(work(), [[stage] for stage in stages])


def plane_sum(rounds, value, work, *values):
    core = lax.axis_index("gc")
    halves = value.reshape((2, value.shape[0] // 2) + value.shape[1:])

    def over_cores(mine, theirs):
        return mine + peer(theirs)

    held = rounds.go(
        [],
        over_cores,
        lax.dynamic_index_in_dim(halves, core, 0, False),
        lax.dynamic_index_in_dim(halves, 1 - core, 0, False),
    )
    stages = first_stages() + second_stages()
    chain = sum_rows(held, stages)
    out = rounds.go([chain], work, *values)
    while not chain.done:
        rounds.go([chain])
    chain = spread_rows(chain.out, stages[::-1])
    while not chain.done:
        rounds.go([chain])
    held = chain.out
    came = rounds.go([], peer, held)
    held = [jnp.where(core == 0, held, came), jnp.where(core == 0, came, held)]
    return jnp.concatenate(held, axis=0), out


def sum_whole(value, stages):
    def work():
        held = value
        for stage in stages:
            came = yield held, stage
            held = held + came
        return held

    return Chain(work(), [[stage] for stage in stages])


def token_mask(placement, counts):
    slot_count = placement.shape[0]
    live = (jnp.arange(slot_count, dtype=jnp.int32) < counts[0]).astype(F32)
    inner = jnp.arange(WIN * WIN, dtype=jnp.int32)
    row_pos = placement[:, 0:1] * WIN + inner[None, :] // WIN
    col_pos = placement[:, 1:2] * WIN + inner[None, :] % WIN
    inside = ((row_pos < GRID) & (col_pos < GRID)).astype(F32)
    return inside * live[:, None]


def normalised(value):
    centred = value - jnp.mean(value, axis=-1, keepdims=True)
    inverse = lax.rsqrt(jnp.mean(centred * centred, axis=-1, keepdims=True) + NORM_EPSILON)
    return centred * inverse, inverse


def norm_back(grad, hat, inverse, gain):
    scaled = grad * gain
    mean_one = jnp.mean(scaled, axis=-1, keepdims=True)
    mean_two = jnp.mean(scaled * hat, axis=-1, keepdims=True)
    return inverse * (scaled - mean_one - hat * mean_two)


def pad_slots(value, rows):
    slots, given, width = value.shape
    return jnp.pad(value, ((0, 0), (0, rows - given), (0, 0))).reshape(slots * rows, width)


def widen_slots(value):
    return pad_slots(value.reshape(-1, ROWS, value.shape[1]), LANES)


def narrow_slots(value):
    return value.reshape(-1, LANES, value.shape[1])[:, :ROWS].reshape(-1, value.shape[1])


def body(
    windows,
    cotangent,
    placement,
    counts,
    qkv_weight,
    proj_weight,
    up_weight,
    down_weight,
    qkv_moment,
    proj_moment,
    up_moment,
    down_moment,
    vectors,
    vector_moment,
    rel_pos,
    rel_moment,
):
    core = lax.axis_index("gc")
    planes = lax.axis_size("gy")
    chips = 1 << len(half_stages())
    devices = 2 * chips
    slots, tokens, _ = windows.shape
    wide = slots * LANES
    first, second, deep = first_stages(), second_stages(), plane_stages()
    rounds = Rounds()

    def block(work, *values):
        shapes = jax.eval_shape(work, *values)

        def idle(*_):
            return jax.tree.map(lambda item: jnp.zeros(item.shape, item.dtype), shapes)

        return lax.cond(counts[0] > 0, work, idle, *values)

    mask = pad_slots(token_mask(placement, counts)[:, :, None], ROWS)
    short_low = pad_slots(windows, ROWS) * mask.astype(BF)
    out_low = pad_slots(cotangent, ROWS) * mask.astype(BF)
    count = short_low.shape[0]
    by_z, by_second, by_first = gather_groups()
    part, spare = qkv_weight.shape[1], vectors.shape[0]
    vec_rows = jnp.pad(vectors.astype(BF)[None], ((0, 7), (0, D - spare)))
    take_qkv = gather_half(jnp.concatenate([qkv_weight.astype(BF).T, vec_rows], axis=0))
    take_proj = gather_half(proj_weight.astype(BF))
    take_up = gather_relative(up_weight.astype(BF).T, by_z + by_second + by_first)
    take_down = gather_relative(down_weight.astype(BF), by_second + by_z + by_first)

    mask_row = jnp.pad(mask.astype(BF).T, ((0, 7), (0, D - count)))
    rounds.go([take_qkv, take_down])
    short_peer = rounds.go([take_qkv, take_proj], peer, jnp.concatenate([short_low, mask_row], axis=0))
    rounds.go([take_qkv, take_up, take_proj])

    def first_hats(mine, theirs):
        return normalised(mine.astype(F32))[0], normalised(theirs[:count].astype(F32))[0]

    (hat_mine, hat_peer), out_peer = rounds.go(
        [take_qkv, take_up, take_proj],
        lambda one, two, three: (block(first_hats, one, two), peer(three)),
        short_low,
        short_peer,
        out_low,
    )
    qkv_half = take_qkv.out
    wide_part = part + 8

    def slim(value):
        return value.reshape((chips, wide_part) + value.shape[1:])[:, :part].reshape((-1,) + value.shape[1:])

    def stout(value):
        value = value.reshape((chips, part) + value.shape[1:])
        return jnp.pad(value, ((0, 0), (0, 8)) + ((0, 0),) * (value.ndim - 2)).reshape((-1,) + value.shape[2:])

    def to_qkv(qkv_half, hat, vec, live, bias):
        rows = widen_slots(((hat * vec[:D] + vec[D : 2 * D]) * live).astype(BF))
        return with_layout_constraint((dot_nt(qkv_half, rows) + bias).astype(BF), Layout((0, 1))), rows

    def both_qkv(qkv_half, hat_mine, hat_peer, short_peer, mask):
        vec_half = qkv_half.reshape(chips, wide_part, D)[:, part, :spare]
        vec = join_halves(vec_half, peer(vec_half)).reshape(-1).astype(F32)
        bias_qkv = jnp.concatenate([vec[2 * D : 3 * D], jnp.zeros((D,), F32), vec[3 * D : 4 * D]])
        bias_qkv = stout(cut_half(bias_qkv, core))[:, None]
        live = short_peer[count, :count].astype(F32)[:, None]
        theirs, pad_peer = block(to_qkv, qkv_half, hat_peer, vec, live, bias_qkv)
        came = tuple(peer(piece) for piece in jnp.split(theirs, 4, axis=0))
        mine, pad_mine = block(to_qkv, qkv_half, hat_mine, vec, mask, bias_qkv)
        return mine, came, vec, pad_mine, pad_peer

    qkv_mine, qkv_came, vec, pad_mine, pad_peer = rounds.go(
        [take_up, take_proj, take_down], both_qkv, qkv_half, hat_mine, hat_peer, short_peer, mask
    )
    proj_half = take_proj.out
    bias_down = vec[7 * D : 8 * D]
    rel_low = rel_pos.astype(BF)[:, ::-1]
    rel_rows = jnp.pad(rel_low, ((0, 0), (0, 5), (0, 0))).reshape(64, HD)
    rel_cols = jnp.concatenate([rel_rows, rel_rows], axis=0).T

    def to_attended(mine, came, proj_half, out_low, out_peer, vec):
        proj_came = peer(proj_half)
        qkv = join_halves(slim(mine), slim(jnp.concatenate(came, axis=0))).reshape(3, HEADS, HD, wide)
        attended, probs = attend(qkv, rel_rows)
        out_both = jnp.concatenate([out_low, out_peer], axis=0)
        bias_up = relative(cut_half(vec[8 * D :], core).reshape(chips, -1)).reshape(1, -1)
        table = vec[: 8 * D].reshape(8, D)
        middle_rows = jnp.concatenate([table[4:7], table[:1], table[:4]], axis=0)
        return join_halves(proj_half, proj_came), out_both, qkv, attended, probs, bias_up, middle_rows

    proj_full, out_both, qkv, attended, probs, bias_up, middle_rows = rounds.go(
        [take_up, take_down], to_attended, qkv_mine, qkv_came, proj_half, out_low, out_peer, vec
    )
    attended = attended.reshape(D, wide)
    up_halves = take_up.out
    width = up_halves[0].shape[0]

    def to_gelu(mine, came, up_full, out_both):
        both = jnp.concatenate([mine, came], axis=0)
        pre = dot_nt(both, up_full) + bias_up
        bell = jnp.exp(-0.5 * pre * pre)
        below = 0.5 * (1.0 + lax.erf(pre * (0.5**0.5)))
        gelu = (pre * below).astype(BF)
        slope = (below + pre * bell * (2.0 * math.pi) ** -0.5).astype(BF)
        send = dot_tn(gelu[:, width:], out_both).astype(BF)
        return both, gelu, slope, dot_tn(gelu[:, :width], out_both).astype(BF), send

    def to_hidden(attended, up_one, up_two):
        middle, normed = to_middle(attended, proj_full, short_low, mask, middle_rows)
        came = peer(normed)
        up_full = jnp.concatenate([up_one, up_two], axis=0)
        return middle, up_full, *to_gelu(normed, came, up_full, out_both)

    middle, up_full, normed_both, gelu_both, slope, keep_down, send_down = rounds.go(
        [take_down], to_hidden, attended, *up_halves
    )
    down_halves = take_down.out

    by_first, by_second, by_z = reduce_groups()
    mixed_order = by_first + by_z + by_second
    plane_last = by_first + by_second + by_z
    give_down = reduce_relative(lambda: keep_down, send_down, mixed_order)

    def to_pre(down_one, down_two, out_both, slope, up_full):
        down_full = jnp.concatenate([down_one, down_two], axis=0)
        pre = (dot_nt(out_both, down_full) * slope.astype(F32)).astype(BF)
        return pre, dot_nn(pre[count:], up_full).astype(BF)

    def second_mine(pre, up_full):
        return dot_nn(pre[:count], up_full)

    def up_back(pre, normed_both):
        send = dot_tn(pre[:, width:], normed_both).astype(BF)
        return send, jnp.sum(pre, axis=0, dtype=F32)

    def to_branch(down_one, down_two, out_both, slope, up_full, normed_both, middle):
        pre, theirs = to_pre(down_one, down_two, out_both, slope, up_full)
        came = peer(theirs)
        send_up, up_bias = block(up_back, pre, normed_both)
        given = (second_mine(pre, up_full), came, middle, out_low, mask, middle_rows)
        shapes = (((count, D), F32), ((wide, D), BF), ((8, D), F32))
        outs = [jax.ShapeDtypeStruct(*shape) for shape in shapes]
        return pre, send_up, up_bias, *by_slots(second_norm_kernel, "second_norm", given, outs)

    pre, send_up, up_bias, grad_total, branch_pad, second_sums = rounds.go(
        [give_down], to_branch, *down_halves, out_both, slope, up_full, normed_both, middle
    )
    kept = {"up": lambda: dot_tn(pre[:, :width], normed_both).astype(BF)}
    give_up = reduce_relative(lambda: kept["up"](), send_up, plane_last)

    def attention_back(branch_pad, attended, pre, normed_both):
        keep_up = dot_tn(pre[:, :width], normed_both).astype(BF)
        grad_proj = dot_nn(attended, branch_pad).astype(BF)
        proj_came = peer(cut_half(grad_proj, 1 - core))
        grad_att = dot_nt(proj_full, branch_pad).astype(BF).reshape(HEADS, HD, wide)
        grad_qkv, grad_rel = attend_back(qkv, grad_att, probs, rel_cols)
        grad_qkv = grad_qkv.reshape(3 * D, wide)
        grad_proj = (cut_half(grad_proj, core).astype(F32) + proj_came.astype(F32)).astype(BF)
        halves = [stout(cut_half(grad_qkv, which)) for which in (core, 1 - core)]
        return grad_qkv, grad_rel, *halves, grad_proj, keep_up

    grad_qkv, grad_rel, qkv_grad_mine, qkv_grad_theirs, grad_proj, keep_up = rounds.go(
        [give_up, give_down], attention_back, branch_pad, attended, pre, normed_both
    )
    kept["up"] = lambda: keep_up
    give_proj = reduce_half(grad_proj, plane_last)
    normed_pad = jnp.concatenate([pad_mine, pad_peer], axis=0)

    def qkv_back(mine, came, normed_pad):
        both = jnp.concatenate([mine, came], axis=1)
        return both, dot_nn(both, normed_pad).astype(BF)

    def to_qkv_grad(mine, theirs, normed_pad):
        return qkv_back(mine, peer(theirs), normed_pad)

    qkv_grad_both, grad_qkv_half = rounds.go(
        [give_up, give_down, give_proj], to_qkv_grad, qkv_grad_mine, qkv_grad_theirs, normed_pad
    )
    give_qkv = reduce_half(grad_qkv_half, plane_last)

    def first_theirs(both, weight):
        return narrow_slots(dot_tn(both[:, wide:], weight).astype(BF))

    def first_mine(both, weight):
        return dot_tn(both[:, :wide], weight)

    def mlp_theirs(gelu_both, down_one, down_two):
        down_full = jnp.concatenate([down_one, down_two], axis=0)
        return dot_nn(gelu_both[count:], down_full).astype(BF)

    def mlp_mine(gelu_both, down_one, down_two, came, middle):
        down_full = jnp.concatenate([down_one, down_two], axis=0)
        mlp_out = dot_nn(gelu_both[:count], down_full) + came.astype(F32) + bias_down
        return ((middle + mlp_out) * mask).astype(BF).reshape(slots, ROWS, D)[:, :tokens]

    def to_small(grad_qkv, branch_pad, second_sums, out_low, up_bias, grad_rel):
        up_bias = relative(up_bias.reshape(chips, -1))
        up_bias = [jnp.where(core == 0, up_bias, 0.0), turned(jnp.where(core == 0, 0.0, up_bias))]
        up_bias = jnp.stack(up_bias, axis=1).reshape(chips // planes, planes, 2, -1)
        up_bias = jnp.swapaxes(up_bias, 1, 2).reshape(-1, D)
        qkv_bias = jnp.sum(grad_qkv, axis=1, dtype=F32).reshape(3, D)
        rows = [
            jnp.zeros((2, D), F32),
            qkv_bias[:1],
            qkv_bias[2:],
            jnp.sum(branch_pad, axis=0, dtype=F32, keepdims=True),
            second_sums[:2],
            jnp.sum(out_low, axis=0, dtype=F32, keepdims=True),
            up_bias,
        ]
        rows = jnp.concatenate(rows).reshape(-1, SIDE), grad_rel.reshape(-1, SIDE)
        return jnp.concatenate(rows)

    def for_peer(both, weight, gelu_both, down_one, down_two, *values):
        ours = block(first_theirs, both, weight), block(mlp_theirs, gelu_both, down_one, down_two)
        return *ours, to_small(*values)

    first_sent, mlp_sent, small_early = rounds.go(
        [give_qkv, give_up, give_down, give_proj],
        for_peer,
        qkv_grad_both,
        qkv_half,
        gelu_both,
        *down_halves,
        grad_qkv,
        branch_pad,
        second_sums,
        out_low,
        up_bias,
        grad_rel,
    )

    stride = max(planes // 4, 1)
    homes = {"qkv": 0, "down": stride, "up": 2 * stride, "proj": 3 * stride}
    me_z = lax.axis_index("gy")
    room = max(up_weight.shape[1], down_weight.shape[0], part, proj_weight.shape[0])
    pieces = [[] for _ in range(planes)]

    def home(**lows):
        parts = []
        for far in range(planes):
            value = sum(
                jnp.where((me_z ^ far) == homes[name], low, jnp.zeros_like(low)) for name, low in lows.items()
            )
            if far:
                value = lax.ppermute(value, "gy", [(homes[name] ^ far, homes[name]) for name in lows])
            parts.append(value)
        return parts

    def arrive(parts):
        for row, piece in zip(pieces, parts):
            row.append(jnp.pad(piece, ((0, room - piece.shape[0]), (0, 0))))

    def moment(old, grad, flip):
        new = MOMENT_MATRIX * old + (grad.T if flip else grad)
        return new, (new.T if flip else new).astype(BF)

    first_came, mlp_came = rounds.go(
        [give_qkv, give_up, give_proj], lambda one, two: (peer(one), peer(two)), first_sent, mlp_sent
    )
    new_down, low_down = moment(down_moment, give_down.out, False)
    new_up, low_up = moment(up_moment, give_up.out, True)

    def to_ends(low_down, low_up, both, weight, first_came, grad_total, short_low):
        arrived = home(down=low_down, up=low_up)
        given = (block(first_mine, both, weight), first_came, short_low, grad_total, mask, middle_rows)
        outs = [jax.ShapeDtypeStruct((slots, tokens, D), F32), jax.ShapeDtypeStruct((8, D), F32)]
        return arrived, *by_slots(first_norm_kernel, "first_norm", given, outs)

    arrived, grad_input, first_sums = rounds.go(
        [give_qkv, give_proj],
        to_ends,
        low_down,
        low_up,
        qkv_grad_both,
        qkv_half,
        first_came,
        grad_total,
        short_low,
    )
    arrive(arrived)
    new_proj, low_proj = moment(proj_moment, give_proj.out, False)

    arrive(rounds.go([give_qkv, give_proj], lambda value: home(proj=value), low_proj))
    while not give_qkv.done:
        rounds.go([give_qkv])
    new_qkv, low_qkv = moment(qkv_moment, give_qkv.out[:part], True)
    arrive(rounds.go([], lambda value: home(qkv=value), low_qkv))
    held = jnp.concatenate([sum(row[1:], row[0]) for row in pieces], axis=0)
    first_rows = jnp.pad(first_sums[:2].reshape(-1, SIDE), ((0, small_early.shape[0] - 2 * D // SIDE), (0, 0)))
    small = small_early + first_rows
    blocks = upper_blocks(dot_tn(held, held))
    fill = -small.shape[0] % (8 * devices // planes)
    summed, block_out = plane_sum(
        rounds,
        jnp.concatenate([blocks, jnp.pad(small, ((0, fill), (0, 0)))], axis=0),
        lambda *values: block(mlp_mine, *values),
        gelu_both,
        *down_halves,
        mlp_came,
        middle,
    )
    gram = summed[: blocks.shape[0]]
    add_small = sum_whole(summed[blocks.shape[0] : blocks.shape[0] + small.shape[0]], deep)

    def send_back(ortho):
        back = [ortho[0]]
        for far in range(1, planes):
            back.append(lax.ppermute(ortho[far], "gy", [(place, place ^ far) for place in range(planes)]))
        return jnp.stack(back)

    ortho = rounds.go([add_small], lambda *pair: chain(*pair, planes), gram, held)
    back = rounds.go([add_small], lambda *parts: send_back(parts), *ortho)
    while not add_small.done:
        rounds.go([add_small])
    small = add_small.out.reshape(-1)
    rel_total = small[devices * spare :].reshape(2, 32, HD)
    vec_total = lax.dynamic_slice_in_dim(small, lax.axis_index(EVERY) * spare, spare)

    def part_of(name, rows):
        return lax.dynamic_index_in_dim(back, me_z ^ homes[name], 0, False)[:rows].astype(F32)

    parts = [
        part_of("qkv", qkv_weight.shape[1]),
        part_of("proj", proj_weight.shape[0]),
        part_of("up", up_weight.shape[1]),
        part_of("down", down_weight.shape[0]),
    ]

    scales = (math.sqrt(3.0), 1.0, math.sqrt(max(1.0, FF / D)), math.sqrt(max(1.0, D / FF)))
    masters = (qkv_weight, proj_weight, up_weight, down_weight)
    flipped = (True, False, True, False)
    new_weights = [
        master - RATE_MATRIX * factor * (part.T if turn else part)
        for master, factor, part, turn in zip(masters, scales, parts, flipped)
    ]

    rate_vec = 0.5 / math.sqrt(float(devices * slots * tokens))
    vec_moment_new = MOMENT_VECTOR * vector_moment + vec_total
    rel_grad = rel_total[:, : 2 * WIN - 1][:, ::-1]
    rel_moment_new = MOMENT_VECTOR * rel_moment + rel_grad
    return (
        block_out,
        grad_input,
        new_qkv,
        new_proj,
        new_up,
        new_down,
        new_weights[0],
        new_weights[1],
        new_weights[2],
        new_weights[3],
        vec_moment_new,
        vectors - rate_vec * vec_moment_new,
        rel_moment_new,
        rel_pos - 0.2 * rate_vec * rel_moment_new,
    )


def solution(mesh):
    size_x, size_y = mesh.shape["gx"], mesh.shape["gy"]
    side = math.isqrt(size_x // 2)
    assert side * side * 2 == size_x
    grid = (side, size_x // 2 // side, 2, size_y)
    split = Mesh(mesh.devices.reshape(grid), ("ga", "gb", "gc", "gy"))
    flat = ("ga", "gb", "gc", "gy")
    slab, cols, rows, line = P(flat, None, None), P(None, flat), P(flat, None), P(flat)
    return jax.shard_map(
        body,
        mesh=split,
        in_specs=(
            (slab, slab, rows, line) + (cols, rows, cols, rows) * 2 + (line, line, P(), P())
        ),
        out_specs=(
            (slab, slab) + (cols, rows, cols, rows) * 2 + (line, line, P(), P())
        ),
        check_vma=False,
    )
```
